32 devices in a mesh: wide: 8 (over z, x), narrow: 4 (over y, core).
Axes of the slice: x: 2, y: 2, z: 4, core: 2. Of those that a mesh axis runs over, the one named last changes fastest.
Arguments:
- latent: bfloat16 [2048, 4096], P('wide', 'narrow'), may hold values from -90 to 90
- actions: int32 [2048], P('wide'), may hold values from 0 to 255
- action_table: bfloat16 [256, 4096], P(None, 'narrow'), may hold values from -3 to 3
- norm1_gain: float32 [4096], P('narrow'), may hold values from 0.5 to 1.5
- w_query: bfloat16 [4096, 2048], P(None, 'narrow'), may hold values from -0.140625 to 0.140625
- w_key: bfloat16 [4096, 2048], P(None, 'narrow'), may hold values from -0.140625 to 0.140625
- w_value: bfloat16 [4096, 2048], P(None, 'narrow'), may hold values from -0.09375 to 0.09375
- w_out: bfloat16 [2048, 4096], P(None, 'narrow'), may hold values from -0.125 to 0.125
- key_cache: bfloat16 [16, 512, 2048], P('wide', None, 'narrow'), may hold values from -460 to 460
- value_cache: bfloat16 [16, 512, 2048], P('wide', None, 'narrow'), may hold values from -6 to 6
- norm2_gain: float32 [4096], P('narrow'), may hold values from 0.5 to 1.5
- policy_in: bfloat16 [4096, 512], P('narrow'), may hold values from -0.09375 to 0.09375
- value_in: bfloat16 [4096, 512], P('narrow'), may hold values from -0.09375 to 0.09375
- policy_out: bfloat16 [512, 256], replicated, may hold values from -12.5 to 12.5
- value_out: bfloat16 [512], replicated, may hold values from -0.25 to 0.25
- targets: int32 [2048], P('wide'), may hold values from 0 to 255
- returns: float32 [2048], P('wide'), may hold values from -19 to 19
Outputs:
- new_latent: bfloat16 [2048, 4096], P('wide', 'narrow')
- losses: float32 [2], replicated
- policy_in_grad: bfloat16 [4096, 512], P('narrow')
- value_in_grad: bfloat16 [4096, 512], P('narrow')
- policy_out_grad: bfloat16 [512, 256], replicated
- value_out_grad: bfloat16 [512], replicated
The draws below stay inside these ranges and needn't reach their ends.
All inputs are finite; a program needn't handle non-finite values.
Results may differ from the reference program's by a relative error of at most 0.019.
Values may be sent and summed in bfloat16 or wider, within the bound.
No kernel may reach another device: no remote copies, remote signals or barrier semaphores. Data moves between devices by JAX's collectives and lax.ppermute only.
A program may use at most 64 MiB of HBM per device.

```python
import math
import jax
import jax.numpy as jnp
from jax import lax

D = 4096
HEADS = 16
HD = 128
CTX = 512
BRANCH = 128
PH = 512
VH = 512
A = 256
HF = 2048
SCENES = 16
ROWS = 2048


def shared_projection(key):
    return jnp.clip(jax.random.normal(key, (D, HF), jnp.float32), -6.0, 6.0) * D ** (-0.5)


def draw_w_query(key, part):
    shared = shared_projection(key)
    key = jax.random.fold_in(key, 15)
    extra = jnp.clip(jax.random.normal(key, (D, HF), jnp.float32), -6.0, 6.0) * D ** (-0.5)
    return (0.8 * shared + 0.6 * extra).astype(jnp.bfloat16)


def draw_w_key(key, part):
    shared = shared_projection(key)
    key = jax.random.fold_in(key, 16)
    extra = jnp.clip(jax.random.normal(key, (D, HF), jnp.float32), -6.0, 6.0) * D ** (-0.5)
    return (0.6 * shared + 0.8 * extra).astype(jnp.bfloat16)


def draw_latent(key, part):
    key = jax.random.fold_in(key, 11)
    key_a, key_b, key_c = jax.random.split(key, 3)
    row_scale = jnp.exp(jax.random.uniform(key_a, (ROWS, 1), jnp.float32, math.log(0.3), math.log(3.0)))
    col_pos = jnp.arange(D).astype(jnp.float32) / D
    col_scale = jnp.exp(math.log(10.0) * (col_pos - 0.5))[None, :] * jnp.exp(jax.random.uniform(key_b, (1, D), jnp.float32, -0.35, 0.35))
    base = jnp.clip(jax.random.normal(key_c, (ROWS, D), jnp.float32), -6.0, 6.0)
    return (base * row_scale * col_scale).astype(jnp.bfloat16)


def draw_key_cache(key, part):
    key = jax.random.fold_in(key, 12)
    key_a = jax.random.fold_in(key, 0)
    base = jnp.clip(jax.random.normal(key_a, (SCENES, CTX, HF), jnp.float32), -6.0, 6.0)
    return base.astype(jnp.bfloat16)


def draw_policy_out(key, part):
    key = jax.random.fold_in(key, 13)
    key_a = jax.random.fold_in(key, 0)
    base = 0.3 * jnp.clip(jax.random.normal(key_a, (PH, A), jnp.float32), -6.0, 6.0)
    return base.astype(jnp.bfloat16)


def draw_returns(key, part):
    key = jax.random.fold_in(key, 14)
    rising = jnp.exp(math.log(3.0) * jnp.arange(ROWS).astype(jnp.float32) / ROWS)
    base = jnp.clip(jax.random.normal(key, (ROWS,), jnp.float32), -6.0, 6.0)
    return base * rising


def with_ends(drawn, stream_key, smallest, high):
    longest = drawn.shape.index(max(drawn.shape))
    spots = []
    for shift in (0, 1):
        where = [jax.random.randint(jax.random.fold_in(stream_key, axis), (), 0, length) for axis, length in enumerate(drawn.shape)]
        where[longest] = (where[longest] + shift) % drawn.shape[longest]
        spots.append(tuple(where))
    return drawn.at[spots[0]].set(smallest).at[spots[1]].set(high)


def levels(rng, shape, pieces, low, high):
    def one(dim, blocks):
        steps = jax.random.uniform(jax.random.fold_in(jax.random.fold_in(rng, 6), dim), (blocks,), jnp.float32, low / len(pieces), high / len(pieces))
        return jnp.repeat(jnp.exp(steps), shape[dim] // blocks).reshape((-1,) + (1,) * (len(shape) - dim - 1))

    level = one(*pieces[0])
    for cut in pieces[1:]:
        level = level * one(*cut)
    return level


def normal_values(own_key, dims, width, bound, shards=(), kind=jnp.bfloat16):
    level = levels(own_key, dims, shards, -0.22, 0.18) if shards else 1.0
    values = jax.random.normal(own_key, dims, jnp.float32) * width * level
    return jnp.minimum(jnp.maximum(values, -bound), bound).astype(kind)


def setup_inputs(seed: int = 0) -> dict:
    keys = jax.random.split(jax.random.key(seed), 18)
    return {
        "latent": draw_latent(jax.random.fold_in(keys[17], 71), 0),
        "actions": with_ends(jax.random.randint(keys[1], (ROWS,), 0, A), jax.random.fold_in(keys[1], 1), 0, A - 1).astype(jnp.int32),
        "action_table": normal_values(keys[2], (A, D), 0.5, 3.0, ((1, 4),)),
        "norm1_gain": jnp.clip(1.0 + 0.1 * jax.random.normal(keys[3], (D,), jnp.float32), 0.5, 1.5),
        "w_query": draw_w_query(jax.random.fold_in(keys[17], 71), 0),
        "w_key": draw_w_key(jax.random.fold_in(keys[17], 71), 0),
        "w_value": normal_values(keys[6], (D, HF), D ** -0.5, 0.09375, ((1, 4),)),
        "w_out": normal_values(keys[7], (HF, D), HF ** -0.5, 0.125, ((1, 4),)),
        "key_cache": draw_key_cache(jax.random.fold_in(keys[17], 71), 0),
        "value_cache": normal_values(keys[9], (SCENES, CTX, HF), 1.0, 6.0, ((0, 8), (2, 4))),
        "norm2_gain": jnp.clip(1.0 + 0.1 * jax.random.normal(keys[10], (D,), jnp.float32), 0.5, 1.5),
        "policy_in": normal_values(keys[11], (D, PH), D ** -0.5, 0.09375, ((0, 4),)),
        "value_in": normal_values(keys[12], (D, VH), D ** -0.5, 0.09375, ((0, 4),)),
        "policy_out": draw_policy_out(jax.random.fold_in(keys[17], 71), 0),
        "value_out": normal_values(keys[14], (VH,), VH ** -0.5, 0.25),
        "targets": with_ends(jax.random.randint(keys[15], (ROWS,), 0, A), jax.random.fold_in(keys[15], 1), 0, A - 1).astype(jnp.int32),
        "returns": draw_returns(jax.random.fold_in(keys[17], 71), 0),
    }


EPSILON = 1e-05

def silu_slope(values):
    sigma = jax.nn.sigmoid(values)
    return sigma * (1.0 + values * (1.0 - sigma))

def reference(latent, actions, action_table, norm1_gain, w_query, w_key, w_value, w_out, key_cache, value_cache, norm2_gain, policy_in, value_in, policy_out, value_out, targets, returns):
    tokens = latent.astype(jnp.float32) + action_table.astype(jnp.float32)[actions]
    inverse = lax.rsqrt(lax.optimization_barrier(jnp.mean(tokens * tokens, axis=1, keepdims=True)) + EPSILON)
    normed = (tokens * inverse * norm1_gain).astype(jnp.bfloat16)
    query = jnp.dot(normed, w_query, preferred_element_type=jnp.float32).astype(jnp.bfloat16)
    key_new = jnp.dot(normed, w_key, preferred_element_type=jnp.float32).astype(jnp.bfloat16)
    value_new = jnp.dot(normed, w_value, preferred_element_type=jnp.float32).astype(jnp.bfloat16)
    scaling = HD ** (-0.5)

    def one_scene(packed):
        query_s, keyn_s, valuen_s, kcache_s, vcache_s = packed
        query_f = query_s.astype(jnp.float32)
        scores = jnp.einsum('bhd,chd->bhc', query_f, kcache_s.astype(jnp.float32), precision=lax.Precision.HIGHEST) * scaling
        own_score = lax.optimization_barrier(jnp.sum(query_f * keyn_s.astype(jnp.float32), axis=-1)) * scaling
        highest = jnp.maximum(lax.optimization_barrier(jnp.max(scores, axis=-1)), own_score)
        expd = jnp.exp(scores - highest[..., None])
        own_exp = jnp.exp(own_score - highest)
        totals = lax.optimization_barrier(jnp.sum(expd, axis=-1)) + own_exp
        weights = (expd / totals[..., None]).astype(jnp.bfloat16)
        own_weight = (own_exp / totals).astype(jnp.bfloat16)
        mixed = jnp.einsum('bhc,chd->bhd', weights.astype(jnp.float32), vcache_s.astype(jnp.float32), precision=lax.Precision.HIGHEST)
        mixed = mixed + own_weight.astype(jnp.float32)[..., None] * valuen_s.astype(jnp.float32)
        return mixed.astype(jnp.bfloat16)
    packed = (query.reshape(SCENES, BRANCH, HEADS, HD), key_new.reshape(SCENES, BRANCH, HEADS, HD), value_new.reshape(SCENES, BRANCH, HEADS, HD), key_cache.reshape(SCENES, CTX, HEADS, HD), value_cache.reshape(SCENES, CTX, HEADS, HD))
    attended = lax.map(one_scene, packed).reshape(ROWS, HF)
    state = tokens + jnp.dot(attended, w_out, preferred_element_type=jnp.float32)
    new_latent = state.astype(jnp.bfloat16)
    inverse_two = lax.rsqrt(lax.optimization_barrier(jnp.mean(state * state, axis=1, keepdims=True)) + EPSILON)
    heads_in = (state * inverse_two * norm2_gain).astype(jnp.bfloat16)
    policy_pre = jnp.dot(heads_in, policy_in, preferred_element_type=jnp.float32)
    value_pre = jnp.dot(heads_in, value_in, preferred_element_type=jnp.float32)
    policy_hidden = jax.nn.silu(policy_pre).astype(jnp.bfloat16)
    value_hidden = jax.nn.silu(value_pre).astype(jnp.bfloat16)
    logits = jnp.dot(policy_hidden, policy_out, preferred_element_type=jnp.float32)
    value = jnp.dot(value_hidden, value_out, preferred_element_type=jnp.float32)
    highest = lax.optimization_barrier(jnp.max(logits, axis=1, keepdims=True))
    log_total = highest[:, 0] + jnp.log(lax.optimization_barrier(jnp.sum(jnp.exp(logits - highest), axis=1)))
    onehot = (targets[:, None] == jnp.arange(A, dtype=jnp.int32)[None, :]).astype(jnp.float32)
    picked = lax.optimization_barrier(jnp.sum(logits * onehot, axis=1))
    errors = value - returns
    losses = jnp.stack([jnp.mean(log_total - picked), 0.5 * jnp.mean(errors * errors)])
    factor = ROWS ** (-0.5)
    dlogits = ((jnp.exp(logits - log_total[:, None]) - onehot) * factor).astype(jnp.bfloat16)
    dvalue = (errors * factor).astype(jnp.bfloat16)
    policy_out_grad = jnp.dot(policy_hidden.T, dlogits, preferred_element_type=jnp.float32).astype(jnp.bfloat16)
    value_out_grad = jnp.dot(dvalue, value_hidden, preferred_element_type=jnp.float32).astype(jnp.bfloat16)
    policy_dpre = (jnp.dot(dlogits, policy_out.T, preferred_element_type=jnp.float32) * silu_slope(policy_pre)).astype(jnp.bfloat16)
    value_dpre = (dvalue.astype(jnp.float32)[:, None] * value_out.astype(jnp.float32)[None, :] * silu_slope(value_pre)).astype(jnp.bfloat16)
    policy_in_grad = jnp.dot(heads_in.T, policy_dpre, preferred_element_type=jnp.float32).astype(jnp.bfloat16)
    value_in_grad = jnp.dot(heads_in.T, value_dpre, preferred_element_type=jnp.float32).astype(jnp.bfloat16)
    return (new_latent, losses, policy_in_grad, value_in_grad, policy_out_grad, value_out_grad)
```

```python
import jax
import jax.numpy as jnp
from jax import lax
from jax.sharding import PartitionSpec as P

HD = 128
EPSILON = 1e-05
F32 = jnp.float32
BF16 = jnp.bfloat16


def silu_slope(values):
    sigma = jax.nn.sigmoid(values)
    return sigma * (1.0 + values * (1.0 - sigma))


def swap(block, bit):
    size = lax.axis_size("narrow")
    return lax.ppermute(block, "narrow", [(n, n ^ bit) for n in range(size)])


def far_bits():
    bit = lax.axis_size("narrow") // 2
    while bit > 1:
        yield bit
        bit //= 2


def narrow_blocks(block):
    blocks = {0: block}
    for bit in (*far_bits(), 1):
        blocks.update({d ^ bit: swap(b, bit) for d, b in list(blocks.items())})
    return blocks


def ring_order(size):
    return list(range(0, size, 2)) + list(range(size - 1, 0, -2))


def ring_blocks(block):
    size = lax.axis_size("wide")
    order = ring_order(size)
    ahead = [(order[i], order[(i + 1) % size]) for i in range(size)]
    back = [(b, a) for a, b in ahead]
    ups, downs = [], []
    up = down = block
    for step in range(size - 1):
        if step % 2 == 0:
            up = lax.ppermute(up, "wide", ahead)
            ups.append(up)
        else:
            down = lax.ppermute(down, "wide", back)
            downs.append(down)
    return [block, *ups, *downs]


def per_device(
    latent,
    actions,
    action_table,
    norm1_gain,
    w_query,
    w_key,
    w_value,
    w_out,
    key_cache,
    value_cache,
    norm2_gain,
    policy_in,
    value_in,
    policy_out,
    value_out,
    targets,
    returns,
):
    row_count = latent.shape[0]
    scene_count = key_cache.shape[0]
    branch_count = row_count // scene_count
    width_local = latent.shape[1]
    narrow_size = lax.axis_size("narrow")
    full_width = width_local * narrow_size
    heads_local = w_query.shape[1] // HD
    total_rows = row_count * lax.axis_size("wide")
    action_count = action_table.shape[0]
    place = lax.axis_index("narrow")
    core = place % 2
    first = core == 0
    chip = place // 2
    chips = narrow_size // 2

    action_onehot = (
        actions[:, None] == jnp.arange(action_count, dtype=jnp.int32)[None, :]
    ).astype(BF16)
    tokens = latent.astype(F32) + jnp.dot(
        action_onehot, action_table, preferred_element_type=F32
    )
    gained = (tokens * norm1_gain).astype(BF16)
    squares = jnp.sum(tokens * tokens, axis=1)
    for bit in (1, *far_bits()):
        squares = squares + swap(squares, bit)
    inverse = lax.rsqrt(squares / full_width + EPSILON)[:, None]
    blocks = narrow_blocks(gained)

    def placed_rows(blocks):
        whole = jnp.zeros((row_count, blocks[0].shape[1] * narrow_size), BF16)
        for d, b in blocks.items():
            whole = lax.dynamic_update_slice(whole, b, (0, (place ^ d) * b.shape[1]))
        return whole

    segment = placed_rows(blocks)
    query, key_new, value_new = tuple(
        (
            (jnp.dot(segment, matrix, preferred_element_type=F32) * inverse)
            .astype(BF16)
            .reshape(scene_count, branch_count, heads_local, HD)
            for matrix in (w_query, w_key, w_value)
        )
    )
    cache_keys = key_cache.reshape(scene_count, key_cache.shape[1], heads_local, HD)
    cache_values = value_cache.reshape(scene_count, value_cache.shape[1], heads_local, HD)
    scaling = HD ** (-0.5)
    scores = (
        jnp.einsum("sbhd,schd->sbhc", query, cache_keys, preferred_element_type=F32) * scaling
    )
    own_score = jnp.sum(query.astype(F32) * key_new.astype(F32), axis=-1) * scaling
    highest = jnp.maximum(jnp.max(scores, axis=-1), own_score)
    expd = jnp.exp(scores - highest[..., None])
    own_exp = jnp.exp(own_score - highest)
    totals = jnp.sum(expd, axis=-1) + own_exp
    weights = (expd / totals[..., None]).astype(BF16)
    own_weight = (own_exp / totals).astype(BF16)
    mixed = jnp.einsum("sbhc,schd->sbhd", weights, cache_values, preferred_element_type=F32)
    mixed = mixed + own_weight.astype(F32)[..., None] * value_new.astype(F32)
    attended = mixed.astype(BF16).reshape(row_count, heads_local * HD)
    update = jnp.dot(
        placed_rows(narrow_blocks(attended)), w_out, preferred_element_type=F32
    )
    state = tokens + update
    new_latent = state.astype(BF16)
    squares_two = jnp.sum(state * state, axis=1)
    for bit in (1, *far_bits()):
        squares_two = squares_two + swap(squares_two, bit)
    inverse_two = lax.rsqrt(squares_two / full_width + EPSILON)[:, None]
    heads_in = (state * norm2_gain).astype(BF16)
    heads_in_all = ring_blocks(heads_in.T)

    policy_part = jnp.dot(heads_in, policy_in, preferred_element_type=F32)
    value_part = jnp.dot(heads_in, value_in, preferred_element_type=F32)
    given = jnp.where(first, value_part, policy_part).astype(BF16)
    pre = jnp.where(first, policy_part, value_part) + swap(given, 1).astype(F32)
    for bit in far_bits():
        rounded = pre.astype(BF16)
        pre = rounded.astype(F32) + swap(rounded, bit).astype(F32)
    pre = pre * inverse_two
    hidden = jax.nn.silu(pre).astype(BF16)
    value_wide = jnp.pad(value_out[:, None], ((0, 0), (0, action_count - 1)))
    out_weight = jnp.where(first, policy_out, value_wide)
    logits = jnp.dot(hidden, out_weight, preferred_element_type=F32)
    top_logit = jnp.max(logits, axis=1, keepdims=True)
    log_total = top_logit[:, 0] + jnp.log(jnp.sum(jnp.exp(logits - top_logit), axis=1))
    columns = jnp.arange(action_count, dtype=jnp.int32)[None, :]
    target_onehot = (targets[:, None] == columns).astype(F32)
    picked = jnp.sum(logits * target_onehot, axis=1)
    errors = logits[:, 0] - returns
    loss_sum = jnp.where(first, jnp.sum(log_total - picked), 0.5 * jnp.sum(errors * errors))
    factor = total_rows ** (-0.5)
    dpolicy = jnp.exp(logits - log_total[:, None]) - target_onehot
    dvalue = jnp.where(columns == 0, errors[:, None], 0.0)
    dlogits = (jnp.where(first, dpolicy, dvalue) * factor).astype(BF16)
    dpre = lax.dot_general(
        dlogits, out_weight, (((1,), (1,)), ((), ())), preferred_element_type=F32
    )
    dpre = (dpre * silu_slope(pre) * inverse_two).astype(BF16)
    dpre_own = ring_blocks(dpre)
    dpre_other = [swap(b, 1) for b in dpre_own]

    part = hidden.shape[1] // chips
    hidden_part = lax.dynamic_slice_in_dim(hidden, chip * part, part, axis=1)
    out_part = lax.dot_general(
        hidden_part, dlogits, (((0,), (0,)), ((), ())), preferred_element_type=F32
    )
    payload = jnp.concatenate([out_part, jnp.full((8, action_count), loss_sum, F32)], axis=0)
    payload = lax.psum(payload, "wide")
    out_part = payload[:part].astype(BF16)
    out_grad = jnp.zeros((hidden.shape[1], action_count), BF16)
    parts = {0: out_part}
    for bit in far_bits():
        parts.update({d ^ bit: swap(b, bit) for d, b in list(parts.items())})
    for d, b in parts.items():
        out_grad = lax.dynamic_update_slice(out_grad, b, ((chip ^ (d // 2)) * part, 0))
    other_grad = swap(out_grad, 1)
    policy_out_grad = jnp.where(first, out_grad, other_grad)
    value_out_grad = jnp.where(first, other_grad, out_grad)[:, 0]
    loss = payload[part, :1] / total_rows
    other_loss = swap(loss, 1)
    losses = jnp.where(first, jnp.concatenate([loss, other_loss]), jnp.concatenate([other_loss, loss]))

    heads_all = jnp.concatenate(heads_in_all, axis=1)
    own_grad = jnp.dot(
        heads_all, jnp.concatenate(dpre_own, axis=0), preferred_element_type=F32
    ).astype(BF16)
    other_in_grad = jnp.dot(
        heads_all, jnp.concatenate(dpre_other, axis=0), preferred_element_type=F32
    ).astype(BF16)
    policy_in_grad = jnp.where(first, own_grad, other_in_grad)
    value_in_grad = jnp.where(first, other_in_grad, own_grad)
    return (new_latent, losses, policy_in_grad, value_in_grad, policy_out_grad, value_out_grad)


def solution(mesh):
    placed = (
        P("wide", "narrow"),
        P("wide"),
        P(None, "narrow"),
        P("narrow"),
        P(None, "narrow"),
        P(None, "narrow"),
        P(None, "narrow"),
        P(None, "narrow"),
        P("wide", None, "narrow"),
        P("wide", None, "narrow"),
        P("narrow"),
        P("narrow", None),
        P("narrow", None),
        P(),
        P(),
        P("wide"),
        P("wide"),
    )
    return jax.shard_map(
        per_device,
        mesh=mesh,
        in_specs=placed,
        out_specs=(P("wide", "narrow"), P(), P("narrow", None), P("narrow", None), P(), P()),
        check_vma=False,
    )
```

```python
import functools

import jax
import jax.numpy as jnp
from jax import lax
from jax.experimental import pallas as pl
from jax.experimental.pallas import tpu as pltpu
from jax.sharding import PartitionSpec as P

HD = 128
EPSILON = 1e-05
F32 = jnp.float32
BF16 = jnp.bfloat16
MIB = 1 << 20


def swap(block, bit):
    size = lax.axis_size("narrow")
    return lax.ppermute(block, "narrow", [(n, n ^ bit) for n in range(size)])


def far_bits():
    bit = lax.axis_size("narrow") // 2
    while bit > 1:
        yield bit
        bit //= 2


def narrow_blocks(block):
    blocks = {0: block}
    for bit in (*far_bits(), 1):
        blocks.update({d ^ bit: swap(b, bit) for d, b in list(blocks.items())})
    return blocks


def dot(a, b):
    return jnp.dot(a, b, preferred_element_type=F32)


def column(row):
    return jnp.transpose(jnp.broadcast_to(row, (128, row.shape[1])))[:, :1]


def whole(shape):
    return pl.BlockSpec(shape, lambda i, p: (0,) * len(shape))


def weight_spec(ds, rows, columns):
    def at(i, p):
        d = jnp.int32(ds[0])
        for j in range(1, len(ds)):
            d = jnp.where(i == j, ds[j], d)
        return (p[0] ^ d, 0)

    return pl.BlockSpec((rows, columns), at)


def add_products(x_refs, w_refs, add):
    for step, x_ref in enumerate(x_refs):

        @pl.when(pl.program_id(0) == step)
        def _():
            for j, w_ref in enumerate(w_refs):
                add(j, dot(x_ref[...], w_ref[...]))


def project_start(count, p_ref, *refs):
    x_refs, w_refs, out = refs[:count], refs[count : count + 3], refs[-1]
    cols = w_refs[0].shape[1]

    @pl.when(pl.program_id(0) == 0)
    def _():
        out[...] = jnp.zeros_like(out)

    def add(j, product):
        out[:, j * cols : (j + 1) * cols] += product

    add_products(x_refs, w_refs, add)


def project_more(count, p_ref, acc_ref, *refs):
    x_refs, w_refs, out = refs[:count], refs[count : count + 3], refs[-1]
    cols = w_refs[0].shape[1]

    @pl.when(pl.program_id(0) == 0)
    def _():
        out[...] = acc_ref[...]

    def add(j, product):
        out[:, j * cols : (j + 1) * cols] += product

    add_products(x_refs, w_refs, add)


def attend(count, full_width, p_ref, acc_ref, squares_ref, keys_ref, values_ref, *refs):
    x_refs, w_refs, out, acc = refs[:count], refs[count : count + 3], refs[-2], refs[-1]
    cols = w_refs[0].shape[1]

    @pl.when(pl.program_id(0) == 0)
    def _():
        acc[...] = acc_ref[...]

    def add(j, product):
        acc[:, j * cols : (j + 1) * cols] += product

    add_products(x_refs, w_refs, add)

    @pl.when(pl.program_id(0) == count - 1)
    def _():
        scenes = keys_ref.shape[0]
        branch = acc.shape[0] // scenes
        inverse = column(lax.rsqrt(squares_ref[:1] / full_width + EPSILON))
        scaling = HD ** (-0.5)
        for s in range(scenes):
            rows = slice(s * branch, (s + 1) * branch)
            scale = inverse[rows]
            for h in range(cols // HD):
                at = slice(h * HD, (h + 1) * HD)
                q, k, v = (
                    (acc[rows, j * cols + h * HD : j * cols + (h + 1) * HD] * scale).astype(BF16)
                    for j in range(3)
                )
                scores = (
                    lax.dot_general(
                        q,
                        keys_ref[s, :, at],
                        (((1,), (1,)), ((), ())),
                        preferred_element_type=F32,
                    )
                    * scaling
                )
                own = jnp.sum(q.astype(F32) * k.astype(F32), axis=1, keepdims=True) * scaling
                highest = jnp.maximum(jnp.max(scores, axis=1, keepdims=True), own)
                expd = jnp.exp(scores - highest)
                own_exp = jnp.exp(own - highest)
                total = jnp.sum(expd, axis=1, keepdims=True) + own_exp
                weights = (expd / total).astype(BF16)
                own_weight = (own_exp / total).astype(BF16)
                mixed = dot(weights, values_ref[s, :, at])
                mixed = mixed + own_weight.astype(F32) * v.astype(F32)
                out[rows, at] = mixed.astype(BF16)


def update_start(count, p_ref, tokens_ref, *refs):
    x_refs, w_ref, out = refs[:count], refs[count], refs[-1]

    @pl.when(pl.program_id(0) == 0)
    def _():
        out[...] = tokens_ref[...]

    def add(j, product):
        out[...] += product

    add_products(x_refs, [w_ref], add)


def update_end(count, p_ref, acc_ref, gain_ref, policy_ref, value_ref, *refs):
    x_refs, w_ref = refs[:count], refs[count]
    latent_out, turned_out, squares_out, keep_out, give_out, acc = refs[count + 1 :]

    @pl.when(pl.program_id(0) == 0)
    def _():
        acc[...] = acc_ref[...]

    def add(j, product):
        acc[...] += product

    add_products(x_refs, [w_ref], add)

    @pl.when(pl.program_id(0) == count - 1)
    def _():
        state = acc[...]
        latent_out[...] = state.astype(BF16)
        squares = jnp.sum(state * state, axis=1, keepdims=True)
        squares_out[...] = jnp.transpose(jnp.broadcast_to(squares, (squares.shape[0], 128)))[:8]
        gained = (state * gain_ref[...]).astype(BF16)
        turned_out[...] = jnp.transpose(gained)
        policy = dot(gained, policy_ref[...])
        value = dot(gained, value_ref[...])

        @pl.when(p_ref[0] % 2 == 0)
        def _():
            keep_out[...] = policy
            give_out[...] = value.astype(BF16)

        @pl.when(p_ref[0] % 2 == 1)
        def _():
            keep_out[...] = value
            give_out[...] = policy.astype(BF16)


def heads(full_width, total_rows, p_ref, mine_ref, theirs_ref, squares_ref, policy_out_ref,
          value_out_ref, targets_ref, returns_ref, dpre_out, part_out, extra_out, hidden_ref):
    inverse = column(lax.rsqrt(squares_ref[:1] / full_width + EPSILON))
    pre = (mine_ref[...].astype(F32) + theirs_ref[...].astype(F32)) * inverse
    sigma = jax.nn.sigmoid(pre)
    hidden = (pre * sigma).astype(BF16)
    hidden_ref[...] = hidden
    slope = sigma * (1.0 + pre * (1.0 - sigma)) * inverse
    factor = total_rows ** (-0.5)
    part, width = part_out.shape
    rows = lax.broadcasted_iota(jnp.int32, extra_out.shape, 0)
    lanes = lax.broadcasted_iota(jnp.int32, extra_out.shape, 1)
    value_rows = hidden.shape[1] // width

    def with_loss(extra, loss):
        for lane in range(3):
            term = loss.astype(BF16).astype(F32)
            extra = jnp.where((rows == value_rows) & (lanes == lane), term, extra)
            loss = loss - term
        return extra.astype(BF16)

    @pl.when(p_ref[0] % 2 == 0)
    def _():
        weight = policy_out_ref[...]
        logits = dot(hidden, weight)
        top = jnp.max(logits, axis=1, keepdims=True)
        log_total = top + jnp.log(jnp.sum(jnp.exp(logits - top), axis=1, keepdims=True))
        actions = lax.broadcasted_iota(jnp.int32, logits.shape, 1).astype(F32)
        onehot = (actions == column(targets_ref[...].astype(F32))).astype(F32)
        picked = jnp.sum(logits * onehot, axis=1, keepdims=True)
        loss = jnp.sum(log_total - picked, axis=0, keepdims=True)
        dlogits = ((jnp.exp(logits - log_total) - onehot) * factor).astype(BF16)
        back = lax.dot_general(
            dlogits, weight, (((1,), (1,)), ((), ())), preferred_element_type=F32
        )
        dpre_out[...] = (back * slope).astype(BF16)
        start = pl.multiple_of((p_ref[0] // 2) * part, part)
        part_out[...] = lax.dot_general(
            hidden_ref[:, pl.ds(start, part)],
            dlogits,
            (((0,), (0,)), ((), ())),
            preferred_element_type=F32,
        ).astype(BF16)
        extra_out[...] = with_loss(jnp.zeros(extra_out.shape, F32), loss)

    @pl.when(p_ref[0] % 2 == 1)
    def _():
        weight = value_out_ref[...].astype(F32)
        hidden_f = hidden.astype(F32)
        value = jnp.sum(hidden_f * weight, axis=1, keepdims=True)
        errors = value - column(returns_ref[...])
        loss = 0.5 * jnp.sum(errors * errors, axis=0, keepdims=True)
        dvalue = (errors * factor).astype(BF16).astype(F32)
        dpre_out[...] = (dvalue * weight * slope).astype(BF16)
        part_out[...] = jnp.zeros_like(part_out)
        grad = jnp.sum(dvalue * hidden_f, axis=0, keepdims=True)
        extra = jnp.zeros(extra_out.shape, F32)
        for r in range(value_rows):
            extra = jnp.where(rows == r, grad[:, r * width : (r + 1) * width], extra)
        extra_out[...] = with_loss(extra, loss)


def gradients(p_ref, turned_ref, own_ref, other_ref, policy_out, value_out):
    def product(d_ref):
        total = dot(turned_ref[0], d_ref[0])
        for w in range(1, d_ref.shape[0]):
            total = total + dot(turned_ref[w], d_ref[w])
        return total.astype(BF16)

    @pl.when(p_ref[0] % 2 == 0)
    def _():
        policy_out[...] = product(own_ref)
        value_out[...] = product(other_ref)

    @pl.when(p_ref[0] % 2 == 1)
    def _():
        value_out[...] = product(own_ref)
        policy_out[...] = product(other_ref)


def call(body, name, place, steps, operands, in_specs, outs, out_specs, flops, limit, scratch=()):
    bytes_accessed = sum(x.size * x.dtype.itemsize for x in (*operands, *outs))
    return pl.pallas_call(
        body,
        name=name,
        out_shape=outs,
        grid_spec=pltpu.PrefetchScalarGridSpec(
            num_scalar_prefetch=1,
            grid=(steps,),
            in_specs=in_specs,
            out_specs=out_specs,
            scratch_shapes=scratch,
        ),
        compiler_params=pltpu.CompilerParams(
            dimension_semantics=("arbitrary",), vmem_limit_bytes=limit
        ),
        cost_estimate=pl.CostEstimate(
            flops=flops, bytes_accessed=bytes_accessed, transcendentals=0
        ),
    )(place, *operands)


def per_device(
    latent,
    actions,
    action_table,
    norm1_gain,
    w_query,
    w_key,
    w_value,
    w_out,
    key_cache,
    value_cache,
    norm2_gain,
    policy_in,
    value_in,
    policy_out,
    value_out,
    targets,
    returns,
):
    rows, width = latent.shape
    narrow_size = lax.axis_size("narrow")
    wide_size = lax.axis_size("wide")
    full_width = width * narrow_size
    cols = w_query.shape[1]
    total_rows = rows * wide_size
    action_count = action_table.shape[0]
    hidden_count = policy_in.shape[1]
    index = lax.axis_index("narrow").astype(jnp.int32)
    place = index[None]
    first = index % 2 == 0
    chips = narrow_size // 2
    near = [0, 1]
    direct = list(range(2, narrow_size, 2))
    passed = [d + 1 for d in direct]

    action_onehot = (
        actions[:, None] == jnp.arange(action_count, dtype=jnp.int32)[None, :]
    ).astype(BF16)
    tokens = latent.astype(F32) + dot(action_onehot, action_table)
    gained = (tokens * norm1_gain).astype(BF16)
    squares = jnp.sum(tokens * tokens, axis=1)
    for bit in (1, *far_bits()):
        squares = squares + swap(squares, bit)
    squares = jnp.broadcast_to(squares[None, :], (8, rows))
    blocks = narrow_blocks(gained)

    weights = [w_query, w_key, w_value]

    def weight_specs(ds):
        return [weight_spec(ds, width, cols)] * 3

    acc_shape = jax.ShapeDtypeStruct((rows, 3 * cols), F32)
    acc_spec = whole((rows, 3 * cols))
    x_spec = whole((rows, width))
    flops = 2 * rows * width * 3 * cols
    acc = call(
        functools.partial(project_start, len(near)), "project_near", place, len(near),
        [*(blocks[d] for d in near), *weights],
        [*[x_spec] * len(near), *weight_specs(near)],
        [acc_shape], [acc_spec], flops * len(near), 20 * MIB,
    )[0]
    acc = call(
        functools.partial(project_more, len(direct)), "project_direct", place, len(direct),
        [acc, *(blocks[d] for d in direct), *weights],
        [acc_spec, *[x_spec] * len(direct), *weight_specs(direct)],
        [acc_shape], [acc_spec], flops * len(direct), 24 * MIB,
    )[0]
    cache_spec = whole(key_cache.shape)
    attended = call(
        functools.partial(attend, len(passed), full_width), "attend", place, len(passed),
        [acc, squares, key_cache, value_cache, *(blocks[d] for d in passed), *weights],
        [
            acc_spec, whole(squares.shape), cache_spec, cache_spec,
            *[x_spec] * len(passed), *weight_specs(passed),
        ],
        [jax.ShapeDtypeStruct((rows, cols), BF16)], [whole((rows, cols))],
        flops * len(passed), 32 * MIB, [pltpu.VMEM((rows, 3 * cols), F32)],
    )[0]

    blocks = narrow_blocks(attended)
    far = direct + passed
    x_spec = whole((rows, cols))
    state_spec = whole((rows, width))
    state_shape = jax.ShapeDtypeStruct((rows, width), F32)
    flops = 2 * rows * width * cols
    acc = call(
        functools.partial(update_start, len(near)), "update_near", place, len(near),
        [tokens, *(blocks[d] for d in near), w_out],
        [state_spec, *[x_spec] * len(near), weight_spec(near, cols, width)],
        [state_shape], [state_spec], flops * len(near), 16 * MIB,
    )[0]
    half = (rows, hidden_count)
    new_latent, turned, squares, keep, give = call(
        functools.partial(update_end, len(far)), "update_end", place, len(far),
        [acc, norm2_gain[None, :], policy_in, value_in, *(blocks[d] for d in far), w_out],
        [
            state_spec, whole((1, width)), whole(policy_in.shape), whole(value_in.shape),
            *[x_spec] * len(far), weight_spec(far, cols, width),
        ],
        [
            jax.ShapeDtypeStruct((rows, width), BF16),
            jax.ShapeDtypeStruct((width, rows), BF16),
            jax.ShapeDtypeStruct((8, rows), F32),
            jax.ShapeDtypeStruct(half, F32),
            jax.ShapeDtypeStruct(half, BF16),
        ],
        [state_spec, whole((width, rows)), whole((8, rows)), whole(half), whole(half)],
        flops * len(far) + 4 * rows * width * hidden_count, 32 * MIB,
        [pltpu.VMEM((rows, width), F32)],
    )
    turned_all = lax.all_gather(turned, "wide", axis=0)

    for bit in (1, *far_bits()):
        squares = squares + swap(squares, bit)
    pre = keep + swap(give, 1).astype(F32)
    mine = pre.astype(BF16)
    *upper, last = far_bits()
    for bit in upper:
        mine = (mine.astype(F32) + swap(mine, bit).astype(F32)).astype(BF16)
    theirs = swap(mine, last)
    part = hidden_count // chips
    dpre, out_part, extra = call(
        functools.partial(heads, full_width, total_rows), "heads", place, 1,
        [
            mine, theirs, squares, policy_out, value_out[None, :], targets[None, :],
            returns[None, :],
        ],
        [
            whole(half), whole(half), whole((8, rows)), whole(policy_out.shape),
            whole((1, hidden_count)), whole((1, rows)), whole((1, rows)),
        ],
        [
            jax.ShapeDtypeStruct(half, BF16),
            jax.ShapeDtypeStruct((part, action_count), BF16),
            jax.ShapeDtypeStruct((16, action_count), BF16),
        ],
        [whole(half), whole((part, action_count)), whole((16, action_count))],
        6 * rows * hidden_count * action_count, 16 * MIB, [pltpu.VMEM(half, BF16)],
    )
    dpre_own = lax.all_gather(dpre, "wide", axis=0)
    dpre_other = swap(dpre_own, 1)

    piece = part // wide_size
    payload = jnp.concatenate(
        [
            out_part.reshape(wide_size, piece, action_count),
            jnp.broadcast_to(extra[None], (wide_size, *extra.shape)),
        ],
        axis=1,
    )
    payload = lax.all_to_all(payload, "wide", 0, 0, tiled=True)
    sums = jnp.sum(payload.astype(F32), axis=0)
    value_rows = hidden_count // action_count
    loss = jnp.sum(sums[piece + value_rows, :3], keepdims=True) / total_rows
    other_loss = swap(loss, 1)
    losses = jnp.concatenate(
        [jnp.where(first, loss, other_loss), jnp.where(first, other_loss, loss)]
    )
    value_grad = sums[piece : piece + value_rows].astype(BF16).reshape(hidden_count)
    value_out_grad = jnp.where(first, swap(value_grad, 1), value_grad)
    parts = {0: sums[:piece].astype(BF16)}
    for bit in far_bits():
        parts.update({d ^ bit: swap(b, bit) for d, b in list(parts.items())})
    mixed = jnp.zeros((chips, piece, action_count), BF16)
    for d, b in parts.items():
        mixed = lax.dynamic_update_slice(mixed, b[None], ((index ^ d) // 2, 0, 0))
    mixed = jnp.where(first, mixed, swap(mixed, 1))
    mixed = lax.all_gather(mixed, "wide", axis=1)
    policy_out_grad = mixed.reshape(hidden_count, action_count)

    block = 256
    gathered = (wide_size, rows, hidden_count)
    grad_shape = jax.ShapeDtypeStruct((width, hidden_count), BF16)
    grad_spec = pl.BlockSpec((block, hidden_count), lambda i, p: (i, 0))
    policy_in_grad, value_in_grad = call(
        gradients, "gradients", place, width // block,
        [turned_all, dpre_own, dpre_other],
        [
            pl.BlockSpec((wide_size, block, rows), lambda i, p: (0, i, 0)),
            whole(gathered), whole(gathered),
        ],
        [grad_shape, grad_shape], [grad_spec, grad_spec],
        4 * total_rows * width * hidden_count, 56 * MIB,
    )
    return (new_latent, losses, policy_in_grad, value_in_grad, policy_out_grad, value_out_grad)


def solution(mesh):
    placed = (
        P("wide", "narrow"),
        P("wide"),
        P(None, "narrow"),
        P("narrow"),
        P(None, "narrow"),
        P(None, "narrow"),
        P(None, "narrow"),
        P(None, "narrow"),
        P("wide", None, "narrow"),
        P("wide", None, "narrow"),
        P("narrow"),
        P("narrow", None),
        P("narrow", None),
        P(),
        P(),
        P("wide"),
        P("wide"),
    )
    return jax.shard_map(
        per_device,
        mesh=mesh,
        in_specs=placed,
        out_specs=(P("wide", "narrow"), P(), P("narrow", None), P("narrow", None), P(), P()),
        check_vma=False,
    )
```

```python
import functools

import jax
import jax.numpy as jnp
from jax import lax
from jax.experimental import pallas as pl
from jax.experimental.pallas import tpu as pltpu
from jax.sharding import PartitionSpec as P

HD = 128
EPSILON = 1e-05
F32 = jnp.float32
BF16 = jnp.bfloat16
MIB = 1 << 20


def swap(block, bit):
    size = lax.axis_size("narrow")
    return lax.ppermute(block, "narrow", [(n, n ^ bit) for n in range(size)])


def far_bits():
    bit = lax.axis_size("narrow") // 2
    while bit > 1:
        yield bit
        bit //= 2


def far_blocks(block):
    blocks = {0: block}
    for bit in far_bits():
        blocks.update({d ^ bit: swap(b, bit) for d, b in list(blocks.items())})
    return blocks


def pass_blocks(blocks, *earlier):
    far = {d ^ 1: swap(after(b, *earlier), 1) for d, b in blocks.items() if d > 1}
    return {**blocks, **far}


def after(block, *earlier):
    return lax.optimization_barrier((block, *earlier))[0]


def ring_order(size):
    return list(range(0, size, 2)) + list(range(size - 1, 0, -2))


def ring_step(block, way):
    order = ring_order(lax.axis_size("wide"))
    pairs = [(a, order[(i + way) % len(order)]) for i, a in enumerate(order)]
    return lax.ppermute(block, "wide", pairs)


def next_round(pair, *earlier):
    up, down = (after(b, *earlier) for b in pair)
    return ring_step(up, 1), ring_step(down, -1)


def last_round(pair, axis, *earlier):
    size = pair[0].shape[axis] // 2
    up = lax.slice_in_dim(pair[0], 0, size, axis=axis)
    down = lax.slice_in_dim(pair[1], size, 2 * size, axis=axis)
    return next_round((up, down), *earlier)


def wide_swap(block, bit):
    size = lax.axis_size("wide")
    return lax.ppermute(block, "wide", [(n, n ^ bit) for n in range(size)])


def dot(a, b):
    return jnp.dot(a, b, preferred_element_type=F32)


def column(row):
    return jnp.transpose(jnp.broadcast_to(row, (128, row.shape[1])))[:, :1]


def whole(shape):
    return pl.BlockSpec(shape, lambda i, p: (0,) * len(shape))


def weight_spec(ds, rows, columns):
    def at(i, p):
        d = jnp.int32(ds[0])
        for j in range(1, len(ds)):
            d = jnp.where(i == j, ds[j], d)
        return (p[0] ^ d, 0)

    return pl.BlockSpec((rows, columns), at)


def add_products(x_refs, w_refs, add):
    for step, x_ref in enumerate(x_refs):

        @pl.when(pl.program_id(0) == step)
        def _():
            for j, w_ref in enumerate(w_refs):
                add(j, dot(x_ref[...], w_ref[...]))


def project_start(count, p_ref, *refs):
    x_refs, w_refs, out = refs[:count], refs[count : count + 3], refs[-1]
    cols = w_refs[0].shape[1]

    @pl.when(pl.program_id(0) == 0)
    def _():
        out[...] = jnp.zeros_like(out)

    def add(j, product):
        out[:, j * cols : (j + 1) * cols] += product

    add_products(x_refs, w_refs, add)


def project_more(count, p_ref, acc_ref, *refs):
    x_refs, w_refs, out = refs[:count], refs[count : count + 3], refs[-1]
    cols = w_refs[0].shape[1]

    @pl.when(pl.program_id(0) == 0)
    def _():
        out[...] = acc_ref[...]

    def add(j, product):
        out[:, j * cols : (j + 1) * cols] += product

    add_products(x_refs, w_refs, add)


def attend(count, full_width, p_ref, acc_ref, squares_ref, keys_ref, values_ref, *refs):
    x_refs, w_refs, out, acc = refs[:count], refs[count : count + 3], refs[-2], refs[-1]
    cols = w_refs[0].shape[1]

    @pl.when(pl.program_id(0) == 0)
    def _():
        acc[...] = acc_ref[...]

    def add(j, product):
        acc[:, j * cols : (j + 1) * cols] += product

    add_products(x_refs, w_refs, add)

    @pl.when(pl.program_id(0) == count - 1)
    def _():
        scenes = keys_ref.shape[0]
        branch = acc.shape[0] // scenes
        inverse = column(lax.rsqrt(squares_ref[:1] / full_width + EPSILON))
        scaling = HD ** (-0.5)
        for s in range(scenes):
            rows = slice(s * branch, (s + 1) * branch)
            scale = inverse[rows]
            for h in range(cols // HD):
                at = slice(h * HD, (h + 1) * HD)
                q, k, v = (
                    (acc[rows, j * cols + h * HD : j * cols + (h + 1) * HD] * scale).astype(BF16)
                    for j in range(3)
                )
                scores = (
                    lax.dot_general(
                        q,
                        keys_ref[s, :, at],
                        (((1,), (1,)), ((), ())),
                        preferred_element_type=F32,
                    )
                    * scaling
                )
                own = jnp.sum(q.astype(F32) * k.astype(F32), axis=1, keepdims=True) * scaling
                highest = jnp.maximum(jnp.max(scores, axis=1, keepdims=True), own)
                expd = jnp.exp(scores - highest)
                own_exp = jnp.exp(own - highest)
                total = jnp.sum(expd, axis=1, keepdims=True) + own_exp
                weights = (expd / total).astype(BF16)
                own_weight = (own_exp / total).astype(BF16)
                mixed = dot(weights, values_ref[s, :, at])
                mixed = mixed + own_weight.astype(F32) * v.astype(F32)
                out[rows, at] = mixed.astype(BF16)


def update_start(count, p_ref, tokens_ref, *refs):
    x_refs, w_ref, out = refs[:count], refs[count], refs[-1]

    @pl.when(pl.program_id(0) == 0)
    def _():
        out[...] = tokens_ref[...]

    def add(j, product):
        out[...] += product

    add_products(x_refs, [w_ref], add)


def update_end(count, p_ref, acc_ref, gain_ref, policy_ref, value_ref, *refs):
    x_refs, w_ref = refs[:count], refs[count]
    latent_out, turned_out, squares_out, keep_out, give_out, acc = refs[count + 1 :]

    @pl.when(pl.program_id(0) == 0)
    def _():
        acc[...] = acc_ref[...]

    def add(j, product):
        acc[...] += product

    add_products(x_refs, [w_ref], add)

    @pl.when(pl.program_id(0) == count - 1)
    def _():
        state = acc[...]
        latent_out[...] = state.astype(BF16)
        squares = jnp.sum(state * state, axis=1, keepdims=True)
        squares_out[...] = jnp.transpose(jnp.broadcast_to(squares, (squares.shape[0], 128)))[:8]
        gained = (state * gain_ref[...]).astype(BF16)
        turned_out[...] = jnp.transpose(gained)
        policy = dot(gained, policy_ref[...])
        value = dot(gained, value_ref[...])

        @pl.when(p_ref[0] % 2 == 0)
        def _():
            keep_out[...] = policy
            give_out[...] = value.astype(BF16)

        @pl.when(p_ref[0] % 2 == 1)
        def _():
            keep_out[...] = value
            give_out[...] = policy.astype(BF16)


def heads(full_width, total_rows, p_ref, mine_ref, theirs_ref, squares_ref, policy_out_ref,
          value_out_ref, targets_ref, returns_ref, dpre_out, part_out, extra_out, hidden_ref):
    inverse = column(lax.rsqrt(squares_ref[:1] / full_width + EPSILON))
    pre = (mine_ref[...].astype(F32) + theirs_ref[...].astype(F32)) * inverse
    sigma = jax.nn.sigmoid(pre)
    hidden = (pre * sigma).astype(BF16)
    hidden_ref[...] = hidden
    slope = sigma * (1.0 + pre * (1.0 - sigma)) * inverse
    factor = total_rows ** (-0.5)
    part, width = part_out.shape
    rows = lax.broadcasted_iota(jnp.int32, extra_out.shape, 0)
    value_rows = hidden.shape[1] // width

    def with_loss(extra, loss):
        return jnp.where(rows == value_rows, loss, extra)

    @pl.when(p_ref[0] % 2 == 0)
    def _():
        weight = policy_out_ref[...]
        logits = dot(hidden, weight)
        top = jnp.max(logits, axis=1, keepdims=True)
        log_total = top + jnp.log(jnp.sum(jnp.exp(logits - top), axis=1, keepdims=True))
        actions = lax.broadcasted_iota(jnp.int32, logits.shape, 1).astype(F32)
        onehot = (actions == column(targets_ref[...].astype(F32))).astype(F32)
        picked = jnp.sum(logits * onehot, axis=1, keepdims=True)
        loss = jnp.sum(log_total - picked, axis=0, keepdims=True)
        dlogits = ((jnp.exp(logits - log_total) - onehot) * factor).astype(BF16)
        back = lax.dot_general(
            dlogits, weight, (((1,), (1,)), ((), ())), preferred_element_type=F32
        )
        dpre_out[...] = (back * slope).astype(BF16)
        start = pl.multiple_of((p_ref[0] // 2) * part, part)
        part_out[...] = lax.dot_general(
            hidden_ref[:, pl.ds(start, part)],
            dlogits,
            (((0,), (0,)), ((), ())),
            preferred_element_type=F32,
        ).astype(BF16)
        extra_out[...] = with_loss(jnp.zeros(extra_out.shape, F32), loss)

    @pl.when(p_ref[0] % 2 == 1)
    def _():
        weight = value_out_ref[...].astype(F32)
        hidden_f = hidden.astype(F32)
        value = jnp.sum(hidden_f * weight, axis=1, keepdims=True)
        errors = value - column(returns_ref[...])
        loss = 0.5 * jnp.sum(errors * errors, axis=0, keepdims=True)
        dvalue = (errors * factor).astype(BF16).astype(F32)
        dpre_out[...] = (dvalue * weight * slope).astype(BF16)
        part_out[...] = jnp.zeros_like(part_out)
        grad = jnp.sum(dvalue * hidden_f, axis=0, keepdims=True)
        extra = jnp.zeros(extra_out.shape, F32)
        for r in range(value_rows):
            extra = jnp.where(rows == r, grad[:, r * width : (r + 1) * width], extra)
        extra_out[...] = with_loss(extra, loss)


def gradients(counts, p_ref, *refs):
    turned_count, count = counts
    turned, own, other = refs[:turned_count], refs[turned_count:][:count], refs[turned_count:][count:-2]
    policy_out, value_out = refs[-2:]
    upper = pl.program_id(0) < pl.num_programs(0) // 2
    *turned, ahead, back = [ref[...] for ref in turned]
    turned = jnp.concatenate([*turned, jnp.where(upper, ahead, back)], axis=1)

    def product(d_refs):
        return dot(turned, jnp.concatenate([ref[...] for ref in d_refs], axis=0)).astype(BF16)

    @pl.when(p_ref[0] % 2 == 0)
    def _():
        policy_out[...] = product(own)
        value_out[...] = product(other)

    @pl.when(p_ref[0] % 2 == 1)
    def _():
        value_out[...] = product(own)
        policy_out[...] = product(other)


def call(body, name, place, steps, operands, in_specs, outs, out_specs, flops, limit, scratch=()):
    bytes_accessed = sum(x.size * x.dtype.itemsize for x in (*operands, *outs))
    return pl.pallas_call(
        body,
        name=name,
        out_shape=outs,
        grid_spec=pltpu.PrefetchScalarGridSpec(
            num_scalar_prefetch=1,
            grid=(steps,),
            in_specs=in_specs,
            out_specs=out_specs,
            scratch_shapes=scratch,
        ),
        compiler_params=pltpu.CompilerParams(
            dimension_semantics=("arbitrary",), vmem_limit_bytes=limit
        ),
        cost_estimate=pl.CostEstimate(
            flops=flops, bytes_accessed=bytes_accessed, transcendentals=0
        ),
    )(place, *operands)


def per_device(
    latent,
    actions,
    action_table,
    norm1_gain,
    w_query,
    w_key,
    w_value,
    w_out,
    key_cache,
    value_cache,
    norm2_gain,
    policy_in,
    value_in,
    policy_out,
    value_out,
    targets,
    returns,
):
    rows, width = latent.shape
    narrow_size = lax.axis_size("narrow")
    wide_size = lax.axis_size("wide")
    full_width = width * narrow_size
    cols = w_query.shape[1]
    total_rows = rows * wide_size
    action_count = action_table.shape[0]
    hidden_count = policy_in.shape[1]
    index = lax.axis_index("narrow").astype(jnp.int32)
    place = index[None]
    first = index % 2 == 0
    chips = narrow_size // 2
    near = [0, 1]
    direct = list(range(2, narrow_size, 2))
    passed = [d + 1 for d in direct]

    action_onehot = (
        actions[:, None] == jnp.arange(action_count, dtype=jnp.int32)[None, :]
    ).astype(BF16)
    tokens = latent.astype(F32) + dot(action_onehot, action_table)
    gained = (tokens * norm1_gain).astype(BF16)
    squares = jnp.sum(tokens * tokens, axis=1)
    for bit in (1, *far_bits()):
        squares = squares + swap(squares, bit)
    squares = jnp.broadcast_to(squares[None, :], (8, rows))
    blocks = far_blocks(gained)
    blocks[1] = swap(gained, 1)

    weights = [pltpu.with_memory_space_constraint(w, pltpu.HBM) for w in (w_query, w_key, w_value)]

    def weight_specs(ds):
        return [weight_spec(ds, width, cols)] * 3

    acc_shape = jax.ShapeDtypeStruct((rows, 3 * cols), F32)
    acc_spec = whole((rows, 3 * cols))
    x_spec = whole((rows, width))
    flops = 2 * rows * width * 3 * cols
    acc = call(
        functools.partial(project_start, len(near)), "project_near", place, len(near),
        [*(blocks[d] for d in near), *weights],
        [*[x_spec] * len(near), *weight_specs(near)],
        [acc_shape], [acc_spec], flops * len(near), 20 * MIB,
    )[0]
    blocks = pass_blocks(blocks, acc, squares)
    acc = call(
        functools.partial(project_more, len(direct)), "project_direct", place, len(direct),
        [acc, *(blocks[d] for d in direct), *weights],
        [acc_spec, *[x_spec] * len(direct), *weight_specs(direct)],
        [acc_shape], [acc_spec], flops * len(direct), 24 * MIB,
    )[0]
    cache_spec = whole(key_cache.shape)
    attended = call(
        functools.partial(attend, len(passed), full_width), "attend", place, len(passed),
        [acc, squares, key_cache, value_cache, *(blocks[d] for d in passed), *weights],
        [
            acc_spec, whole(squares.shape), cache_spec, cache_spec,
            *[x_spec] * len(passed), *weight_specs(passed),
        ],
        [jax.ShapeDtypeStruct((rows, cols), BF16)], [whole((rows, cols))],
        flops * len(passed), 32 * MIB, [pltpu.VMEM((rows, 3 * cols), F32)],
    )[0]

    blocks = far_blocks(attended)
    blocks[1] = swap(attended, 1)
    far = direct + passed
    x_spec = whole((rows, cols))
    state_spec = whole((rows, width))
    state_shape = jax.ShapeDtypeStruct((rows, width), F32)
    flops = 2 * rows * width * cols
    acc = call(
        functools.partial(update_start, len(near)), "update_near", place, len(near),
        [tokens, *(blocks[d] for d in near), w_out],
        [state_spec, *[x_spec] * len(near), weight_spec(near, cols, width)],
        [state_shape], [state_spec], flops * len(near), 16 * MIB,
    )[0]
    blocks = pass_blocks(blocks, acc)
    half = (rows, hidden_count)
    new_latent, turned, squares, keep, give = call(
        functools.partial(update_end, len(far)), "update_end", place, len(far),
        [acc, norm2_gain[None, :], policy_in, value_in, *(blocks[d] for d in far), w_out],
        [
            state_spec, whole((1, width)), whole(policy_in.shape), whole(value_in.shape),
            *[x_spec] * len(far), weight_spec(far, cols, width),
        ],
        [
            jax.ShapeDtypeStruct((rows, width), BF16),
            jax.ShapeDtypeStruct((width, rows), BF16),
            jax.ShapeDtypeStruct((8, rows), F32),
            jax.ShapeDtypeStruct(half, F32),
            jax.ShapeDtypeStruct(half, BF16),
        ],
        [state_spec, whole((width, rows)), whole((8, rows)), whole(half), whole(half)],
        flops * len(far) + 4 * rows * width * hidden_count, 32 * MIB,
        [pltpu.VMEM((rows, width), F32)],
    )
    rounds = wide_size // 2
    turned_rounds = [(turned, turned)]
    turned_rounds.append(next_round(turned_rounds[0]))

    for bit in (1, *far_bits()):
        squares = squares + swap(squares, bit)
    pre = keep + swap(give, 1).astype(F32)
    mine = pre.astype(BF16)
    *upper, last = far_bits()
    for bit in upper:
        mine = (mine.astype(F32) + swap(mine, bit).astype(F32)).astype(BF16)
    theirs = after(swap(mine, last), *turned_rounds[1])
    part = hidden_count // chips
    dpre, out_part, extra = call(
        functools.partial(heads, full_width, total_rows), "heads", place, 1,
        [
            mine, theirs, squares, policy_out, value_out[None, :], targets[None, :],
            returns[None, :],
        ],
        [
            whole(half), whole(half), whole((8, rows)), whole(policy_out.shape),
            whole((1, hidden_count)), whole((1, rows)), whole((1, rows)),
        ],
        [
            jax.ShapeDtypeStruct(half, BF16),
            jax.ShapeDtypeStruct((part, action_count), BF16),
            jax.ShapeDtypeStruct((8, action_count), F32),
        ],
        [whole(half), whole((part, action_count)), whole((8, action_count))],
        6 * rows * hidden_count * action_count, 16 * MIB, [pltpu.VMEM(half, BF16)],
    )

    spot = lax.axis_index("wide").astype(jnp.int32)
    bits = [1 << k for k in range(wide_size.bit_length() - 1)]
    dpre_rounds = [(dpre, dpre)]
    done = ()
    for step in range(1, rounds + 1):
        ahead = turned_rounds[-1], dpre_rounds[-1]
        if step < rounds - 1:
            turned_rounds.append(next_round(ahead[0], *ahead[1], *done))
        elif step == rounds - 1:
            turned_rounds.append(last_round(ahead[0], 0, *ahead[1], *done))
        if step < rounds:
            dpre_rounds.append(next_round(ahead[1], *ahead[0], *done))
        else:
            dpre_rounds.append(last_round(ahead[1], 0, *ahead[0]))
        if step == 1:
            piece = after(out_part, *dpre_rounds[-1], *turned_rounds[-1])
            for bit in bits:
                low, high = jnp.split(piece, 2, axis=0)
                upper = spot & bit != 0
                given = wide_swap(jnp.where(upper, low, high), bit)
                piece = jnp.where(upper, high, low).astype(F32) + given.astype(F32)
                piece = piece.astype(BF16)
        done = (piece,) if step == 2 else ()
        if step == 2:
            piece, extra = (
                after(b, *dpre_rounds[-1], *turned_rounds[-1]) for b in (piece, extra)
            )
    turned_all = [turned, *(b for pair in turned_rounds[1:] for b in pair)]
    dpre_own = [dpre, *(b for pair in dpre_rounds[1:] for b in pair)]
    dpre_other = [swap(b, 1) for b in dpre_own]

    for bit in bits:
        extra = extra + wide_swap(extra, bit)
    extra_other = swap(extra, 1)
    policy_extra = jnp.where(first, extra, extra_other)
    value_extra = jnp.where(first, extra_other, extra)
    value_rows = hidden_count // action_count
    losses = (
        jnp.stack([policy_extra[value_rows, 0], value_extra[value_rows, 0]]) / total_rows
    )
    value_out_grad = value_extra[:value_rows].reshape(hidden_count).astype(BF16)

    def joined(block, bit, is_upper, send, axis):
        got = send(block, bit)
        return jnp.where(
            is_upper,
            jnp.concatenate([got, block], axis=axis),
            jnp.concatenate([block, got], axis=axis),
        )

    piece = piece[None]
    for bit in reversed(list(far_bits())):
        piece = joined(piece, bit, index & bit != 0, swap, 0)
    piece = jnp.where(first, piece, swap(piece, 1))
    for bit in reversed(bits):
        piece = joined(piece, bit, spot & bit != 0, wide_swap, 1)
    policy_out_grad = piece.reshape(hidden_count, action_count)

    block = 256
    half_steps = width // block // 2
    turned_specs = [pl.BlockSpec((block, rows), lambda i, p: (i, 0))] * (len(turned_all) - 2)
    turned_specs += [
        pl.BlockSpec((block, rows), lambda i, p: (jnp.minimum(i, half_steps - 1), 0)),
        pl.BlockSpec((block, rows), lambda i, p: (jnp.maximum(i - half_steps, 0), 0)),
    ]
    dpre_specs = [whole(b.shape) for b in dpre_own]
    grad_shape = jax.ShapeDtypeStruct((width, hidden_count), BF16)
    grad_spec = pl.BlockSpec((block, hidden_count), lambda i, p: (i, 0))
    policy_in_grad, value_in_grad = call(
        functools.partial(gradients, (len(turned_all), len(dpre_own))), "gradients", place,
        width // block, [*turned_all, *dpre_own, *dpre_other],
        [*turned_specs, *dpre_specs, *dpre_specs],
        [grad_shape, grad_shape], [grad_spec, grad_spec],
        4 * total_rows * width * hidden_count, 40 * MIB,
    )
    return (new_latent, losses, policy_in_grad, value_in_grad, policy_out_grad, value_out_grad)


def solution(mesh):
    placed = (
        P("wide", "narrow"),
        P("wide"),
        P(None, "narrow"),
        P("narrow"),
        P(None, "narrow"),
        P(None, "narrow"),
        P(None, "narrow"),
        P(None, "narrow"),
        P("wide", None, "narrow"),
        P("wide", None, "narrow"),
        P("narrow"),
        P("narrow", None),
        P("narrow", None),
        P(),
        P(),
        P("wide"),
        P("wide"),
    )
    return jax.shard_map(
        per_device,
        mesh=mesh,
        in_specs=placed,
        out_specs=(P("wide", "narrow"), P(), P("narrow", None), P("narrow", None), P(), P()),
        check_vma=False,
    )
```

```python
import functools

import jax
import jax.numpy as jnp
from jax import lax
from jax.experimental import pallas as pl
from jax.experimental.pallas import tpu as pltpu
from jax.sharding import PartitionSpec as P

HD = 128
EPSILON = 1e-05
F32 = jnp.float32
BF16 = jnp.bfloat16
MIB = 1 << 20


def swap(block, bit):
    size = lax.axis_size("narrow")
    return lax.ppermute(block, "narrow", [(n, n ^ bit) for n in range(size)])


def far_bits():
    bit = lax.axis_size("narrow") // 2
    while bit > 1:
        yield bit
        bit //= 2


def far_blocks(block):
    blocks = {0: block}
    for bit in far_bits():
        blocks.update({d ^ bit: swap(b, bit) for d, b in list(blocks.items())})
    return blocks


def pass_blocks(blocks, *earlier):
    far = {d ^ 1: swap(after(b, *earlier), 1) for d, b in blocks.items() if d > 1}
    return {**blocks, **far}


def after(block, *earlier):
    return lax.optimization_barrier((block, *earlier))[0]


def ring_order(size):
    return list(range(0, size, 2)) + list(range(size - 1, 0, -2))


def ring_step(block, way):
    order = ring_order(lax.axis_size("wide"))
    pairs = [(a, order[(i + way) % len(order)]) for i, a in enumerate(order)]
    return lax.ppermute(block, "wide", pairs)


def next_round(pair, *earlier):
    up, down = (after(b, *earlier) for b in pair)
    return ring_step(up, 1), ring_step(down, -1)


def halves(pair, axis):
    size = pair[0].shape[axis] // 2
    return (
        lax.slice_in_dim(pair[0], 0, size, axis=axis),
        lax.slice_in_dim(pair[1], size, 2 * size, axis=axis),
    )


def dot(a, b):
    return jnp.dot(a, b, preferred_element_type=F32)


def column(row):
    return jnp.transpose(jnp.broadcast_to(row, (128, row.shape[1])))[:, :1]


def whole(shape):
    return pl.BlockSpec(shape, lambda i, p: (0,) * len(shape))


def weight_spec(ds, rows, columns):
    def at(i, p):
        d = jnp.int32(ds[0])
        for j in range(1, len(ds)):
            d = jnp.where(i == j, ds[j], d)
        return (p[0] ^ d, 0)

    return pl.BlockSpec((rows, columns), at)


def add_products(x_refs, w_refs, add):
    for step, x_ref in enumerate(x_refs):

        @pl.when(pl.program_id(0) == step)
        def _():
            for j, w_ref in enumerate(w_refs):
                add(j, dot(x_ref[...], w_ref[...]))


def project_start(count, p_ref, *refs):
    x_refs, w_refs, out = refs[:count], refs[count : count + 3], refs[-1]
    cols = w_refs[0].shape[1]

    @pl.when(pl.program_id(0) == 0)
    def _():
        out[...] = jnp.zeros_like(out)

    def add(j, product):
        out[:, j * cols : (j + 1) * cols] += product

    add_products(x_refs, w_refs, add)


def stage(ds, p_ref, *refs):
    *refs, sems = refs
    weights, caches, outs = refs[:3], refs[3:5], refs[5:]
    rows = outs[0].shape[0]
    copies = []
    for i, d in enumerate(ds):
        start = pl.multiple_of((p_ref[0] ^ d) * rows, rows)
        copies += [(w.at[pl.ds(start, rows)], outs[i * 3 + j]) for j, w in enumerate(weights)]
    copies += list(zip(caches, outs[-2:]))
    copies = [
        pltpu.make_async_copy(src, dst, sems.at[k]) for k, (src, dst) in enumerate(copies)
    ]
    for copy in copies:
        copy.start()
    for copy in copies:
        copy.wait()


def project_more(count, p_ref, acc_ref, *refs):
    x_refs, w_refs, out = refs[:count], refs[count:-1], refs[-1]
    cols = w_refs[0].shape[1]
    for j in range(3):
        at = slice(j * cols, (j + 1) * cols)
        total = acc_ref[:, at]
        for i, x_ref in enumerate(x_refs):
            total = total + dot(x_ref[...], w_refs[i * 3 + j][...])
        out[:, at] = total


def attend(count, full_width, p_ref, acc_ref, squares_ref, keys_ref, values_ref, *refs):
    project_more(count, p_ref, acc_ref, *refs[:-2], refs[-1])
    out, acc = refs[-2:]
    cols = refs[count].shape[1]
    attend_heads(full_width, cols, squares_ref, keys_ref, values_ref, out, acc)


def attend_heads(full_width, cols, squares_ref, keys_ref, values_ref, out, acc):
    scenes = keys_ref.shape[0]
    branch = acc.shape[0] // scenes
    inverse = column(lax.rsqrt(squares_ref[:1] / full_width + EPSILON))
    scaling = HD ** (-0.5)
    for s in range(scenes):
        rows = slice(s * branch, (s + 1) * branch)
        scale = inverse[rows]
        for h in range(cols // HD):
            at = slice(h * HD, (h + 1) * HD)
            q, k, v = (
                (acc[rows, j * cols + h * HD : j * cols + (h + 1) * HD] * scale).astype(BF16)
                for j in range(3)
            )
            scores = (
                lax.dot_general(
                    q,
                    keys_ref[s, :, at],
                    (((1,), (1,)), ((), ())),
                    preferred_element_type=F32,
                )
                * scaling
            )
            own = jnp.sum(q.astype(F32) * k.astype(F32), axis=1, keepdims=True) * scaling
            highest = jnp.maximum(jnp.max(scores, axis=1, keepdims=True), own)
            expd = jnp.exp(scores - highest)
            own_exp = jnp.exp(own - highest)
            total = jnp.sum(expd, axis=1, keepdims=True) + own_exp
            weights = (expd / total).astype(BF16)
            own_weight = (own_exp / total).astype(BF16)
            mixed = dot(weights, values_ref[s, :, at])
            mixed = mixed + own_weight.astype(F32) * v.astype(F32)
            out[rows, at] = mixed.astype(BF16)


def update_start(count, p_ref, tokens_ref, *refs):
    x_refs, w_ref, out = refs[:count], refs[count], refs[-1]

    @pl.when(pl.program_id(0) == 0)
    def _():
        out[...] = tokens_ref[...]

    def add(j, product):
        out[...] += product

    add_products(x_refs, [w_ref], add)


def update_end(count, p_ref, acc_ref, gain_ref, policy_ref, value_ref, *refs):
    x_refs, w_ref = refs[:count], refs[count]
    latent_out, turned_out, squares_out, keep_out, give_out, acc = refs[count + 1 :]

    @pl.when(pl.program_id(0) == 0)
    def _():
        acc[...] = acc_ref[...]

    def add(j, product):
        acc[...] += product

    add_products(x_refs, [w_ref], add)

    @pl.when(pl.program_id(0) == count - 1)
    def _():
        state = acc[...]
        latent_out[...] = state.astype(BF16)
        squares = jnp.sum(state * state, axis=1, keepdims=True)
        squares_out[...] = jnp.transpose(jnp.broadcast_to(squares, (squares.shape[0], 128)))[:8]
        gained = (state * gain_ref[...]).astype(BF16)
        turned_out[...] = jnp.transpose(gained)
        policy = dot(gained, policy_ref[...])
        value = dot(gained, value_ref[...])

        @pl.when(p_ref[0] % 2 == 0)
        def _():
            keep_out[...] = policy
            give_out[...] = value.astype(BF16)

        @pl.when(p_ref[0] % 2 == 1)
        def _():
            keep_out[...] = value
            give_out[...] = policy.astype(BF16)


def heads(full_width, total_rows, p_ref, mine_ref, theirs_ref, squares_ref, policy_out_ref,
          value_out_ref, targets_ref, returns_ref, payload_out, give_out, hidden_ref):
    inverse = column(lax.rsqrt(squares_ref[:1] / full_width + EPSILON))
    pre = (mine_ref[...].astype(F32) + theirs_ref[...].astype(F32)) * inverse
    sigma = jax.nn.sigmoid(pre)
    hidden = (pre * sigma).astype(BF16)
    hidden_ref[...] = hidden
    slope = sigma * (1.0 + pre * (1.0 - sigma)) * inverse
    factor = total_rows ** (-0.5)
    count = hidden.shape[0]
    quarter = give_out.shape[0]
    part = 4 * quarter
    at = slice(count, count + quarter)

    def put_sums(grad, loss):
        shape = (payload_out.shape[0] - count - quarter, hidden.shape[1])
        rows = lax.broadcasted_iota(jnp.int32, shape, 0)
        lanes = lax.broadcasted_iota(jnp.int32, shape, 1)
        sums = jnp.where(rows == 0, grad, 0.0)
        for lane in range(3):
            term = loss.astype(BF16).astype(F32)
            sums = jnp.where((rows == 1) & (lanes == lane), term, sums)
            loss = loss - term
        payload_out[count + quarter :] = sums.astype(BF16)

    @pl.when(p_ref[0] % 2 == 0)
    def _():
        weight = policy_out_ref[...]
        logits = dot(hidden, weight)
        top = jnp.max(logits, axis=1, keepdims=True)
        log_total = top + jnp.log(jnp.sum(jnp.exp(logits - top), axis=1, keepdims=True))
        actions = lax.broadcasted_iota(jnp.int32, logits.shape, 1).astype(F32)
        onehot = (actions == column(targets_ref[...].astype(F32))).astype(F32)
        picked = jnp.sum(logits * onehot, axis=1, keepdims=True)
        loss = jnp.sum(log_total - picked, axis=0, keepdims=True)
        dlogits = ((jnp.exp(logits - log_total) - onehot) * factor).astype(BF16)
        back = lax.dot_general(
            dlogits, weight, (((1,), (1,)), ((), ())), preferred_element_type=F32
        )
        payload_out[:count] = (back * slope).astype(BF16)
        start = pl.multiple_of((p_ref[0] // 2) * part, part)
        grad = lax.dot_general(
            hidden_ref[:, pl.ds(start, part)],
            dlogits,
            (((0,), (0,)), ((), ())),
            preferred_element_type=F32,
        ).astype(BF16)
        parts = [grad[k * quarter : (k + 1) * quarter] for k in range(4)]
        payload_out[at] = jnp.concatenate(parts[:2], axis=1)
        give_out[...] = jnp.concatenate(parts[2:], axis=1)
        put_sums(jnp.zeros((1, hidden.shape[1]), F32), loss)

    @pl.when(p_ref[0] % 2 == 1)
    def _():
        weight = value_out_ref[...].astype(F32)
        hidden_f = hidden.astype(F32)
        value = jnp.sum(hidden_f * weight, axis=1, keepdims=True)
        errors = value - column(returns_ref[...])
        loss = 0.5 * jnp.sum(errors * errors, axis=0, keepdims=True)
        dvalue = (errors * factor).astype(BF16).astype(F32)
        payload_out[:count] = (dvalue * weight * slope).astype(BF16)
        payload_out[at] = jnp.zeros_like(give_out)
        give_out[...] = jnp.zeros_like(give_out)
        put_sums(jnp.sum(dvalue * hidden_f, axis=0, keepdims=True), loss)


def sums(total_rows, p_ref, *refs):
    count = (len(refs) - 3) // 4
    share_out, losses_out, grad_out = refs[-3:]

    def total(d_refs):
        *shards, ahead, back = [ref[...].astype(F32) for ref in d_refs]
        return sum(shards, jnp.concatenate([ahead, back], axis=1))

    own, other, own_sums, other_sums = (
        total(refs[k * count : (k + 1) * count]) for k in range(4)
    )
    first = p_ref[0] % 2 == 0
    quarter = own.shape[0]
    width = share_out.shape[1]
    for k, part in enumerate((jnp.where(first, own, other), jnp.where(first, other, own))):
        for j in range(2):
            at = (2 * k + j) * quarter
            share_out[at : at + quarter] = part[:, j * width : (j + 1) * width].astype(BF16)
    policy = jnp.where(first, own_sums, other_sums)
    value = jnp.where(first, other_sums, own_sums)
    grad_out[...] = value[:1].astype(BF16)

    def loss(part):
        lanes = lax.broadcasted_iota(jnp.int32, (1, part.shape[1]), 1)
        return jnp.sum(jnp.where(lanes < 3, part[1:2], 0.0), axis=1, keepdims=True) / total_rows

    lanes = lax.broadcasted_iota(jnp.int32, (1, 2), 1)
    losses_out[...] = jnp.where(lanes == 0, loss(policy), loss(value))


def join(ds, p_ref, *refs):
    out = refs[-1]
    size = refs[0].shape[0]
    for d, ref in zip(ds, refs[:-1]):
        out[pl.ds(pl.multiple_of(((p_ref[0] ^ d) // 2) * size, size), size)] = ref[...]


def gradients(counts, p_ref, *refs):
    turned_count, count = counts
    turned, own, other = refs[:turned_count], refs[turned_count:][:count], refs[turned_count:][count:-2]
    policy_out, value_out = refs[-2:]
    upper = pl.program_id(0) < pl.num_programs(0) // 2
    *turned, ahead, back = [ref[...] for ref in turned]
    turned = jnp.concatenate([*turned, jnp.where(upper, ahead, back)], axis=1)

    def product(d_refs):
        *shards, ahead, back = [ref[...] for ref in d_refs]
        shards.append(jnp.concatenate([ahead, back], axis=1))
        return dot(turned, jnp.concatenate(shards, axis=0)).astype(BF16)

    @pl.when(p_ref[0] % 2 == 0)
    def _():
        policy_out[...] = product(own)
        value_out[...] = product(other)

    @pl.when(p_ref[0] % 2 == 1)
    def _():
        value_out[...] = product(own)
        policy_out[...] = product(other)


def call(body, name, place, steps, operands, in_specs, outs, out_specs, flops, limit, scratch=()):
    bytes_accessed = sum(x.size * x.dtype.itemsize for x in (*operands, *outs))
    return pl.pallas_call(
        body,
        name=name,
        out_shape=outs,
        grid_spec=pltpu.PrefetchScalarGridSpec(
            num_scalar_prefetch=1,
            grid=(steps,),
            in_specs=in_specs,
            out_specs=out_specs,
            scratch_shapes=scratch,
        ),
        compiler_params=pltpu.CompilerParams(
            dimension_semantics=("arbitrary",), vmem_limit_bytes=limit
        ),
        cost_estimate=pl.CostEstimate(
            flops=flops, bytes_accessed=bytes_accessed, transcendentals=0
        ),
    )(place, *operands)


def per_device(
    latent,
    actions,
    action_table,
    norm1_gain,
    w_query,
    w_key,
    w_value,
    w_out,
    key_cache,
    value_cache,
    norm2_gain,
    policy_in,
    value_in,
    policy_out,
    value_out,
    targets,
    returns,
):
    rows, width = latent.shape
    narrow_size = lax.axis_size("narrow")
    wide_size = lax.axis_size("wide")
    full_width = width * narrow_size
    cols = w_query.shape[1]
    total_rows = rows * wide_size
    action_count = action_table.shape[0]
    hidden_count = policy_in.shape[1]
    index = lax.axis_index("narrow").astype(jnp.int32)
    place = index[None]
    first = index % 2 == 0
    chips = narrow_size // 2
    near = [0, 1]
    direct = list(range(2, narrow_size, 2))
    passed = [d + 1 for d in direct]

    action_onehot = (
        actions[:, None] == jnp.arange(action_count, dtype=jnp.int32)[None, :]
    ).astype(BF16)
    tokens = latent.astype(F32) + dot(action_onehot, action_table)
    gained = (tokens * norm1_gain).astype(BF16)
    squares = jnp.sum(tokens * tokens, axis=1)
    squares = squares + swap(squares, 1)
    blocks = far_blocks(gained)
    blocks[1] = swap(gained, 1)

    weights = [pltpu.with_memory_space_constraint(w, pltpu.HBM) for w in (w_query, w_key, w_value)]

    def weight_specs(ds):
        return [weight_spec(ds, width, cols)] * 3

    acc_shape = jax.ShapeDtypeStruct((rows, 3 * cols), F32)
    acc_spec = whole((rows, 3 * cols))
    x_spec = whole((rows, width))
    flops = 2 * rows * width * 3 * cols
    acc = call(
        functools.partial(project_start, len(near)), "project_near", place, len(near),
        [*(blocks[d] for d in near), *weights],
        [*[x_spec] * len(near), *weight_specs(near)],
        [acc_shape], [acc_spec], flops * len(near), 20 * MIB,
    )[0]
    far = direct + passed
    block_shape = jax.ShapeDtypeStruct((width, cols), BF16)
    cache_shape = jax.ShapeDtypeStruct(key_cache.shape, BF16)
    outs = [block_shape] * (3 * len(far)) + [cache_shape] * 2
    anywhere = pl.BlockSpec(memory_space=pl.ANY)
    *staged, keys, values = call(
        functools.partial(stage, far), "stage", place, 1,
        [*weights, *(pltpu.with_memory_space_constraint(c, pltpu.HBM) for c in (key_cache, value_cache))],
        [anywhere] * 5, outs, [anywhere] * len(outs),
        0, 4 * MIB, [pltpu.SemaphoreType.DMA((len(outs),))],
    )
    staged_direct = staged[: 3 * len(direct)]
    staged_passed = staged[3 * len(direct) :]
    block_spec = whole((width, cols))
    blocks = pass_blocks(blocks, acc, *staged, keys, values)
    for bit in far_bits():
        squares = squares + swap(after(squares, acc), bit)
    squares = jnp.broadcast_to(squares[None, :], (8, rows))
    acc = call(
        functools.partial(project_more, len(direct)), "project_direct", place, 1,
        [acc, *(blocks[d] for d in direct), *staged_direct],
        [acc_spec, *[x_spec] * len(direct), *[block_spec] * len(staged_direct)],
        [acc_shape], [acc_spec], flops * len(direct), 24 * MIB,
    )[0]
    cache_spec = whole(key_cache.shape)
    attended = call(
        functools.partial(attend, len(passed), full_width), "attend", place, 1,
        [acc, squares, keys, values, *(blocks[d] for d in passed), *staged_passed],
        [
            acc_spec, whole(squares.shape), cache_spec, cache_spec,
            *[x_spec] * len(passed), *[block_spec] * len(staged_passed),
        ],
        [jax.ShapeDtypeStruct((rows, cols), BF16)], [whole((rows, cols))],
        flops * len(passed), 32 * MIB, [pltpu.VMEM((rows, 3 * cols), F32)],
    )[0]

    blocks = far_blocks(attended)
    blocks[1] = swap(attended, 1)
    x_spec = whole((rows, cols))
    state_spec = whole((rows, width))
    state_shape = jax.ShapeDtypeStruct((rows, width), F32)
    flops = 2 * rows * width * cols
    acc = call(
        functools.partial(update_start, len(near)), "update_near", place, len(near),
        [tokens, *(blocks[d] for d in near), w_out],
        [state_spec, *[x_spec] * len(near), weight_spec(near, cols, width)],
        [state_shape], [state_spec], flops * len(near), 16 * MIB,
    )[0]
    blocks = pass_blocks(blocks, acc)
    half = (rows, hidden_count)
    new_latent, turned, squares, keep, give = call(
        functools.partial(update_end, len(far)), "update_end", place, len(far),
        [acc, norm2_gain[None, :], policy_in, value_in, *(blocks[d] for d in far), w_out],
        [
            state_spec, whole((1, width)), whole(policy_in.shape), whole(value_in.shape),
            *[x_spec] * len(far), weight_spec(far, cols, width),
        ],
        [
            jax.ShapeDtypeStruct((rows, width), BF16),
            jax.ShapeDtypeStruct((width, rows), BF16),
            jax.ShapeDtypeStruct((8, rows), F32),
            jax.ShapeDtypeStruct(half, F32),
            jax.ShapeDtypeStruct(half, BF16),
        ],
        [state_spec, whole((width, rows)), whole((8, rows)), whole(half), whole(half)],
        flops * len(far) + 4 * rows * width * hidden_count, 32 * MIB,
        [pltpu.VMEM((rows, width), F32)],
    )
    rounds = wide_size // 2
    turned_rounds = [(turned, turned)]
    turned_rounds.append(next_round(turned_rounds[0]))

    for bit in (1, *far_bits()):
        squares = squares + swap(squares, bit)
    pre = keep + swap(give, 1).astype(F32)
    mine = pre.astype(BF16)
    *upper, last = far_bits()
    for bit in upper:
        mine = (mine.astype(F32) + swap(mine, bit).astype(F32)).astype(BF16)
    theirs = after(swap(mine, last), *turned_rounds[1])
    quarter = hidden_count // chips // 4
    payload_shape = (rows + quarter + 16, hidden_count)
    payload, give = call(
        functools.partial(heads, full_width, total_rows), "heads", place, 1,
        [
            mine, theirs, squares, policy_out, value_out[None, :], targets[None, :],
            returns[None, :],
        ],
        [
            whole(half), whole(half), whole((8, rows)), whole(policy_out.shape),
            whole((1, hidden_count)), whole((1, rows)), whole((1, rows)),
        ],
        [
            jax.ShapeDtypeStruct(payload_shape, BF16),
            jax.ShapeDtypeStruct((quarter, hidden_count), BF16),
        ],
        [whole(payload_shape), whole((quarter, hidden_count))],
        6 * rows * hidden_count * action_count, 16 * MIB, [pltpu.VMEM(half, BF16)],
    )
    taken = jnp.where(first, payload[rows : rows + quarter], swap(give, 1))
    payload = lax.dynamic_update_slice(payload, taken, (rows, 0))

    payload_rounds = [(payload, payload)]
    for step in range(1, rounds + 1):
        if step < rounds:
            ahead = turned_rounds[step] if step < rounds - 1 else halves(turned_rounds[step], 0)
            turned_rounds.append(next_round(ahead))
        ahead = payload_rounds[step - 1]
        ahead = ahead if step < rounds else halves(ahead, 1)
        payload_rounds.append(next_round(ahead, *turned_rounds[step]))
    turned_all = [turned, *(b for pair in turned_rounds[1:] for b in pair)]
    payload_own = [payload, *(b for pair in payload_rounds[1:] for b in pair)]
    payload_other = [swap(b, 1) for b in payload_own]

    pieces = [*payload_own, *payload_other]
    share_shape = (4 * quarter, action_count)
    share, losses, value_out_grad = call(
        functools.partial(sums, total_rows), "sums", place, 1, [*pieces, *pieces],
        [
            pl.BlockSpec((count, b.shape[1]), functools.partial(lambda at, i, p: (at, 0), start // count))
            for start, count in ((rows, quarter), (rows + quarter, 16))
            for b in pieces
        ],
        [
            jax.ShapeDtypeStruct(share_shape, BF16),
            jax.ShapeDtypeStruct((1, 2), F32),
            jax.ShapeDtypeStruct((1, hidden_count), BF16),
        ],
        [whole(share_shape), whole((1, 2)), whole((1, hidden_count))], 0, 8 * MIB,
    )
    losses = losses.reshape(2)
    value_out_grad = value_out_grad.reshape(hidden_count)
    shares = far_blocks(share)
    policy_out_grad = call(
        functools.partial(join, list(shares)), "join", place, 1, list(shares.values()),
        [whole(share_shape)] * len(shares),
        [jax.ShapeDtypeStruct((hidden_count, action_count), BF16)],
        [whole((hidden_count, action_count))], 0, 8 * MIB,
    )[0]

    block = 256
    half_steps = width // block // 2
    turned_specs = [pl.BlockSpec((block, rows), lambda i, p: (i, 0))] * (len(turned_all) - 2)
    turned_specs += [
        pl.BlockSpec((block, rows), lambda i, p: (jnp.minimum(i, half_steps - 1), 0)),
        pl.BlockSpec((block, rows), lambda i, p: (jnp.maximum(i - half_steps, 0), 0)),
    ]
    dpre_specs = [
        pl.BlockSpec((rows, b.shape[1]), lambda i, p: (0, 0), pipeline_mode=pl.Buffered(1))
        for b in payload_own
    ]
    grad_shape = jax.ShapeDtypeStruct((width, hidden_count), BF16)
    grad_spec = pl.BlockSpec((block, hidden_count), lambda i, p: (i, 0))
    policy_in_grad, value_in_grad = call(
        functools.partial(gradients, (len(turned_all), len(payload_own))), "gradients", place,
        width // block, [*turned_all, *payload_own, *payload_other],
        [*turned_specs, *dpre_specs, *dpre_specs],
        [grad_shape, grad_shape], [grad_spec, grad_spec],
        4 * total_rows * width * hidden_count, 28 * MIB,
    )
    return (new_latent, losses, policy_in_grad, value_in_grad, policy_out_grad, value_out_grad)


def solution(mesh):
    placed = (
        P("wide", "narrow"),
        P("wide"),
        P(None, "narrow"),
        P("narrow"),
        P(None, "narrow"),
        P(None, "narrow"),
        P(None, "narrow"),
        P(None, "narrow"),
        P("wide", None, "narrow"),
        P("wide", None, "narrow"),
        P("narrow"),
        P("narrow", None),
        P("narrow", None),
        P(),
        P(),
        P("wide"),
        P("wide"),
    )
    return jax.shard_map(
        per_device,
        mesh=mesh,
        in_specs=placed,
        out_specs=(P("wide", "narrow"), P(), P("narrow", None), P("narrow", None), P(), P()),
        check_vma=False,
    )
```

```python
import functools

import jax
import jax.numpy as jnp
from jax import lax
from jax.experimental import pallas as pl
from jax.experimental.pallas import tpu as pltpu
from jax.sharding import PartitionSpec as P

HD = 128
EPSILON = 1e-05
EARLY = 3
F32 = jnp.float32
BF16 = jnp.bfloat16
MIB = 1 << 20


def swap(block, bit):
    size = lax.axis_size("narrow")
    return lax.ppermute(block, "narrow", [(n, n ^ bit) for n in range(size)])


def far_bits():
    bit = lax.axis_size("narrow") // 2
    while bit > 1:
        yield bit
        bit //= 2


def far_blocks(block):
    blocks = {0: block}
    for bit in far_bits():
        blocks.update({d ^ bit: swap(b, bit) for d, b in list(blocks.items())})
    return blocks


def pass_blocks(blocks, *earlier):
    far = {d ^ 1: swap(after(b, *earlier), 1) for d, b in blocks.items() if d > 1}
    return {**blocks, **far}


def after(block, *earlier):
    return lax.optimization_barrier((block, *earlier))[0]


def ring_order(size):
    return list(range(0, size, 2)) + list(range(size - 1, 0, -2))


def ring_step(block, way):
    order = ring_order(lax.axis_size("wide"))
    pairs = [(a, order[(i + way) % len(order)]) for i, a in enumerate(order)]
    return lax.ppermute(block, "wide", pairs)


class Ring:
    def __init__(self):
        self.arrived = []

    def step(self, *pair):
        held = self.arrived[-2] if len(self.arrived) > 1 else ((), ())
        up, down = (after(b, *h) for b, h in zip(pair, held))
        self.arrived.append(((ring_step(up, 1),), (ring_step(down, -1),)))
        return [self.arrived[-1][0][0], self.arrived[-1][1][0]]


def dot(a, b):
    return jnp.dot(a, b, preferred_element_type=F32)


def column(row):
    return jnp.transpose(jnp.broadcast_to(row, (128, row.shape[1])))[:, :1]


def whole(shape):
    return pl.BlockSpec(shape, lambda i, p: (0,) * len(shape))


def weight_spec(ds, rows, columns):
    def at(i, p):
        d = jnp.int32(ds[0])
        for j in range(1, len(ds)):
            d = jnp.where(i == j, ds[j], d)
        return (p[0] ^ d, 0)

    return pl.BlockSpec((rows, columns), at)


def add_products(x_refs, w_refs, add):
    for step, x_ref in enumerate(x_refs):

        @pl.when(pl.program_id(0) == step)
        def _():
            for j, w_ref in enumerate(w_refs):
                add(j, dot(x_ref[...], w_ref[...]))


def row_of(values):
    return jnp.transpose(jnp.broadcast_to(values, (values.shape[0], 128)))[:8]


def embed(p_ref, latent_ref, actions_ref, table_ref, gain_ref, tokens_out, block_out):
    count = latent_ref.shape[0]
    shape = (table_ref.shape[0], count)
    onehot = (lax.broadcasted_iota(jnp.int32, shape, 0) == actions_ref[...]).astype(BF16)
    picked = lax.dot_general(
        onehot, table_ref[...], (((0,), (0,)), ((), ())), preferred_element_type=F32
    )
    tokens = latent_ref[...].astype(F32) + picked
    tokens_out[...] = tokens
    block_out[:count] = (tokens * gain_ref[...]).astype(BF16)
    block_out[count:] = jnp.zeros_like(block_out[count:])
    rest = row_of(jnp.sum(tokens * tokens, axis=1, keepdims=True))[:1]
    rows = lax.broadcasted_iota(jnp.int32, (16, count), 0)
    terms = jnp.zeros((16, count), F32)
    for k in range(3):
        term = rest.astype(BF16).astype(F32)
        terms = jnp.where(rows == k, term, terms)
        rest = rest - term
    block_out[count:, :count] = terms.astype(BF16)


def begin(near, far, scenes, p_ref, *refs):
    count = scenes * len(near)
    x_refs, weights, caches = refs[:count], refs[count : count + 3], refs[count + 3 : count + 5]
    acc, *outs, held, sems = refs[count + 5 :]
    size, cols = held.shape[1:]
    copies = []

    def send(src, dst):
        copies.append(pltpu.make_async_copy(src, dst, sems.at[len(copies)]))
        copies[-1].start()

    for i, d in enumerate(near + far):
        start = pl.multiple_of((p_ref[0] ^ d) * size, size)
        for j, w_ref in enumerate(weights):
            k = i * 3 + j
            send(
                w_ref.at[pl.ds(start, size)],
                held.at[k] if i < len(near) else outs[k - 3 * len(near)],
            )
    for src, dst in zip(caches, outs[-2:]):
        send(src, dst)
    for i in range(len(near)):
        x = jnp.concatenate([ref[...] for ref in x_refs[i * scenes : (i + 1) * scenes]], axis=0)
        for j in range(3):
            copies[i * 3 + j].wait()
            product = dot(x, held[i * 3 + j])
            at = slice(j * cols, (j + 1) * cols)
            acc[:, at] = product if i == 0 else acc[:, at] + product
    for copy in copies[3 * len(near) :]:
        copy.wait()


def project_more(count, p_ref, acc_ref, *refs):
    x_refs, w_refs, out = refs[:count], refs[count:-1], refs[-1]
    cols = w_refs[0].shape[1]
    for j in range(3):
        at = slice(j * cols, (j + 1) * cols)
        total = acc_ref[:, at]
        for i, x_ref in enumerate(x_refs):
            total = total + dot(x_ref[...], w_refs[i * 3 + j][...])
        out[:, at] = total


def attend(count, sources, full_width, p_ref, acc_ref, keys_ref, values_ref, *refs):
    squares_refs, refs = refs[:sources], refs[sources:]
    project_more(count, p_ref, acc_ref, *refs[:-2], refs[-1])
    out, acc = refs[-2:]
    cols = refs[count].shape[1]
    squares = sum(jnp.sum(ref[:8].astype(F32), axis=0, keepdims=True) for ref in squares_refs)
    attend_heads(full_width, cols, squares, keys_ref, values_ref, out, acc)


def attend_heads(full_width, cols, squares, keys_ref, values_ref, out, acc):
    scenes = keys_ref.shape[0]
    branch = acc.shape[0] // scenes
    inverse = column(lax.rsqrt(squares / full_width + EPSILON))
    scaling = HD ** (-0.5)
    for s in range(scenes):
        rows = slice(s * branch, (s + 1) * branch)
        scale = inverse[rows]
        for h in range(cols // HD):
            at = slice(h * HD, (h + 1) * HD)
            q, k, v = (
                (acc[rows, j * cols + h * HD : j * cols + (h + 1) * HD] * scale).astype(BF16)
                for j in range(3)
            )
            scores = (
                lax.dot_general(
                    q,
                    keys_ref[s, :, at],
                    (((1,), (1,)), ((), ())),
                    preferred_element_type=F32,
                )
                * scaling
            )
            own = jnp.sum(q.astype(F32) * k.astype(F32), axis=1, keepdims=True) * scaling
            highest = jnp.maximum(jnp.max(scores, axis=1, keepdims=True), own)
            expd = jnp.exp(scores - highest)
            own_exp = jnp.exp(own - highest)
            total = jnp.sum(expd, axis=1, keepdims=True) + own_exp
            weights = (expd / total).astype(BF16)
            own_weight = (own_exp / total).astype(BF16)
            mixed = dot(weights, values_ref[s, :, at])
            mixed = mixed + own_weight.astype(F32) * v.astype(F32)
            out[rows, at] = mixed.astype(BF16)


def update(count, p_ref, tokens_ref, gain_ref, policy_ref, value_ref, *refs):
    x_refs, w_ref = refs[:count], refs[count]
    latent_out, keep_out, give_out, squares_out, turned_out, acc = refs[-6:]

    @pl.when(pl.program_id(0) == 0)
    def _():
        acc[...] = tokens_ref[...]

    def add(j, product):
        acc[...] += product

    add_products(x_refs, [w_ref], add)

    @pl.when(pl.program_id(0) == count - 1)
    def _():
        state = acc[...]
        latent_out[...] = state.astype(BF16)
        squares = jnp.sum(state * state, axis=1, keepdims=True)
        squares_out[...] = row_of(squares)
        gained = (state * gain_ref[...]).astype(BF16)
        turned_out[...] = jnp.transpose(gained)
        policy = dot(gained, policy_ref[...])
        value = dot(gained, value_ref[...])

        @pl.when(p_ref[0] % 2 == 0)
        def _():
            keep_out[...] = policy
            give_out[...] = value.astype(BF16)

        @pl.when(p_ref[0] % 2 == 1)
        def _():
            keep_out[...] = value
            give_out[...] = policy.astype(BF16)


def heads(full_width, total_rows, p_ref, mine_ref, theirs_ref, squares_ref, policy_out_ref,
          value_out_ref, targets_ref, returns_ref, payload_out, give_out, hidden_ref):
    inverse = column(lax.rsqrt(squares_ref[:1] / full_width + EPSILON))
    pre = (mine_ref[...].astype(F32) + theirs_ref[...].astype(F32)) * inverse
    sigma = jax.nn.sigmoid(pre)
    hidden = (pre * sigma).astype(BF16)
    hidden_ref[...] = hidden
    slope = sigma * (1.0 + pre * (1.0 - sigma)) * inverse
    factor = total_rows ** (-0.5)
    count = hidden.shape[0]
    quarter = give_out.shape[0]
    part = 4 * quarter
    at = slice(count, count + quarter)

    def put_sums(grad, loss):
        shape = (payload_out.shape[0] - count - quarter, hidden.shape[1])
        rows = lax.broadcasted_iota(jnp.int32, shape, 0)
        lanes = lax.broadcasted_iota(jnp.int32, shape, 1)
        sums = jnp.where(rows == 0, grad, 0.0)
        for lane in range(3):
            term = loss.astype(BF16).astype(F32)
            sums = jnp.where((rows == 1) & (lanes == lane), term, sums)
            loss = loss - term
        payload_out[count + quarter :] = sums.astype(BF16)

    @pl.when(p_ref[0] % 2 == 0)
    def _():
        weight = policy_out_ref[...]
        logits = dot(hidden, weight)
        top = jnp.max(logits, axis=1, keepdims=True)
        log_total = top + jnp.log(jnp.sum(jnp.exp(logits - top), axis=1, keepdims=True))
        actions = lax.broadcasted_iota(jnp.int32, logits.shape, 1).astype(F32)
        onehot = (actions == column(targets_ref[...].astype(F32))).astype(F32)
        picked = jnp.sum(logits * onehot, axis=1, keepdims=True)
        loss = jnp.sum(log_total - picked, axis=0, keepdims=True)
        dlogits = ((jnp.exp(logits - log_total) - onehot) * factor).astype(BF16)
        back = lax.dot_general(
            dlogits, weight, (((1,), (1,)), ((), ())), preferred_element_type=F32
        )
        payload_out[:count] = (back * slope).astype(BF16)
        start = pl.multiple_of((p_ref[0] // 2) * part, part)
        grad = lax.dot_general(
            hidden_ref[:, pl.ds(start, part)],
            dlogits,
            (((0,), (0,)), ((), ())),
            preferred_element_type=F32,
        ).astype(BF16)
        parts = [grad[k * quarter : (k + 1) * quarter] for k in range(4)]
        payload_out[at] = jnp.concatenate(parts[:2], axis=1)
        give_out[...] = jnp.concatenate(parts[2:], axis=1)
        put_sums(jnp.zeros((1, hidden.shape[1]), F32), loss)

    @pl.when(p_ref[0] % 2 == 1)
    def _():
        weight = value_out_ref[...].astype(F32)
        hidden_f = hidden.astype(F32)
        value = jnp.sum(hidden_f * weight, axis=1, keepdims=True)
        errors = value - column(returns_ref[...])
        loss = 0.5 * jnp.sum(errors * errors, axis=0, keepdims=True)
        dvalue = (errors * factor).astype(BF16).astype(F32)
        payload_out[:count] = (dvalue * weight * slope).astype(BF16)
        payload_out[at] = jnp.zeros_like(give_out)
        give_out[...] = jnp.zeros_like(give_out)
        put_sums(jnp.sum(dvalue * hidden_f, axis=0, keepdims=True), loss)


def sums(total_rows, p_ref, *refs):
    count = (len(refs) - 3) // 4
    share_out, losses_out, grad_out = refs[-3:]

    def total(d_refs):
        *shards, ahead, back = [ref[...].astype(F32) for ref in d_refs]
        return sum(shards, jnp.concatenate([ahead, back], axis=1))

    own, other, own_sums, other_sums = (
        total(refs[k * count : (k + 1) * count]) for k in range(4)
    )
    first = p_ref[0] % 2 == 0
    quarter = own.shape[0]
    width = share_out.shape[1]
    for k, part in enumerate((jnp.where(first, own, other), jnp.where(first, other, own))):
        for j in range(2):
            at = (2 * k + j) * quarter
            share_out[at : at + quarter] = part[:, j * width : (j + 1) * width].astype(BF16)
    policy = jnp.where(first, own_sums, other_sums)
    value = jnp.where(first, other_sums, own_sums)
    grad_out[...] = value[:1].astype(BF16)

    def loss(part):
        lanes = lax.broadcasted_iota(jnp.int32, (1, part.shape[1]), 1)
        return jnp.sum(jnp.where(lanes < 3, part[1:2], 0.0), axis=1, keepdims=True) / total_rows

    lanes = lax.broadcasted_iota(jnp.int32, (1, 2), 1)
    losses_out[...] = jnp.where(lanes == 0, loss(policy), loss(value))


def join(ds, p_ref, *refs):
    out = refs[-1]
    size = refs[0].shape[0]
    for d, ref in zip(ds, refs[:-1]):
        out[pl.ds(pl.multiple_of(((p_ref[0] ^ d) // 2) * size, size), size)] = ref[...]


def gradients(counts, p_ref, *refs):
    turned_count, count = counts
    turned, own, other = refs[:turned_count], refs[turned_count:][:count], refs[turned_count:][count:-2]
    policy_out, value_out = refs[-2:]
    turned = jnp.concatenate([ref[...] for ref in turned], axis=1)

    def product(d_refs):
        *shards, ahead, back = [ref[...] for ref in d_refs]
        shards.append(jnp.concatenate([ahead, back], axis=1))
        return dot(turned, jnp.concatenate(shards, axis=0)).astype(BF16)

    @pl.when(p_ref[0] % 2 == 0)
    def _():
        policy_out[...] = product(own)
        value_out[...] = product(other)

    @pl.when(p_ref[0] % 2 == 1)
    def _():
        value_out[...] = product(own)
        policy_out[...] = product(other)


def call(body, name, place, steps, operands, in_specs, outs, out_specs, flops, limit, scratch=(), aliases=None):
    bytes_accessed = sum(x.size * x.dtype.itemsize for x in (*operands, *outs))
    return pl.pallas_call(
        body,
        name=name,
        out_shape=outs,
        input_output_aliases=aliases or {},
        grid_spec=pltpu.PrefetchScalarGridSpec(
            num_scalar_prefetch=1,
            grid=(steps,),
            in_specs=in_specs,
            out_specs=out_specs,
            scratch_shapes=scratch,
        ),
        compiler_params=pltpu.CompilerParams(
            dimension_semantics=("arbitrary",), vmem_limit_bytes=limit
        ),
        cost_estimate=pl.CostEstimate(
            flops=flops, bytes_accessed=bytes_accessed, transcendentals=0
        ),
    )(place, *operands)


def per_device(
    latent,
    actions,
    action_table,
    norm1_gain,
    w_query,
    w_key,
    w_value,
    w_out,
    key_cache,
    value_cache,
    norm2_gain,
    policy_in,
    value_in,
    policy_out,
    value_out,
    targets,
    returns,
):
    rows, width = latent.shape
    narrow_size = lax.axis_size("narrow")
    wide_size = lax.axis_size("wide")
    full_width = width * narrow_size
    cols = w_query.shape[1]
    total_rows = rows * wide_size
    action_count = action_table.shape[0]
    hidden_count = policy_in.shape[1]
    index = lax.axis_index("narrow").astype(jnp.int32)
    place = index[None]
    first = index % 2 == 0
    chips = narrow_size // 2
    near = [0, 1]
    direct = list(range(2, narrow_size, 2))
    passed = [d + 1 for d in direct]

    far = direct + passed
    scenes = key_cache.shape[0]
    branch = rows // scenes
    hbm = functools.partial(pltpu.with_memory_space_constraint, memory_space=pltpu.HBM)

    tokens, blocks = [], []
    block_shape = (branch + 16, width)
    state_spec = whole((branch, width))
    for s in range(scenes):
        at = functools.partial(lambda s, i, p: (s, 0), s)
        one_tokens, block = call(
            embed, f"embed{s}", place, 1,
            [hbm(latent), actions[None, :], hbm(action_table), norm1_gain[None, :]],
            [
                pl.BlockSpec((branch, width), at),
                pl.BlockSpec((1, branch), functools.partial(lambda s, i, p: (0, s), s)),
                whole(action_table.shape), whole((1, width)),
            ],
            [
                jax.ShapeDtypeStruct((branch, width), F32),
                jax.ShapeDtypeStruct(block_shape, BF16),
            ],
            [state_spec, whole(block_shape)], 2 * branch * width * action_count, 8 * MIB,
        )
        tokens.append(one_tokens)
        blocks.append({**far_blocks(block), 1: swap(block, 1)})

    weights = [hbm(w) for w in (w_query, w_key, w_value)]
    x_spec = whole((branch, width))
    acc_shape = jax.ShapeDtypeStruct((rows, 3 * cols), F32)
    weight_shape = jax.ShapeDtypeStruct((width, cols), BF16)
    weight_block = whole((width, cols))
    cache_shape = jax.ShapeDtypeStruct(key_cache.shape, BF16)
    outs = [weight_shape] * (3 * len(far)) + [cache_shape] * 2
    anywhere = pl.BlockSpec(memory_space=pl.ANY)
    flops = 2 * branch * width * 3 * cols
    acc, *staged, keys, values = call(
        functools.partial(begin, near, far, scenes), "begin", place, 1,
        [
            *(blocks[s][d] for d in near for s in range(scenes)), *weights,
            hbm(key_cache), hbm(value_cache),
        ],
        [*[x_spec] * (scenes * len(near)), *[anywhere] * 5],
        [acc_shape, *outs], [whole(acc_shape.shape), *[anywhere] * len(outs)],
        flops * scenes * len(near), 20 * MIB,
        [
            pltpu.VMEM((3 * len(near), width, cols), BF16),
            pltpu.SemaphoreType.DMA((3 * len(near) + len(outs),)),
        ],
    )
    staged_direct = staged[: 3 * len(direct)]
    staged_passed = staged[3 * len(direct) :]

    part_spec = whole((branch, 3 * cols))
    squares_spec = pl.BlockSpec((16, branch), lambda i, p: (branch // 16, 0))
    attended = []
    for s in range(scenes):
        blocks[s] = pass_blocks(blocks[s], acc)
        part = call(
            functools.partial(project_more, len(direct)), f"project{s}", place, 1,
            [acc, *(blocks[s][d] for d in direct), *staged_direct],
            [
                pl.BlockSpec(
                    (branch, 3 * cols), functools.partial(lambda s, i, p: (s, 0), s)
                ),
                *[x_spec] * len(direct), *[weight_block] * len(staged_direct),
            ],
            [jax.ShapeDtypeStruct((branch, 3 * cols), F32)], [part_spec],
            flops * len(direct), 20 * MIB,
        )[0]
        cache_spec = pl.BlockSpec(
            (1, *key_cache.shape[1:]), functools.partial(lambda s, i, p: (s, 0, 0), s)
        )
        one = call(
            functools.partial(attend, len(passed), narrow_size, full_width), f"attend{s}", place, 1,
            [
                part, keys, values, *blocks[s].values(),
                *(blocks[s][d] for d in passed), *staged_passed,
            ],
            [
                part_spec, cache_spec, cache_spec, *[squares_spec] * narrow_size,
                *[x_spec] * len(passed), *[weight_block] * len(staged_passed),
            ],
            [jax.ShapeDtypeStruct((branch, cols), BF16)], [whole((branch, cols))],
            flops * len(passed), 20 * MIB, [pltpu.VMEM((branch, 3 * cols), F32)],
        )[0]
        attended.append({**far_blocks(one), 1: swap(one, 1)})

    half = (rows, hidden_count)
    full_shapes = [
        jax.ShapeDtypeStruct((rows, width), BF16),
        jax.ShapeDtypeStruct(half, F32),
        jax.ShapeDtypeStruct(half, BF16),
        jax.ShapeDtypeStruct((8, rows), F32),
    ]
    filled, turned, shards = [], [], []
    ring = Ring()
    for s in range(scenes):
        ds = near + far
        around = pass_blocks(attended[s])
        at = functools.partial(lambda s, i, p: (s, 0), s)
        operands = [
            tokens[s], norm2_gain[None, :], policy_in, value_in,
            *(around[d] for d in ds), w_out, *filled,
        ]
        *filled, one = call(
            functools.partial(update, len(ds)), f"update{s}", place, len(ds), operands,
            [
                state_spec, whole((1, width)), whole(policy_in.shape), whole(value_in.shape),
                *[whole((branch, cols))] * len(ds), weight_spec(ds, cols, width),
                *[anywhere] * len(filled),
            ],
            [*full_shapes, jax.ShapeDtypeStruct((width, branch), BF16)],
            [
                pl.BlockSpec((branch, width), at),
                pl.BlockSpec((branch, hidden_count), at),
                pl.BlockSpec((branch, hidden_count), at),
                pl.BlockSpec((8, branch), functools.partial(lambda s, i, p: (0, s), s)),
                whole((width, branch)),
            ],
            2 * branch * width * (cols * len(ds) + 2 * hidden_count), 28 * MIB,
            [pltpu.VMEM((branch, width), F32)],
            {1 + len(operands) - len(filled) + k: k for k in range(len(filled))},
        )
        turned.append(one)
        if s == 0:
            shards.append([ring.step(one, one)])
    new_latent, keep, give, squares = filled

    for bit in (1, *far_bits()):
        squares = squares + swap(squares, bit)
    pre = keep + swap(give, 1).astype(F32)
    mine = pre.astype(BF16)
    *upper, last = far_bits()
    for bit in upper:
        mine = (mine.astype(F32) + swap(mine, bit).astype(F32)).astype(BF16)
    rounds = wide_size // 2
    while len(shards[0]) < min(EARLY, rounds - 1):
        shards[0].append(ring.step(*shards[0][-1]))
    theirs = after(swap(mine, last), *shards[0][-1])
    quarter = hidden_count // chips // 4
    payload_shape = (rows + quarter + 16, hidden_count)
    payload, give = call(
        functools.partial(heads, full_width, total_rows), "heads", place, 1,
        [
            mine, theirs, squares, policy_out, value_out[None, :], targets[None, :],
            returns[None, :],
        ],
        [
            whole(half), whole(half), whole((8, rows)), whole(policy_out.shape),
            whole((1, hidden_count)), whole((1, rows)), whole((1, rows)),
        ],
        [
            jax.ShapeDtypeStruct(payload_shape, BF16),
            jax.ShapeDtypeStruct((quarter, hidden_count), BF16),
        ],
        [whole(payload_shape), whole((quarter, hidden_count))],
        6 * rows * hidden_count * action_count, 16 * MIB, [pltpu.VMEM(half, BF16)],
    )
    taken = jnp.where(first, payload[rows : rows + quarter], swap(give, 1))
    payload = lax.dynamic_update_slice(payload, taken, (rows, 0))

    shards += [[ring.step(one, one)] for one in turned[1:]]
    payload_rounds = [[payload, payload]]
    for shard in shards:
        while len(shard) < rounds - 1:
            if len(payload_rounds) < rounds:
                payload_rounds.append(ring.step(*payload_rounds[-1]))
            shard.append(ring.step(*shard[-1]))
    while len(payload_rounds) < rounds:
        payload_rounds.append(ring.step(*payload_rounds[-1]))
    cut = scenes // 2
    for one, other in zip(shards[:cut], shards[cut:]):
        up, down = ring.step(one[-1][0], other[-1][1])
        one.append([up])
        other.append([down])
    size = hidden_count // 2
    up, down = payload_rounds[-1]
    payload_rounds.append(ring.step(up[:, :size], down[:, size:]))
    turned_all = list(turned)
    for step in range(rounds):
        for way in range(len(shards[0][step])):
            turned_all += [shard[step][way] for shard in shards]
    payload_own = [payload, *(b for pair in payload_rounds[1:] for b in pair)]
    payload_other = [swap(b, 1) for b in payload_own]

    pieces = [*payload_own, *payload_other]
    share_shape = (4 * quarter, action_count)
    share, losses, value_out_grad = call(
        functools.partial(sums, total_rows), "sums", place, 1, [*pieces, *pieces],
        [
            pl.BlockSpec((count, b.shape[1]), functools.partial(lambda at, i, p: (at, 0), start // count))
            for start, count in ((rows, quarter), (rows + quarter, 16))
            for b in pieces
        ],
        [
            jax.ShapeDtypeStruct(share_shape, BF16),
            jax.ShapeDtypeStruct((1, 2), F32),
            jax.ShapeDtypeStruct((1, hidden_count), BF16),
        ],
        [whole(share_shape), whole((1, 2)), whole((1, hidden_count))], 0, 8 * MIB,
    )
    losses = losses.reshape(2)
    value_out_grad = value_out_grad.reshape(hidden_count)
    shares = far_blocks(share)
    policy_out_grad = call(
        functools.partial(join, list(shares)), "join", place, 1, list(shares.values()),
        [whole(share_shape)] * len(shares),
        [jax.ShapeDtypeStruct((hidden_count, action_count), BF16)],
        [whole((hidden_count, action_count))], 0, 8 * MIB,
    )[0]

    block = 256
    turned_specs = [pl.BlockSpec((block, branch), lambda i, p: (i, 0))] * len(turned_all)
    dpre_specs = [
        pl.BlockSpec((rows, b.shape[1]), lambda i, p: (0, 0), pipeline_mode=pl.Buffered(1))
        for b in payload_own
    ]
    grad_shape = jax.ShapeDtypeStruct((width, hidden_count), BF16)
    grad_spec = pl.BlockSpec((block, hidden_count), lambda i, p: (i, 0))
    policy_in_grad, value_in_grad = call(
        functools.partial(gradients, (len(turned_all), len(payload_own))), "gradients", place,
        width // block, [*turned_all, *payload_own, *payload_other],
        [*turned_specs, *dpre_specs, *dpre_specs],
        [grad_shape, grad_shape], [grad_spec, grad_spec],
        4 * total_rows * width * hidden_count, 28 * MIB,
    )
    return (new_latent, losses, policy_in_grad, value_in_grad, policy_out_grad, value_out_grad)


def solution(mesh):
    placed = (
        P("wide", "narrow"),
        P("wide"),
        P(None, "narrow"),
        P("narrow"),
        P(None, "narrow"),
        P(None, "narrow"),
        P(None, "narrow"),
        P(None, "narrow"),
        P("wide", None, "narrow"),
        P("wide", None, "narrow"),
        P("narrow"),
        P("narrow", None),
        P("narrow", None),
        P(),
        P(),
        P("wide"),
        P("wide"),
    )
    return jax.shard_map(
        per_device,
        mesh=mesh,
        in_specs=placed,
        out_specs=(P("wide", "narrow"), P(), P("narrow", None), P("narrow", None), P(), P()),
        check_vma=False,
    )
```

```python
import functools

import jax
import jax.numpy as jnp
from jax import lax
from jax.experimental import pallas as pl
from jax.experimental.pallas import tpu as pltpu
from jax.sharding import PartitionSpec as P

HD = 128
EPSILON = 1e-05
EARLY = 3
F32 = jnp.float32
BF16 = jnp.bfloat16
MIB = 1 << 20


def swap(block, bit):
    size = lax.axis_size("narrow")
    return lax.ppermute(block, "narrow", [(n, n ^ bit) for n in range(size)])


def far_bits():
    bit = lax.axis_size("narrow") // 2
    while bit > 1:
        yield bit
        bit //= 2


def far_blocks(block):
    blocks = {0: block}
    for bit in far_bits():
        blocks.update({d ^ bit: swap(b, bit) for d, b in list(blocks.items())})
    return blocks


def pass_blocks(blocks, *earlier):
    far = {d ^ 1: swap(after(b, *earlier), 1) for d, b in blocks.items() if d > 1}
    return {**blocks, **far}


def after(block, *earlier):
    return lax.optimization_barrier((block, *earlier))[0]


def ring_order(size):
    return list(range(0, size, 2)) + list(range(size - 1, 0, -2))


def ring_step(block, way):
    order = ring_order(lax.axis_size("wide"))
    pairs = [(a, order[(i + way) % len(order)]) for i, a in enumerate(order)]
    return lax.ppermute(block, "wide", pairs)


class Ring:
    def __init__(self):
        self.arrived = []

    def step(self, *pair):
        held = self.arrived[-2] if len(self.arrived) > 1 else ((), ())
        up, down = (after(b, *h) for b, h in zip(pair, held))
        self.arrived.append(((ring_step(up, 1),), (ring_step(down, -1),)))
        return [self.arrived[-1][0][0], self.arrived[-1][1][0]]


def dot(a, b):
    return jnp.dot(a, b, preferred_element_type=F32)


def column(row):
    return jnp.transpose(jnp.broadcast_to(row, (128, row.shape[1])))[:, :1]


def whole(shape):
    return pl.BlockSpec(shape, lambda i, p: (0,) * len(shape))


def weight_spec(ds, rows, columns):
    def at(i, p):
        d = jnp.int32(ds[0])
        for j in range(1, len(ds)):
            d = jnp.where(i == j, ds[j], d)
        return (p[0] ^ d, 0)

    return pl.BlockSpec((rows, columns), at)


def add_products(x_refs, w_refs, add):
    for step, x_ref in enumerate(x_refs):

        @pl.when(pl.program_id(0) == step)
        def _():
            for j, w_ref in enumerate(w_refs):
                add(j, dot(x_ref[...], w_ref[...]))


def row_of(values):
    return jnp.transpose(jnp.broadcast_to(values, (values.shape[0], 128)))[:8]


def embed(scenes, p_ref, latent_ref, actions_ref, table_ref, gain_ref, tokens_out, *blocks_out):
    shape = (table_ref.shape[0], latent_ref.shape[0])
    onehot = (lax.broadcasted_iota(jnp.int32, shape, 0) == actions_ref[...]).astype(BF16)
    picked = lax.dot_general(
        onehot, table_ref[...], (((0,), (0,)), ((), ())), preferred_element_type=F32
    )
    tokens = latent_ref[...].astype(F32) + picked
    tokens_out[...] = tokens
    count = latent_ref.shape[0] // scenes
    rows = lax.broadcasted_iota(jnp.int32, (16, count), 0)
    for s, block_out in enumerate(blocks_out):
        part = tokens[s * count : (s + 1) * count]
        block_out[:count] = (part * gain_ref[...]).astype(BF16)
        block_out[count:] = jnp.zeros_like(block_out[count:])
        rest = row_of(jnp.sum(part * part, axis=1, keepdims=True))[:1]
        terms = jnp.zeros((16, count), F32)
        for k in range(3):
            term = rest.astype(BF16).astype(F32)
            terms = jnp.where(rows == k, term, terms)
            rest = rest - term
        block_out[count:, :count] = terms.astype(BF16)


def begin(near, far, scenes, p_ref, *refs):
    count = scenes * len(near)
    x_refs, weights, caches = refs[:count], refs[count : count + 3], refs[count + 3 : count + 5]
    acc, *outs, held, sems = refs[count + 5 :]
    size, cols = held.shape[1:]
    copies = []

    def send(src, dst):
        copies.append(pltpu.make_async_copy(src, dst, sems.at[len(copies)]))
        copies[-1].start()

    for i, d in enumerate(near + far):
        start = pl.multiple_of((p_ref[0] ^ d) * size, size)
        for j, w_ref in enumerate(weights):
            k = i * 3 + j
            send(
                w_ref.at[pl.ds(start, size)],
                held.at[k] if i < len(near) else outs[k - 3 * len(near)],
            )
    for src, dst in zip(caches, outs[-2:]):
        send(src, dst)
    for i in range(len(near)):
        x = jnp.concatenate([ref[...] for ref in x_refs[i * scenes : (i + 1) * scenes]], axis=0)
        for j in range(3):
            copies[i * 3 + j].wait()
            product = dot(x, held[i * 3 + j])
            at = slice(j * cols, (j + 1) * cols)
            acc[:, at] = product if i == 0 else acc[:, at] + product
    for copy in copies[3 * len(near) :]:
        copy.wait()


def project_more(count, p_ref, acc_ref, *refs):
    x_refs, w_refs, out = refs[:count], refs[count:-1], refs[-1]
    cols = w_refs[0].shape[1]
    for j in range(3):
        at = slice(j * cols, (j + 1) * cols)
        total = acc_ref[:, at]
        for i, x_ref in enumerate(x_refs):
            total = total + dot(x_ref[...], w_refs[i * 3 + j][...])
        out[:, at] = total


def attend(count, sources, full_width, p_ref, acc_ref, keys_ref, values_ref, *refs):
    squares_refs, refs = refs[:sources], refs[sources:]
    project_more(count, p_ref, acc_ref, *refs[:-2], refs[-1])
    out, acc = refs[-2:]
    cols = refs[count].shape[1]
    squares = sum(jnp.sum(ref[:8].astype(F32), axis=0, keepdims=True) for ref in squares_refs)
    attend_heads(full_width, cols, squares, keys_ref, values_ref, out, acc)


def attend_heads(full_width, cols, squares, keys_ref, values_ref, out, acc):
    scenes = keys_ref.shape[0]
    branch = acc.shape[0] // scenes
    inverse = column(lax.rsqrt(squares / full_width + EPSILON))
    scaling = HD ** (-0.5)
    for s in range(scenes):
        rows = slice(s * branch, (s + 1) * branch)
        scale = inverse[rows]
        for h in range(cols // HD):
            at = slice(h * HD, (h + 1) * HD)
            q, k, v = (
                (acc[rows, j * cols + h * HD : j * cols + (h + 1) * HD] * scale).astype(BF16)
                for j in range(3)
            )
            scores = (
                lax.dot_general(
                    q,
                    keys_ref[s, :, at],
                    (((1,), (1,)), ((), ())),
                    preferred_element_type=F32,
                )
                * scaling
            )
            own = jnp.sum(q.astype(F32) * k.astype(F32), axis=1, keepdims=True) * scaling
            highest = jnp.maximum(jnp.max(scores, axis=1, keepdims=True), own)
            expd = jnp.exp(scores - highest)
            own_exp = jnp.exp(own - highest)
            total = jnp.sum(expd, axis=1, keepdims=True) + own_exp
            weights = (expd / total).astype(BF16)
            own_weight = (own_exp / total).astype(BF16)
            mixed = dot(weights, values_ref[s, :, at])
            mixed = mixed + own_weight.astype(F32) * v.astype(F32)
            out[rows, at] = mixed.astype(BF16)


def update_near(scenes, p_ref, tokens_ref, *refs):
    x_refs, w_ref, out = refs[:-2], refs[-2], refs[-1]
    for step in range(len(x_refs) // scenes):

        @pl.when(pl.program_id(0) == step)
        def _():
            x = jnp.concatenate(
                [ref[...] for ref in x_refs[step * scenes : (step + 1) * scenes]], axis=0
            )
            out[...] = (tokens_ref if step == 0 else out)[...] + dot(x, w_ref[...])


def update(count, p_ref, acc_ref, gain_ref, policy_ref, value_ref, *refs):
    x_refs, w_ref = refs[:count], refs[count]
    latent_out, keep_out, give_out, squares_out, turned_out, acc = refs[-6:]

    @pl.when(pl.program_id(0) == 0)
    def _():
        acc[...] = acc_ref[...]

    def add(j, product):
        acc[...] += product

    add_products(x_refs, [w_ref], add)

    @pl.when(pl.program_id(0) == count - 1)
    def _():
        state = acc[...]
        latent_out[...] = state.astype(BF16)
        squares = jnp.sum(state * state, axis=1, keepdims=True)
        squares_out[...] = row_of(squares)
        gained = (state * gain_ref[...]).astype(BF16)
        turned_out[...] = jnp.transpose(gained)
        policy = dot(gained, policy_ref[...])
        value = dot(gained, value_ref[...])

        @pl.when(p_ref[0] % 2 == 0)
        def _():
            keep_out[...] = policy
            give_out[...] = value.astype(BF16)

        @pl.when(p_ref[0] % 2 == 1)
        def _():
            keep_out[...] = value
            give_out[...] = policy.astype(BF16)


def heads(full_width, total_rows, p_ref, mine_ref, theirs_ref, squares_ref, policy_out_ref,
          value_out_ref, targets_ref, returns_ref, payload_out, give_out, hidden_ref):
    inverse = column(lax.rsqrt(squares_ref[:1] / full_width + EPSILON))
    pre = (mine_ref[...].astype(F32) + theirs_ref[...].astype(F32)) * inverse
    sigma = jax.nn.sigmoid(pre)
    hidden = (pre * sigma).astype(BF16)
    hidden_ref[...] = hidden
    slope = sigma * (1.0 + pre * (1.0 - sigma)) * inverse
    factor = total_rows ** (-0.5)
    count = hidden.shape[0]
    quarter = give_out.shape[0]
    part = 4 * quarter
    at = slice(count, count + quarter)

    def put_sums(grad, loss):
        shape = (payload_out.shape[0] - count - quarter, hidden.shape[1])
        rows = lax.broadcasted_iota(jnp.int32, shape, 0)
        lanes = lax.broadcasted_iota(jnp.int32, shape, 1)
        sums = jnp.where(rows == 0, grad, 0.0)
        for lane in range(3):
            term = loss.astype(BF16).astype(F32)
            sums = jnp.where((rows == 1) & (lanes == lane), term, sums)
            loss = loss - term
        payload_out[count + quarter :] = sums.astype(BF16)

    @pl.when(p_ref[0] % 2 == 0)
    def _():
        weight = policy_out_ref[...]
        logits = dot(hidden, weight)
        top = jnp.max(logits, axis=1, keepdims=True)
        log_total = top + jnp.log(jnp.sum(jnp.exp(logits - top), axis=1, keepdims=True))
        actions = lax.broadcasted_iota(jnp.int32, logits.shape, 1).astype(F32)
        onehot = (actions == column(targets_ref[...].astype(F32))).astype(F32)
        picked = jnp.sum(logits * onehot, axis=1, keepdims=True)
        loss = jnp.sum(log_total - picked, axis=0, keepdims=True)
        dlogits = ((jnp.exp(logits - log_total) - onehot) * factor).astype(BF16)
        back = lax.dot_general(
            dlogits, weight, (((1,), (1,)), ((), ())), preferred_element_type=F32
        )
        payload_out[:count] = (back * slope).astype(BF16)
        start = pl.multiple_of((p_ref[0] // 2) * part, part)
        grad = lax.dot_general(
            hidden_ref[:, pl.ds(start, part)],
            dlogits,
            (((0,), (0,)), ((), ())),
            preferred_element_type=F32,
        ).astype(BF16)
        parts = [grad[k * quarter : (k + 1) * quarter] for k in range(4)]
        payload_out[at] = jnp.concatenate(parts[:2], axis=1)
        give_out[...] = jnp.concatenate(parts[2:], axis=1)
        put_sums(jnp.zeros((1, hidden.shape[1]), F32), loss)

    @pl.when(p_ref[0] % 2 == 1)
    def _():
        weight = value_out_ref[...].astype(F32)
        hidden_f = hidden.astype(F32)
        value = jnp.sum(hidden_f * weight, axis=1, keepdims=True)
        errors = value - column(returns_ref[...])
        loss = 0.5 * jnp.sum(errors * errors, axis=0, keepdims=True)
        dvalue = (errors * factor).astype(BF16).astype(F32)
        payload_out[:count] = (dvalue * weight * slope).astype(BF16)
        payload_out[at] = jnp.zeros_like(give_out)
        give_out[...] = jnp.zeros_like(give_out)
        put_sums(jnp.sum(dvalue * hidden_f, axis=0, keepdims=True), loss)


def sums(total_rows, p_ref, *refs):
    count = (len(refs) - 3) // 4
    share_out, losses_out, grad_out = refs[-3:]

    def total(d_refs):
        *shards, ahead, back = [ref[...].astype(F32) for ref in d_refs]
        return sum(shards, jnp.concatenate([ahead, back], axis=1))

    own, other, own_sums, other_sums = (
        total(refs[k * count : (k + 1) * count]) for k in range(4)
    )
    first = p_ref[0] % 2 == 0
    quarter = own.shape[0]
    width = share_out.shape[1]
    for k, part in enumerate((jnp.where(first, own, other), jnp.where(first, other, own))):
        for j in range(2):
            at = (2 * k + j) * quarter
            share_out[at : at + quarter] = part[:, j * width : (j + 1) * width].astype(BF16)
    policy = jnp.where(first, own_sums, other_sums)
    value = jnp.where(first, other_sums, own_sums)
    grad_out[...] = value[:1].astype(BF16)

    def loss(part):
        lanes = lax.broadcasted_iota(jnp.int32, (1, part.shape[1]), 1)
        return jnp.sum(jnp.where(lanes < 3, part[1:2], 0.0), axis=1, keepdims=True) / total_rows

    lanes = lax.broadcasted_iota(jnp.int32, (1, 2), 1)
    losses_out[...] = jnp.where(lanes == 0, loss(policy), loss(value))


def join(ds, p_ref, *refs):
    out = refs[-1]
    size = refs[0].shape[0]
    for d, ref in zip(ds, refs[:-1]):
        out[pl.ds(pl.multiple_of(((p_ref[0] ^ d) // 2) * size, size), size)] = ref[...]


def factors(turned_refs, own_refs, other_refs, halved):
    turned = jnp.concatenate([ref[...] for ref in turned_refs], axis=1)
    for d_refs in (own_refs, other_refs):
        shards = [ref[...] for ref in d_refs]
        if halved:
            shards[-2:] = [jnp.concatenate(shards[-2:], axis=1)]
        yield dot(turned, jnp.concatenate(shards, axis=0))


def gradients_start(turned_count, count, p_ref, *refs):
    turned, own, other = refs[:turned_count], refs[turned_count:][:count], refs[turned_count + count : -2]
    for out, product in zip(refs[-2:], factors(turned, own, other, False)):
        out[...] = product


def gradients_end(turned_count, count, p_ref, *refs):
    sums, refs, outs = refs[:2], refs[2:-2], refs[-2:]
    turned, own, other = refs[:turned_count], refs[turned_count:][:count], refs[turned_count + count :]
    own, other = (
        (acc[...] + product).astype(BF16)
        for acc, product in zip(sums, factors(turned, own, other, True))
    )

    @pl.when(p_ref[0] % 2 == 0)
    def _():
        outs[0][...] = own
        outs[1][...] = other

    @pl.when(p_ref[0] % 2 == 1)
    def _():
        outs[1][...] = own
        outs[0][...] = other


def call(body, name, place, steps, operands, in_specs, outs, out_specs, flops, limit, scratch=(), aliases=None):
    bytes_accessed = sum(x.size * x.dtype.itemsize for x in (*operands, *outs)) if flops else 0
    return pl.pallas_call(
        body,
        name=name,
        out_shape=outs,
        input_output_aliases=aliases or {},
        grid_spec=pltpu.PrefetchScalarGridSpec(
            num_scalar_prefetch=1,
            grid=(steps,),
            in_specs=in_specs,
            out_specs=out_specs,
            scratch_shapes=scratch,
        ),
        compiler_params=pltpu.CompilerParams(
            dimension_semantics=("arbitrary",), vmem_limit_bytes=limit
        ),
        cost_estimate=pl.CostEstimate(
            flops=flops, bytes_accessed=bytes_accessed, transcendentals=0
        ),
    )(place, *operands)


def per_device(
    latent,
    actions,
    action_table,
    norm1_gain,
    w_query,
    w_key,
    w_value,
    w_out,
    key_cache,
    value_cache,
    norm2_gain,
    policy_in,
    value_in,
    policy_out,
    value_out,
    targets,
    returns,
):
    rows, width = latent.shape
    narrow_size = lax.axis_size("narrow")
    wide_size = lax.axis_size("wide")
    full_width = width * narrow_size
    cols = w_query.shape[1]
    total_rows = rows * wide_size
    action_count = action_table.shape[0]
    hidden_count = policy_in.shape[1]
    index = lax.axis_index("narrow").astype(jnp.int32)
    place = index[None]
    first = index % 2 == 0
    chips = narrow_size // 2
    near = [0, 1]
    direct = list(range(2, narrow_size, 2))
    passed = [d + 1 for d in direct]

    far = direct + passed
    scenes = key_cache.shape[0]
    branch = rows // scenes
    hbm = functools.partial(pltpu.with_memory_space_constraint, memory_space=pltpu.HBM)

    block_shape = (branch + 16, width)
    state_spec = whole((branch, width))
    tokens, *blocks = call(
        functools.partial(embed, scenes), "embed", place, 1,
        [
            hbm(latent), hbm(actions[None, :]), hbm(action_table),
            hbm(norm1_gain[None, :]),
        ],
        [
            whole((rows, width)), whole((1, rows)), whole(action_table.shape),
            whole((1, width)),
        ],
        [
            jax.ShapeDtypeStruct((rows, width), F32),
            *[jax.ShapeDtypeStruct(block_shape, BF16)] * scenes,
        ],
        [whole((rows, width)), *[whole(block_shape)] * scenes],
        2 * rows * width * action_count, 16 * MIB,
    )
    blocks = [{**far_blocks(block), 1: swap(block, 1)} for block in blocks]

    weights = [hbm(w) for w in (w_query, w_key, w_value)]
    x_spec = whole((branch, width))
    acc_shape = jax.ShapeDtypeStruct((rows, 3 * cols), F32)
    weight_shape = jax.ShapeDtypeStruct((width, cols), BF16)
    weight_block = whole((width, cols))
    cache_shape = jax.ShapeDtypeStruct(key_cache.shape, BF16)
    outs = [weight_shape] * (3 * len(far)) + [cache_shape] * 2
    anywhere = pl.BlockSpec(memory_space=pl.ANY)
    flops = 2 * branch * width * 3 * cols
    acc, *staged, keys, values = call(
        functools.partial(begin, near, far, scenes), "begin", place, 1,
        [
            *(blocks[s][d] for d in near for s in range(scenes)), *weights,
            hbm(key_cache), hbm(value_cache),
        ],
        [*[x_spec] * (scenes * len(near)), *[anywhere] * 5],
        [acc_shape, *outs], [whole(acc_shape.shape), *[anywhere] * len(outs)],
        flops * scenes * len(near), 20 * MIB,
        [
            pltpu.VMEM((3 * len(near), width, cols), BF16),
            pltpu.SemaphoreType.DMA((3 * len(near) + len(outs),)),
        ],
    )
    staged_direct = staged[: 3 * len(direct)]
    staged_passed = staged[3 * len(direct) :]

    part_spec = whole((branch, 3 * cols))
    squares_spec = pl.BlockSpec((16, branch), lambda i, p: (branch // 16, 0))
    attended = []
    for s in range(scenes):
        blocks[s] = pass_blocks(blocks[s], acc, *(one[0] for one in attended))
        part = call(
            functools.partial(project_more, len(direct)), f"project{s}", place, 1,
            [acc, *(blocks[s][d] for d in direct), *staged_direct],
            [
                pl.BlockSpec(
                    (branch, 3 * cols), functools.partial(lambda s, i, p: (s, 0), s)
                ),
                *[x_spec] * len(direct), *[weight_block] * len(staged_direct),
            ],
            [jax.ShapeDtypeStruct((branch, 3 * cols), F32)], [part_spec],
            0, 20 * MIB,
        )[0]
        cache_spec = pl.BlockSpec(
            (1, *key_cache.shape[1:]), functools.partial(lambda s, i, p: (s, 0, 0), s)
        )
        one = call(
            functools.partial(attend, len(passed), narrow_size, full_width), f"attend{s}", place, 1,
            [
                part, keys, values, *blocks[s].values(),
                *(blocks[s][d] for d in passed), *staged_passed,
            ],
            [
                part_spec, cache_spec, cache_spec, *[squares_spec] * narrow_size,
                *[x_spec] * len(passed), *[weight_block] * len(staged_passed),
            ],
            [jax.ShapeDtypeStruct((branch, cols), BF16)], [whole((branch, cols))],
            0, 20 * MIB, [pltpu.VMEM((branch, 3 * cols), F32)],
        )[0]
        attended.append({**far_blocks(one), 1: swap(one, 1)})

    half = (rows, hidden_count)
    full_shapes = [
        jax.ShapeDtypeStruct((rows, width), BF16),
        jax.ShapeDtypeStruct(half, F32),
        jax.ShapeDtypeStruct(half, BF16),
        jax.ShapeDtypeStruct((8, rows), F32),
    ]
    chunk = whole((branch, cols))
    acc = call(
        functools.partial(update_near, scenes), "update_near", place, len(near),
        [tokens, *(one[d] for d in near for one in attended), w_out],
        [
            whole((rows, width)), *[chunk] * (scenes * len(near)),
            weight_spec(near, cols, width),
        ],
        [jax.ShapeDtypeStruct((rows, width), F32)], [whole((rows, width))],
        2 * rows * width * cols * len(near), 16 * MIB,
    )[0]
    filled, turned, shards = [], [], []
    ring = Ring()
    for s in range(scenes):
        ds = far
        around = pass_blocks(attended[s], *turned)
        at = functools.partial(lambda s, i, p: (s, 0), s)
        operands = [
            acc, norm2_gain[None, :], policy_in, value_in,
            *(around[d] for d in ds), w_out, *filled,
        ]
        *filled, one = call(
            functools.partial(update, len(ds)), f"update{s}", place, len(ds), operands,
            [
                pl.BlockSpec((branch, width), at),
                whole((1, width)), whole(policy_in.shape), whole(value_in.shape),
                *[chunk] * len(ds), weight_spec(ds, cols, width),
                *[anywhere] * len(filled),
            ],
            [*full_shapes, jax.ShapeDtypeStruct((width, branch), BF16)],
            [
                pl.BlockSpec((branch, width), at),
                pl.BlockSpec((branch, hidden_count), at),
                pl.BlockSpec((branch, hidden_count), at),
                pl.BlockSpec((8, branch), functools.partial(lambda s, i, p: (0, s), s)),
                whole((width, branch)),
            ],
            2 * branch * width * (cols * len(ds) + 2 * hidden_count), 28 * MIB,
            [pltpu.VMEM((branch, width), F32)],
            {1 + len(operands) - len(filled) + k: k for k in range(len(filled))},
        )
        turned.append(one)
        if s == 0:
            shards.append([ring.step(one, one)])
    new_latent, keep, give, squares = filled

    for bit in (1, *far_bits()):
        squares = squares + swap(squares, bit)
    pre = keep + swap(give, 1).astype(F32)
    mine = pre.astype(BF16)
    *upper, last = far_bits()
    for bit in upper:
        mine = (mine.astype(F32) + swap(mine, bit).astype(F32)).astype(BF16)
    rounds = wide_size // 2
    shards[0].append(ring.step(*shards[0][-1]))
    for one in turned[1:]:
        shards.append([ring.step(one, one)])
    while len(shards[0]) < min(EARLY, rounds - 1):
        shards[0].append(ring.step(*shards[0][-1]))
    theirs = after(swap(mine, last), *shards[0][-1], *(b for one in shards[1:] for b in one[0]))
    quarter = hidden_count // chips // 4
    payload_shape = (rows + quarter + 16, hidden_count)
    payload, give = call(
        functools.partial(heads, full_width, total_rows), "heads", place, 1,
        [
            mine, theirs, squares, policy_out, value_out[None, :], targets[None, :],
            returns[None, :],
        ],
        [
            whole(half), whole(half), whole((8, rows)), whole(policy_out.shape),
            whole((1, hidden_count)), whole((1, rows)), whole((1, rows)),
        ],
        [
            jax.ShapeDtypeStruct(payload_shape, BF16),
            jax.ShapeDtypeStruct((quarter, hidden_count), BF16),
        ],
        [whole(payload_shape), whole((quarter, hidden_count))],
        6 * rows * hidden_count * action_count, 16 * MIB, [pltpu.VMEM(half, BF16)],
    )
    taken = jnp.where(first, payload[rows : rows + quarter], swap(give, 1))
    payload = lax.dynamic_update_slice(payload, taken, (rows, 0))

    payload_rounds = [[payload, payload]]
    for shard in shards:
        while len(shard) < rounds - 1:
            if len(payload_rounds) < rounds:
                payload_rounds.append(ring.step(*payload_rounds[-1]))
            shard.append(ring.step(*shard[-1]))
    while len(payload_rounds) < rounds:
        payload_rounds.append(ring.step(*payload_rounds[-1]))
    cut = scenes // 2
    for one, other in zip(shards[:cut], shards[cut:]):
        up, down = ring.step(one[-1][0], other[-1][1])
        one.append([up])
        other.append([down])
    size = hidden_count // 2
    up, down = payload_rounds[-1]
    payload_rounds.append(ring.step(up[:, :size], down[:, size:]))
    turned_all = list(turned)
    for step in range(rounds):
        for way in range(len(shards[0][step])):
            turned_all += [shard[step][way] for shard in shards]
    payload_own = [payload, *(b for pair in payload_rounds[1:] for b in pair)]
    payload_other = [swap(b, 1) for b in payload_own]

    pieces = [*payload_own, *payload_other]
    share_shape = (4 * quarter, action_count)
    share, losses, value_out_grad = call(
        functools.partial(sums, total_rows), "sums", place, 1, [*pieces, *pieces],
        [
            pl.BlockSpec((count, b.shape[1]), functools.partial(lambda at, i, p: (at, 0), start // count))
            for start, count in ((rows, quarter), (rows + quarter, 16))
            for b in pieces
        ],
        [
            jax.ShapeDtypeStruct(share_shape, BF16),
            jax.ShapeDtypeStruct((1, 2), F32),
            jax.ShapeDtypeStruct((1, hidden_count), BF16),
        ],
        [whole(share_shape), whole((1, 2)), whole((1, hidden_count))], 0, 8 * MIB,
    )
    losses = losses.reshape(2)
    value_out_grad = value_out_grad.reshape(hidden_count)
    shares = far_blocks(share)
    policy_out_grad = call(
        functools.partial(join, list(shares)), "join", place, 1, list(shares.values()),
        [whole(share_shape)] * len(shares),
        [jax.ShapeDtypeStruct((hidden_count, action_count), BF16)],
        [whole((hidden_count, action_count))], 0, 8 * MIB,
    )[0]

    block = 256
    grad_spec = pl.BlockSpec((block, hidden_count), lambda i, p: (i, 0))
    grad_flops = 4 * rows * width * hidden_count
    split = wide_size - 3

    def gradient(body, name, operands, specs, count, turned, own, other, dtype):
        return call(
            functools.partial(body, len(turned), len(own)), name, place, width // block,
            [*operands, *turned, *own, *other],
            [
                *specs,
                *[pl.BlockSpec((block, branch), lambda i, p: (i, 0))] * len(turned),
                *[
                    pl.BlockSpec(
                        (rows, b.shape[1]), lambda i, p: (0, 0), pipeline_mode=pl.Buffered(1)
                    )
                    for b in (*own, *other)
                ],
            ],
            [jax.ShapeDtypeStruct((width, hidden_count), dtype)] * 2, [grad_spec] * 2,
            grad_flops * count, 24 * MIB,
        )

    starts = gradient(
        gradients_start, "gradients_start", [], [], split, turned_all[: scenes * split],
        payload_own[:split], payload_other[:split], F32,
    )
    policy_in_grad, value_in_grad = gradient(
        gradients_end, "gradients_end", starts, [grad_spec] * 2, wide_size - split,
        turned_all[scenes * split :], payload_own[split:], payload_other[split:], BF16,
    )
    return (new_latent, losses, policy_in_grad, value_in_grad, policy_out_grad, value_out_grad)


def solution(mesh):
    placed = (
        P("wide", "narrow"),
        P("wide"),
        P(None, "narrow"),
        P("narrow"),
        P(None, "narrow"),
        P(None, "narrow"),
        P(None, "narrow"),
        P(None, "narrow"),
        P("wide", None, "narrow"),
        P("wide", None, "narrow"),
        P("narrow"),
        P("narrow", None),
        P("narrow", None),
        P(),
        P(),
        P("wide"),
        P("wide"),
    )
    return jax.shard_map(
        per_device,
        mesh=mesh,
        in_specs=placed,
        out_specs=(P("wide", "narrow"), P(), P("narrow", None), P("narrow", None), P(), P()),
        check_vma=False,
    )
```

```python
import functools

import jax
import jax.numpy as jnp
from jax import lax
from jax.experimental import pallas as pl
from jax.experimental.pallas import tpu as pltpu
from jax.sharding import PartitionSpec as P

HD = 128
EPSILON = 1e-05
F32 = jnp.float32
BF16 = jnp.bfloat16
MIB = 1 << 20


def swap(block, bit):
    size = lax.axis_size("narrow")
    return lax.ppermute(block, "narrow", [(n, n ^ bit) for n in range(size)])


def far_bits():
    bit = lax.axis_size("narrow") // 2
    while bit > 1:
        yield bit
        bit //= 2


def far_blocks(block):
    blocks = {0: block}
    for bit in far_bits():
        blocks.update({d ^ bit: swap(b, bit) for d, b in list(blocks.items())})
    return blocks


def pass_blocks(blocks, *earlier):
    far = {d ^ 1: swap(after(b, *earlier), 1) for d, b in blocks.items() if d > 1}
    return {**blocks, **far}


def after(block, *earlier):
    return lax.optimization_barrier((block, *earlier))[0]


def ring_order(size):
    return list(range(0, size, 2)) + list(range(size - 1, 0, -2))


def ring_step(block, way):
    order = ring_order(lax.axis_size("wide"))
    pairs = [(a, order[(i + way) % len(order)]) for i, a in enumerate(order)]
    return lax.ppermute(block, "wide", pairs)


class Ring:
    def __init__(self):
        self.arrived = []

    def step(self, *pair):
        held = self.arrived[-2] if len(self.arrived) > 1 else ((), ())
        up, down = (after(b, *h) for b, h in zip(pair, held))
        self.arrived.append(((ring_step(up, 1),), (ring_step(down, -1),)))
        return [self.arrived[-1][0][0], self.arrived[-1][1][0]]


def dot(a, b):
    return jnp.dot(a, b, preferred_element_type=F32)


def column(row):
    return jnp.transpose(jnp.broadcast_to(row, (128, row.shape[1])))[:, :1]


def whole(shape):
    return pl.BlockSpec(shape, lambda i, p: (0,) * len(shape))


def weight_spec(ds, rows, columns):
    def at(i, p):
        d = jnp.int32(ds[0])
        for j in range(1, len(ds)):
            d = jnp.where(i == j, ds[j], d)
        return (p[0] ^ d, 0)

    return pl.BlockSpec((rows, columns), at)


def add_products(x_refs, w_refs, add):
    for step, x_ref in enumerate(x_refs):

        @pl.when(pl.program_id(0) == step)
        def _():
            for j, w_ref in enumerate(w_refs):
                add(j, dot(x_ref[...], w_ref[...]))


def row_of(values):
    return jnp.transpose(jnp.broadcast_to(values, (values.shape[0], 128)))[:8]


def embed(p_ref, latent_ref, actions_ref, table_ref, gain_ref, tokens_out, block_out):
    shape = (table_ref.shape[0], latent_ref.shape[0])
    onehot = (lax.broadcasted_iota(jnp.int32, shape, 0) == actions_ref[...]).astype(BF16)
    picked = lax.dot_general(
        onehot, table_ref[...], (((0,), (0,)), ((), ())), preferred_element_type=F32
    )
    tokens = latent_ref[...].astype(F32) + picked
    tokens_out[...] = tokens
    count = latent_ref.shape[0]
    block_out[:count] = (tokens * gain_ref[...]).astype(BF16)
    block_out[count:] = jnp.zeros_like(block_out[count:])
    rest = row_of(jnp.sum(tokens * tokens, axis=1, keepdims=True))[:1]
    rows = lax.broadcasted_iota(jnp.int32, (16, count), 0)
    terms = jnp.zeros((16, count), F32)
    for k in range(3):
        term = rest.astype(BF16).astype(F32)
        terms = jnp.where(rows == k, term, terms)
        rest = rest - term
    block_out[count:, :count] = terms.astype(BF16)


def begin(near, far, p_ref, *refs):
    count = len(near)
    x_refs, weights, caches = refs[:count], refs[count : count + 3], refs[count + 3 : count + 5]
    acc, *outs, held, sems = refs[count + 5 :]
    size, cols = held.shape[1:]
    copies = []

    def send(src, dst):
        copies.append(pltpu.make_async_copy(src, dst, sems.at[len(copies)]))
        copies[-1].start()

    for i, d in enumerate(near + far):
        start = pl.multiple_of((p_ref[0] ^ d) * size, size)
        for j, w_ref in enumerate(weights):
            k = i * 3 + j
            send(
                w_ref.at[pl.ds(start, size)],
                held.at[k] if i < len(near) else outs[k - 3 * len(near)],
            )
    for src, dst in zip(caches, outs[-2:]):
        send(src, dst)
    for i in range(len(near)):
        for j in range(3):
            copies[i * 3 + j].wait()
            product = dot(x_refs[i][...], held[i * 3 + j])
            at = slice(j * cols, (j + 1) * cols)
            acc[:, at] = product if i == 0 else acc[:, at] + product
    for copy in copies[3 * len(near) :]:
        copy.wait()


def project_more(count, p_ref, acc_ref, *refs):
    x_refs, w_refs, out = refs[:count], refs[count:-1], refs[-1]
    cols = w_refs[0].shape[1]
    for j in range(3):
        at = slice(j * cols, (j + 1) * cols)
        total = acc_ref[:, at]
        for i, x_ref in enumerate(x_refs):
            total = total + dot(x_ref[...], w_refs[i * 3 + j][...])
        out[:, at] = total


def attend(count, sources, full_width, p_ref, acc_ref, keys_ref, values_ref, *refs):
    squares_refs, refs = refs[:sources], refs[sources:]
    project_more(count, p_ref, acc_ref, *refs[:-2], refs[-1])
    out, acc = refs[-2:]
    cols = refs[count].shape[1]
    squares = sum(jnp.sum(ref[:8].astype(F32), axis=0, keepdims=True) for ref in squares_refs)
    attend_heads(full_width, cols, squares, keys_ref, values_ref, out, acc)


def attend_heads(full_width, cols, squares, keys_ref, values_ref, out, acc):
    scenes = keys_ref.shape[0]
    branch = acc.shape[0] // scenes
    inverse = column(lax.rsqrt(squares / full_width + EPSILON))
    scaling = HD ** (-0.5)
    for s in range(scenes):
        rows = slice(s * branch, (s + 1) * branch)
        scale = inverse[rows]
        for h in range(cols // HD):
            at = slice(h * HD, (h + 1) * HD)
            q, k, v = (
                (acc[rows, j * cols + h * HD : j * cols + (h + 1) * HD] * scale).astype(BF16)
                for j in range(3)
            )
            scores = (
                lax.dot_general(
                    q,
                    keys_ref[s, :, at],
                    (((1,), (1,)), ((), ())),
                    preferred_element_type=F32,
                )
                * scaling
            )
            own = jnp.sum(q.astype(F32) * k.astype(F32), axis=1, keepdims=True) * scaling
            highest = jnp.maximum(jnp.max(scores, axis=1, keepdims=True), own)
            expd = jnp.exp(scores - highest)
            own_exp = jnp.exp(own - highest)
            total = jnp.sum(expd, axis=1, keepdims=True) + own_exp
            weights = (expd / total).astype(BF16)
            own_weight = (own_exp / total).astype(BF16)
            mixed = dot(weights, values_ref[s, :, at])
            mixed = mixed + own_weight.astype(F32) * v.astype(F32)
            out[rows, at] = mixed.astype(BF16)


def update_near(scenes, p_ref, tokens_ref, *refs):
    x_refs, w_ref, out = refs[:-2], refs[-2], refs[-1]
    for step in range(len(x_refs) // scenes):

        @pl.when(pl.program_id(0) == step)
        def _():
            x = jnp.concatenate(
                [ref[...] for ref in x_refs[step * scenes : (step + 1) * scenes]], axis=0
            )
            out[...] = (tokens_ref if step == 0 else out)[...] + dot(x, w_ref[...])


def update(count, p_ref, acc_ref, gain_ref, policy_ref, value_ref, *refs):
    x_refs, w_ref = refs[:count], refs[count]
    latent_out, keep_out, give_out, squares_out, turned_out, acc = refs[-6:]

    @pl.when(pl.program_id(0) == 0)
    def _():
        acc[...] = acc_ref[...]

    def add(j, product):
        acc[...] += product

    add_products(x_refs, [w_ref], add)

    @pl.when(pl.program_id(0) == count - 1)
    def _():
        state = acc[...]
        latent_out[...] = state.astype(BF16)
        squares = jnp.sum(state * state, axis=1, keepdims=True)
        squares_out[...] = row_of(squares)
        gained = (state * gain_ref[...]).astype(BF16)
        turned_out[...] = jnp.transpose(gained)
        policy = dot(gained, policy_ref[...])
        value = dot(gained, value_ref[...])

        @pl.when(p_ref[0] % 2 == 0)
        def _():
            keep_out[...] = policy
            give_out[...] = value.astype(BF16)

        @pl.when(p_ref[0] % 2 == 1)
        def _():
            keep_out[...] = value
            give_out[...] = policy.astype(BF16)


def heads(full_width, total_rows, p_ref, mine_ref, theirs_ref, squares_ref, policy_out_ref,
          value_out_ref, targets_ref, returns_ref, payload_out, give_out, hidden_ref):
    inverse = column(lax.rsqrt(squares_ref[:1] / full_width + EPSILON))
    pre = (mine_ref[...].astype(F32) + theirs_ref[...].astype(F32)) * inverse
    sigma = jax.nn.sigmoid(pre)
    hidden = (pre * sigma).astype(BF16)
    hidden_ref[...] = hidden
    slope = sigma * (1.0 + pre * (1.0 - sigma)) * inverse
    factor = total_rows ** (-0.5)
    count = hidden.shape[0]
    quarter = give_out.shape[0]
    part = 4 * quarter
    at = slice(count, count + quarter)

    def put_sums(grad, loss):
        shape = (payload_out.shape[0] - count - quarter, hidden.shape[1])
        rows = lax.broadcasted_iota(jnp.int32, shape, 0)
        lanes = lax.broadcasted_iota(jnp.int32, shape, 1)
        sums = jnp.where(rows == 0, grad, 0.0)
        for lane in range(3):
            term = loss.astype(BF16).astype(F32)
            sums = jnp.where((rows == 1) & (lanes == lane), term, sums)
            loss = loss - term
        payload_out[count + quarter :] = sums.astype(BF16)

    @pl.when(p_ref[0] % 2 == 0)
    def _():
        weight = policy_out_ref[...]
        logits = dot(hidden, weight)
        top = jnp.max(logits, axis=1, keepdims=True)
        log_total = top + jnp.log(jnp.sum(jnp.exp(logits - top), axis=1, keepdims=True))
        actions = lax.broadcasted_iota(jnp.int32, logits.shape, 1).astype(F32)
        onehot = (actions == column(targets_ref[...].astype(F32))).astype(F32)
        picked = jnp.sum(logits * onehot, axis=1, keepdims=True)
        loss = jnp.sum(log_total - picked, axis=0, keepdims=True)
        dlogits = ((jnp.exp(logits - log_total) - onehot) * factor).astype(BF16)
        back = lax.dot_general(
            dlogits, weight, (((1,), (1,)), ((), ())), preferred_element_type=F32
        )
        payload_out[:count] = (back * slope).astype(BF16)
        start = pl.multiple_of((p_ref[0] // 2) * part, part)
        grad = lax.dot_general(
            hidden_ref[:, pl.ds(start, part)],
            dlogits,
            (((0,), (0,)), ((), ())),
            preferred_element_type=F32,
        ).astype(BF16)
        parts = [grad[k * quarter : (k + 1) * quarter] for k in range(4)]
        payload_out[at] = jnp.concatenate(parts[:2], axis=1)
        give_out[...] = jnp.concatenate(parts[2:], axis=1)
        put_sums(jnp.zeros((1, hidden.shape[1]), F32), loss)

    @pl.when(p_ref[0] % 2 == 1)
    def _():
        weight = value_out_ref[...].astype(F32)
        hidden_f = hidden.astype(F32)
        value = jnp.sum(hidden_f * weight, axis=1, keepdims=True)
        errors = value - column(returns_ref[...])
        loss = 0.5 * jnp.sum(errors * errors, axis=0, keepdims=True)
        dvalue = (errors * factor).astype(BF16).astype(F32)
        payload_out[:count] = (dvalue * weight * slope).astype(BF16)
        payload_out[at] = jnp.zeros_like(give_out)
        give_out[...] = jnp.zeros_like(give_out)
        put_sums(jnp.sum(dvalue * hidden_f, axis=0, keepdims=True), loss)


def sums(total_rows, p_ref, *refs):
    count = (len(refs) - 3) // 4
    share_out, losses_out, grad_out = refs[-3:]

    def total(d_refs):
        *shards, ahead, back = [ref[...].astype(F32) for ref in d_refs]
        return sum(shards, jnp.concatenate([ahead, back], axis=1))

    own, other, own_sums, other_sums = (
        total(refs[k * count : (k + 1) * count]) for k in range(4)
    )
    first = p_ref[0] % 2 == 0
    quarter = own.shape[0]
    width = share_out.shape[1]
    for k, part in enumerate((jnp.where(first, own, other), jnp.where(first, other, own))):
        for j in range(2):
            at = (2 * k + j) * quarter
            share_out[at : at + quarter] = part[:, j * width : (j + 1) * width].astype(BF16)
    policy = jnp.where(first, own_sums, other_sums)
    value = jnp.where(first, other_sums, own_sums)
    grad_out[...] = value[0].astype(BF16)

    def loss(part):
        lanes = lax.broadcasted_iota(jnp.int32, (1, part.shape[1]), 1)
        return jnp.sum(jnp.where(lanes < 3, part[1:2], 0.0), axis=1, keepdims=True) / total_rows

    lanes = lax.broadcasted_iota(jnp.int32, (1, 2), 1)
    losses_out[...] = jnp.where(lanes == 0, loss(policy), loss(value))


def join(ds, p_ref, *refs):
    out = refs[-1]
    size = refs[0].shape[0]
    for d, ref in zip(ds, refs[:-1]):
        out[pl.ds(pl.multiple_of(((p_ref[0] ^ d) // 2) * size, size), size)] = ref[...]


def factors(turned_refs, own_refs, other_refs, halved):
    turned = jnp.concatenate([ref[...] for ref in turned_refs], axis=1)
    for d_refs in (own_refs, other_refs):
        shards = [ref[...] for ref in d_refs]
        if halved:
            shards[-2:] = [jnp.concatenate(shards[-2:], axis=1)]
        yield dot(turned, jnp.concatenate(shards, axis=0))


def gradients_start(turned_count, count, p_ref, *refs):
    turned, own, other = refs[:turned_count], refs[turned_count:][:count], refs[turned_count + count : -2]
    for out, product in zip(refs[-2:], factors(turned, own, other, False)):
        out[...] = product


def gradients_end(turned_count, count, p_ref, *refs):
    sums, refs, outs = refs[:2], refs[2:-2], refs[-2:]
    turned, own, other = refs[:turned_count], refs[turned_count:][:count], refs[turned_count + count :]
    own, other = (
        (acc[...] + product).astype(BF16)
        for acc, product in zip(sums, factors(turned, own, other, True))
    )

    @pl.when(p_ref[0] % 2 == 0)
    def _():
        outs[0][...] = own
        outs[1][...] = other

    @pl.when(p_ref[0] % 2 == 1)
    def _():
        outs[1][...] = own
        outs[0][...] = other


def call(body, name, place, steps, operands, in_specs, outs, out_specs, flops, limit, scratch=(), aliases=None):
    bytes_accessed = sum(x.size * x.dtype.itemsize for x in (*operands, *outs)) if flops else 0
    return pl.pallas_call(
        body,
        name=name,
        out_shape=outs,
        input_output_aliases=aliases or {},
        grid_spec=pltpu.PrefetchScalarGridSpec(
            num_scalar_prefetch=1,
            grid=(steps,),
            in_specs=in_specs,
            out_specs=out_specs,
            scratch_shapes=scratch,
        ),
        compiler_params=pltpu.CompilerParams(
            dimension_semantics=("arbitrary",), vmem_limit_bytes=limit
        ),
        cost_estimate=pl.CostEstimate(
            flops=flops, bytes_accessed=bytes_accessed, transcendentals=0
        ),
    )(place, *operands)


def per_device(
    latent,
    actions,
    action_table,
    norm1_gain,
    w_query,
    w_key,
    w_value,
    w_out,
    key_cache,
    value_cache,
    norm2_gain,
    policy_in,
    value_in,
    policy_out,
    value_out,
    targets,
    returns,
):
    rows, width = latent.shape
    narrow_size = lax.axis_size("narrow")
    wide_size = lax.axis_size("wide")
    full_width = width * narrow_size
    cols = w_query.shape[1]
    total_rows = rows * wide_size
    action_count = action_table.shape[0]
    hidden_count = policy_in.shape[1]
    index = lax.axis_index("narrow").astype(jnp.int32)
    place = index[None]
    first = index % 2 == 0
    chips = narrow_size // 2
    near = [0, 1]
    direct = list(range(2, narrow_size, 2))
    passed = [d + 1 for d in direct]

    far = direct + passed
    scenes = key_cache.shape[0]
    branch = rows // scenes
    hbm = functools.partial(pltpu.with_memory_space_constraint, memory_space=pltpu.HBM)

    block_shape = (rows + 16, width)
    tokens, block = call(
        embed, "embed", place, 1,
        [
            hbm(latent), hbm(actions[None, :]), hbm(action_table),
            hbm(norm1_gain[None, :]),
        ],
        [
            whole((rows, width)), whole((1, rows)), whole(action_table.shape),
            whole((1, width)),
        ],
        [
            jax.ShapeDtypeStruct((rows, width), F32),
            jax.ShapeDtypeStruct(block_shape, BF16),
        ],
        [whole((rows, width)), whole(block_shape)],
        2 * rows * width * action_count, 16 * MIB,
    )
    blocks = {**far_blocks(block), 1: swap(block, 1)}

    weights = [hbm(w) for w in (w_query, w_key, w_value)]
    x_spec = whole((rows, width))
    acc_shape = jax.ShapeDtypeStruct((rows, 3 * cols), F32)
    weight_shape = jax.ShapeDtypeStruct((width, cols), BF16)
    weight_block = whole((width, cols))
    cache_shape = jax.ShapeDtypeStruct(key_cache.shape, BF16)
    outs = [weight_shape] * (3 * len(far)) + [cache_shape] * 2
    anywhere = pl.BlockSpec(memory_space=pl.ANY)
    flops = 2 * rows * width * 3 * cols
    acc, *staged, keys, values = call(
        functools.partial(begin, near, far), "begin", place, 1,
        [
            *(blocks[d] for d in near), *weights,
            hbm(key_cache), hbm(value_cache),
        ],
        [*[x_spec] * len(near), *[anywhere] * 5],
        [acc_shape, *outs], [whole(acc_shape.shape), *[anywhere] * len(outs)],
        flops * len(near), 20 * MIB,
        [
            pltpu.VMEM((3 * len(near), width, cols), BF16),
            pltpu.SemaphoreType.DMA((3 * len(near) + len(outs),)),
        ],
    )
    staged_direct = staged[: 3 * len(direct)]
    staged_passed = staged[3 * len(direct) :]

    acc_spec = whole(acc_shape.shape)
    blocks = pass_blocks(blocks, acc)
    acc = call(
        functools.partial(project_more, len(direct)), "project", place, 1,
        [acc, *(blocks[d] for d in direct), *staged_direct],
        [acc_spec, *[x_spec] * len(direct), *[weight_block] * len(staged_direct)],
        [acc_shape], [acc_spec], flops * len(direct), 24 * MIB,
    )[0]

    attended = []
    for s in range(scenes):
        at = functools.partial(lambda s, i, p: (s, 0), s)
        squares_spec = pl.BlockSpec(
            (16, branch), functools.partial(lambda s, i, p: (rows // 16, s), s)
        )
        cache_spec = pl.BlockSpec(
            (1, *key_cache.shape[1:]), functools.partial(lambda s, i, p: (s, 0, 0), s)
        )
        one = call(
            functools.partial(attend, len(passed), narrow_size, full_width), f"attend{s}", place, 1,
            [
                acc, keys, values, *blocks.values(),
                *(blocks[d] for d in passed), *staged_passed,
            ],
            [
                pl.BlockSpec((branch, 3 * cols), at), cache_spec, cache_spec,
                *[squares_spec] * narrow_size,
                *[pl.BlockSpec((branch, width), at)] * len(passed), *[weight_block] * len(staged_passed),
            ],
            [jax.ShapeDtypeStruct((branch, cols), BF16)], [whole((branch, cols))],
            0, 20 * MIB, [pltpu.VMEM((branch, 3 * cols), F32)],
        )[0]
        attended.append({**far_blocks(one), 1: swap(one, 1)})

    half = (rows, hidden_count)
    full_shapes = [
        jax.ShapeDtypeStruct((rows, width), BF16),
        jax.ShapeDtypeStruct(half, F32),
        jax.ShapeDtypeStruct(half, BF16),
        jax.ShapeDtypeStruct((8, rows), F32),
    ]
    chunk = whole((branch, cols))
    acc = call(
        functools.partial(update_near, scenes), "update_near", place, len(near),
        [tokens, *(one[d] for d in near for one in attended), w_out],
        [
            whole((rows, width)), *[chunk] * (scenes * len(near)),
            weight_spec(near, cols, width),
        ],
        [jax.ShapeDtypeStruct((rows, width), F32)], [whole((rows, width))],
        2 * rows * width * cols * len(near), 16 * MIB,
    )[0]
    filled, turned, shards = [], [], []
    ring = Ring()
    for s in range(scenes):
        ds = far
        around = pass_blocks(attended[s], *turned)
        at = functools.partial(lambda s, i, p: (s, 0), s)
        operands = [
            acc, norm2_gain[None, :], policy_in, value_in,
            *(around[d] for d in ds), w_out, *filled,
        ]
        *filled, one = call(
            functools.partial(update, len(ds)), f"update{s}", place, len(ds), operands,
            [
                pl.BlockSpec((branch, width), at),
                whole((1, width)), whole(policy_in.shape), whole(value_in.shape),
                *[chunk] * len(ds), weight_spec(ds, cols, width),
                *[anywhere] * len(filled),
            ],
            [*full_shapes, jax.ShapeDtypeStruct((width, branch), BF16)],
            [
                pl.BlockSpec((branch, width), at),
                pl.BlockSpec((branch, hidden_count), at),
                pl.BlockSpec((branch, hidden_count), at),
                pl.BlockSpec((8, branch), functools.partial(lambda s, i, p: (0, s), s)),
                whole((width, branch)),
            ],
            2 * branch * width * (cols * len(ds) + 2 * hidden_count), 28 * MIB,
            [pltpu.VMEM((branch, width), F32)],
            {1 + len(operands) - len(filled) + k: k for k in range(len(filled))},
        )
        turned.append(one)
        if s == 0:
            shards.append([ring.step(one, one)])
    new_latent, keep, give, squares = filled

    for bit in (1, *far_bits()):
        squares = squares + swap(squares, bit)
    pre = keep + swap(after(give, *shards[0][0]), 1).astype(F32)
    mine = pre.astype(BF16)
    *upper, last = far_bits()
    for bit in upper:
        mine = (mine.astype(F32) + swap(mine, bit).astype(F32)).astype(BF16)
    rounds = wide_size // 2
    shards += [[ring.step(one, one)] for one in turned[1:]]
    for shard in shards:
        shard.append(ring.step(*shard[-1]))
    theirs = after(swap(mine, last), *shards[0][-1], *(b for one in shards for b in one[0]))
    quarter = hidden_count // chips // 4
    payload_shape = (rows + quarter + 16, hidden_count)
    payload, give = call(
        functools.partial(heads, full_width, total_rows), "heads", place, 1,
        [
            mine, theirs, squares, policy_out, value_out[None, :], targets[None, :],
            returns[None, :],
        ],
        [
            whole(half), whole(half), whole((8, rows)), whole(policy_out.shape),
            whole((1, hidden_count)), whole((1, rows)), whole((1, rows)),
        ],
        [
            jax.ShapeDtypeStruct(payload_shape, BF16),
            jax.ShapeDtypeStruct((quarter, hidden_count), BF16),
        ],
        [whole(payload_shape), whole((quarter, hidden_count))],
        6 * rows * hidden_count * action_count, 16 * MIB, [pltpu.VMEM(half, BF16)],
    )
    taken = jnp.where(first, payload[rows : rows + quarter], swap(give, 1))
    payload = lax.dynamic_update_slice(payload, taken, (rows, 0))

    payload_rounds = [[payload, payload]]
    for step in range(2, rounds - 1):
        for shard in shards:
            if len(payload_rounds) < rounds:
                payload_rounds.append(ring.step(*payload_rounds[-1]))
            shard.append(ring.step(*shard[-1]))
    while len(payload_rounds) < rounds:
        payload_rounds.append(ring.step(*payload_rounds[-1]))
    cut = scenes // 2
    for one, other in zip(shards[:cut], shards[cut:]):
        up, down = ring.step(one[-1][0], other[-1][1])
        one.append([up])
        other.append([down])
    size = hidden_count // 2
    up, down = payload_rounds[-1]
    payload_rounds.append(ring.step(up[:, :size], down[:, size:]))
    turned_all = list(turned)
    for step in range(rounds):
        for way in range(len(shards[0][step])):
            turned_all += [shard[step][way] for shard in shards]
    payload_own = [payload, *(b for pair in payload_rounds[1:] for b in pair)]
    payload_other = [swap(b, 1) for b in payload_own]

    pieces = [*payload_own, *payload_other]
    share_shape = (4 * quarter, action_count)
    share, losses, value_out_grad = call(
        functools.partial(sums, total_rows), "sums", place, 1, [*pieces, *pieces],
        [
            pl.BlockSpec((count, b.shape[1]), functools.partial(lambda at, i, p: (at, 0), start // count))
            for start, count in ((rows, quarter), (rows + quarter, 16))
            for b in pieces
        ],
        [
            jax.ShapeDtypeStruct(share_shape, BF16),
            jax.ShapeDtypeStruct((1, 2), F32),
            jax.ShapeDtypeStruct((hidden_count,), BF16),
        ],
        [whole(share_shape), whole((1, 2)), whole((hidden_count,))], 0, 8 * MIB,
    )
    losses = losses.reshape(2)
    shares = far_blocks(share)
    policy_out_grad = call(
        functools.partial(join, list(shares)), "join", place, 1, list(shares.values()),
        [whole(share_shape)] * len(shares),
        [jax.ShapeDtypeStruct((hidden_count, action_count), BF16)],
        [whole((hidden_count, action_count))], 0, 8 * MIB,
    )[0]

    block = 256
    grad_spec = pl.BlockSpec((block, hidden_count), lambda i, p: (i, 0))
    grad_flops = 4 * rows * width * hidden_count
    split = wide_size - 3

    def gradient(body, name, operands, specs, count, turned, own, other, dtype):
        return call(
            functools.partial(body, len(turned), len(own)), name, place, width // block,
            [*operands, *turned, *own, *other],
            [
                *specs,
                *[pl.BlockSpec((block, branch), lambda i, p: (i, 0))] * len(turned),
                *[
                    pl.BlockSpec(
                        (rows, b.shape[1]), lambda i, p: (0, 0), pipeline_mode=pl.Buffered(1)
                    )
                    for b in (*own, *other)
                ],
            ],
            [jax.ShapeDtypeStruct((width, hidden_count), dtype)] * 2, [grad_spec] * 2,
            grad_flops * count, 18 * MIB,
        )

    starts = gradient(
        gradients_start, "gradients_start", [], [], split, turned_all[: scenes * split],
        payload_own[:split], payload_other[:split], F32,
    )
    policy_in_grad, value_in_grad = gradient(
        gradients_end, "gradients_end", starts, [grad_spec] * 2, wide_size - split,
        turned_all[scenes * split :], payload_own[split:], payload_other[split:], BF16,
    )
    return (new_latent, losses, policy_in_grad, value_in_grad, policy_out_grad, value_out_grad)


def solution(mesh):
    placed = (
        P("wide", "narrow"),
        P("wide"),
        P(None, "narrow"),
        P("narrow"),
        P(None, "narrow"),
        P(None, "narrow"),
        P(None, "narrow"),
        P(None, "narrow"),
        P("wide", None, "narrow"),
        P("wide", None, "narrow"),
        P("narrow"),
        P("narrow", None),
        P("narrow", None),
        P(),
        P(),
        P("wide"),
        P("wide"),
    )
    return jax.shard_map(
        per_device,
        mesh=mesh,
        in_specs=placed,
        out_specs=(P("wide", "narrow"), P(), P("narrow", None), P("narrow", None), P(), P()),
        check_vma=False,
    )
```

```python
import functools

import jax
import jax.numpy as jnp
from jax import lax
from jax.experimental import pallas as pl
from jax.experimental.pallas import tpu as pltpu
from jax.sharding import PartitionSpec as P

HD = 128
EPSILON = 1e-05
F32 = jnp.float32
BF16 = jnp.bfloat16
MIB = 1 << 20


def swap(block, bit):
    size = lax.axis_size("narrow")
    return lax.ppermute(block, "narrow", [(n, n ^ bit) for n in range(size)])


def far_bits():
    bit = lax.axis_size("narrow") // 2
    while bit > 1:
        yield bit
        bit //= 2


def far_blocks(block):
    blocks = {0: block}
    for bit in far_bits():
        blocks.update({d ^ bit: swap(b, bit) for d, b in list(blocks.items())})
    return blocks


def pass_blocks(blocks, *earlier):
    far = {d ^ 1: swap(after(b, *earlier), 1) for d, b in blocks.items() if d > 1}
    return {**blocks, **far}


def after(block, *earlier):
    return lax.optimization_barrier((block, *earlier))[0]


def ring_order(size):
    return list(range(0, size, 2)) + list(range(size - 1, 0, -2))


def ring_step(block, way):
    order = ring_order(lax.axis_size("wide"))
    pairs = [(a, order[(i + way) % len(order)]) for i, a in enumerate(order)]
    return lax.ppermute(block, "wide", pairs)


class Ring:
    def __init__(self):
        self.arrived = []

    def step(self, *pair):
        held = self.arrived[-2] if len(self.arrived) > 1 else ((), ())
        up, down = (after(b, *h) for b, h in zip(pair, held))
        self.arrived.append(((ring_step(up, 1),), (ring_step(down, -1),)))
        return [self.arrived[-1][0][0], self.arrived[-1][1][0]]


def dot(a, b):
    return jnp.dot(a, b, preferred_element_type=F32)


def column(row):
    return jnp.transpose(jnp.broadcast_to(row, (128, row.shape[1])))[:, :1]


def whole(shape):
    return pl.BlockSpec(shape, lambda i, p: (0,) * len(shape))


def weight_spec(ds, rows, columns):
    def at(i, p):
        d = jnp.int32(ds[0])
        for j in range(1, len(ds)):
            d = jnp.where(i == j, ds[j], d)
        return (p[0] ^ d, 0)

    return pl.BlockSpec((rows, columns), at)


def add_products(x_refs, w_refs, add):
    for step, x_ref in enumerate(x_refs):

        @pl.when(pl.program_id(0) == step)
        def _():
            for j, w_ref in enumerate(w_refs):
                add(j, dot(x_ref[...], w_ref[...]))


def row_of(values):
    return jnp.transpose(jnp.broadcast_to(values, (values.shape[0], 128)))[:8]


def embed(p_ref, latent_ref, actions_ref, table_ref, gain_ref, tokens_out, block_out):
    shape = (table_ref.shape[0], latent_ref.shape[0])
    onehot = (lax.broadcasted_iota(jnp.int32, shape, 0) == actions_ref[...]).astype(BF16)
    picked = lax.dot_general(
        onehot, table_ref[...], (((0,), (0,)), ((), ())), preferred_element_type=F32
    )
    tokens = latent_ref[...].astype(F32) + picked
    tokens_out[...] = tokens
    count = latent_ref.shape[0]
    block_out[:count] = (tokens * gain_ref[...]).astype(BF16)
    block_out[count:] = jnp.zeros_like(block_out[count:])
    rest = row_of(jnp.sum(tokens * tokens, axis=1, keepdims=True))[:1]
    rows = lax.broadcasted_iota(jnp.int32, (16, count), 0)
    terms = jnp.zeros((16, count), F32)
    for k in range(3):
        term = rest.astype(BF16).astype(F32)
        terms = jnp.where(rows == k, term, terms)
        rest = rest - term
    block_out[count:, :count] = terms.astype(BF16)


def begin(near, far, p_ref, *refs):
    count = len(near)
    x_refs, weights, caches = refs[:count], refs[count : count + 3], refs[count + 3 : count + 5]
    acc, *outs, held, sems = refs[count + 5 :]
    size, cols = held.shape[1:]
    copies = []

    def send(src, dst):
        copies.append(pltpu.make_async_copy(src, dst, sems.at[len(copies)]))
        copies[-1].start()

    for i, d in enumerate(near + far):
        start = pl.multiple_of((p_ref[0] ^ d) * size, size)
        for j, w_ref in enumerate(weights):
            k = i * 3 + j
            send(
                w_ref.at[pl.ds(start, size)],
                held.at[k] if i < len(near) else outs[k - 3 * len(near)],
            )
    for src, dst in zip(caches, outs[-2:]):
        send(src, dst)
    for i in range(len(near)):
        for j in range(3):
            copies[i * 3 + j].wait()
            product = dot(x_refs[i][...], held[i * 3 + j])
            at = slice(j * cols, (j + 1) * cols)
            acc[:, at] = product if i == 0 else acc[:, at] + product
    for copy in copies[3 * len(near) :]:
        copy.wait()


def project_more(count, p_ref, acc_ref, *refs):
    x_refs, w_refs, out = refs[:count], refs[count:-1], refs[-1]
    cols = w_refs[0].shape[1]
    for j in range(3):
        at = slice(j * cols, (j + 1) * cols)
        total = acc_ref[:, at]
        for i, x_ref in enumerate(x_refs):
            total = total + dot(x_ref[...], w_refs[i * 3 + j][...])
        out[:, at] = total


def attend(count, sources, full_width, p_ref, acc_ref, keys_ref, values_ref, *refs):
    squares_refs, refs = refs[:sources], refs[sources:]
    project_more(count, p_ref, acc_ref, *refs[:-2], refs[-1])
    out, acc = refs[-2:]
    cols = refs[count].shape[1]
    squares = sum(jnp.sum(ref[:8].astype(F32), axis=0, keepdims=True) for ref in squares_refs)
    attend_heads(full_width, cols, squares, keys_ref, values_ref, out, acc)


def attend_heads(full_width, cols, squares, keys_ref, values_ref, out, acc):
    scenes = keys_ref.shape[0]
    branch = acc.shape[0] // scenes
    inverse = column(lax.rsqrt(squares / full_width + EPSILON))
    scaling = HD ** (-0.5)
    for s in range(scenes):
        rows = slice(s * branch, (s + 1) * branch)
        scale = inverse[rows]
        for h in range(cols // HD):
            at = slice(h * HD, (h + 1) * HD)
            q, k, v = (
                (acc[rows, j * cols + h * HD : j * cols + (h + 1) * HD] * scale).astype(BF16)
                for j in range(3)
            )
            scores = (
                lax.dot_general(
                    q,
                    keys_ref[s, :, at],
                    (((1,), (1,)), ((), ())),
                    preferred_element_type=F32,
                )
                * scaling
            )
            own = jnp.sum(q.astype(F32) * k.astype(F32), axis=1, keepdims=True) * scaling
            highest = jnp.maximum(jnp.max(scores, axis=1, keepdims=True), own)
            expd = jnp.exp(scores - highest)
            own_exp = jnp.exp(own - highest)
            total = jnp.sum(expd, axis=1, keepdims=True) + own_exp
            weights = (expd / total).astype(BF16)
            own_weight = (own_exp / total).astype(BF16)
            mixed = dot(weights, values_ref[s, :, at])
            mixed = mixed + own_weight.astype(F32) * v.astype(F32)
            out[rows, at] = mixed.astype(BF16)


def update_near(scenes, p_ref, tokens_ref, *refs):
    x_refs, w_ref, out = refs[:-2], refs[-2], refs[-1]
    for step in range(len(x_refs) // scenes):

        @pl.when(pl.program_id(0) == step)
        def _():
            x = jnp.concatenate(
                [ref[...] for ref in x_refs[step * scenes : (step + 1) * scenes]], axis=0
            )
            out[...] = (tokens_ref if step == 0 else out)[...] + dot(x, w_ref[...])


def update(count, p_ref, acc_ref, gain_ref, policy_ref, value_ref, *refs):
    x_refs, w_ref = refs[:count], refs[count]
    latent_out, keep_out, give_out, squares_out, turned_out, acc = refs[-6:]

    @pl.when(pl.program_id(0) == 0)
    def _():
        acc[...] = acc_ref[...]

    def add(j, product):
        acc[...] += product

    add_products(x_refs, [w_ref], add)

    @pl.when(pl.program_id(0) == count - 1)
    def _():
        state = acc[...]
        latent_out[...] = state.astype(BF16)
        squares = jnp.sum(state * state, axis=1, keepdims=True)
        squares_out[...] = row_of(squares)
        gained = (state * gain_ref[...]).astype(BF16)
        turned_out[...] = jnp.transpose(gained)
        policy = dot(gained, policy_ref[...])
        value = dot(gained, value_ref[...])

        @pl.when(p_ref[0] % 2 == 0)
        def _():
            keep_out[...] = policy
            give_out[...] = value.astype(BF16)

        @pl.when(p_ref[0] % 2 == 1)
        def _():
            keep_out[...] = value
            give_out[...] = policy.astype(BF16)


def heads(full_width, total_rows, p_ref, mine_ref, theirs_ref, squares_ref, policy_out_ref,
          value_out_ref, targets_ref, returns_ref, payload_out, give_out, hidden_ref):
    inverse = column(lax.rsqrt(squares_ref[:1] / full_width + EPSILON))
    pre = (mine_ref[...].astype(F32) + theirs_ref[...].astype(F32)) * inverse
    sigma = jax.nn.sigmoid(pre)
    hidden = (pre * sigma).astype(BF16)
    hidden_ref[...] = hidden
    slope = sigma * (1.0 + pre * (1.0 - sigma)) * inverse
    factor = total_rows ** (-0.5)
    count = hidden.shape[0]
    quarter = give_out.shape[0]
    part = 4 * quarter
    at = slice(count, count + quarter)

    def put_sums(grad, loss):
        shape = (payload_out.shape[0] - count - quarter, hidden.shape[1])
        rows = lax.broadcasted_iota(jnp.int32, shape, 0)
        lanes = lax.broadcasted_iota(jnp.int32, shape, 1)
        sums = jnp.where(rows == 0, grad, 0.0)
        for lane in range(3):
            term = loss.astype(BF16).astype(F32)
            sums = jnp.where((rows == 1) & (lanes == lane), term, sums)
            loss = loss - term
        payload_out[count + quarter :] = sums.astype(BF16)

    @pl.when(p_ref[0] % 2 == 0)
    def _():
        weight = policy_out_ref[...]
        logits = dot(hidden, weight)
        top = jnp.max(logits, axis=1, keepdims=True)
        log_total = top + jnp.log(jnp.sum(jnp.exp(logits - top), axis=1, keepdims=True))
        actions = lax.broadcasted_iota(jnp.int32, logits.shape, 1).astype(F32)
        onehot = (actions == column(targets_ref[...].astype(F32))).astype(F32)
        picked = jnp.sum(logits * onehot, axis=1, keepdims=True)
        loss = jnp.sum(log_total - picked, axis=0, keepdims=True)
        dlogits = ((jnp.exp(logits - log_total) - onehot) * factor).astype(BF16)
        back = lax.dot_general(
            dlogits, weight, (((1,), (1,)), ((), ())), preferred_element_type=F32
        )
        payload_out[:count] = (back * slope).astype(BF16)
        start = pl.multiple_of((p_ref[0] // 2) * part, part)
        grad = lax.dot_general(
            hidden_ref[:, pl.ds(start, part)],
            dlogits,
            (((0,), (0,)), ((), ())),
            preferred_element_type=F32,
        ).astype(BF16)
        parts = [grad[k * quarter : (k + 1) * quarter] for k in range(4)]
        payload_out[at] = jnp.concatenate(parts[:2], axis=1)
        give_out[...] = jnp.concatenate(parts[2:], axis=1)
        put_sums(jnp.zeros((1, hidden.shape[1]), F32), loss)

    @pl.when(p_ref[0] % 2 == 1)
    def _():
        weight = value_out_ref[...].astype(F32)
        hidden_f = hidden.astype(F32)
        value = jnp.sum(hidden_f * weight, axis=1, keepdims=True)
        errors = value - column(returns_ref[...])
        loss = 0.5 * jnp.sum(errors * errors, axis=0, keepdims=True)
        dvalue = (errors * factor).astype(BF16).astype(F32)
        payload_out[:count] = (dvalue * weight * slope).astype(BF16)
        payload_out[at] = jnp.zeros_like(give_out)
        give_out[...] = jnp.zeros_like(give_out)
        put_sums(jnp.sum(dvalue * hidden_f, axis=0, keepdims=True), loss)


def sums(total_rows, p_ref, *refs):
    count = (len(refs) - 3) // 4
    share_out, losses_out, grad_out = refs[-3:]

    def total(d_refs):
        *shards, ahead, back = [ref[...].astype(F32) for ref in d_refs]
        return sum(shards, jnp.concatenate([ahead, back], axis=1))

    own, other, own_sums, other_sums = (
        total(refs[k * count : (k + 1) * count]) for k in range(4)
    )
    first = p_ref[0] % 2 == 0
    quarter = own.shape[0]
    width = share_out.shape[1]
    for k, part in enumerate((jnp.where(first, own, other), jnp.where(first, other, own))):
        for j in range(2):
            at = (2 * k + j) * quarter
            share_out[at : at + quarter] = part[:, j * width : (j + 1) * width].astype(BF16)
    policy = jnp.where(first, own_sums, other_sums)
    value = jnp.where(first, other_sums, own_sums)
    grad_out[...] = value[0].astype(BF16)

    def loss(part):
        lanes = lax.broadcasted_iota(jnp.int32, (1, part.shape[1]), 1)
        return jnp.sum(jnp.where(lanes < 3, part[1:2], 0.0), axis=1, keepdims=True) / total_rows

    lanes = lax.broadcasted_iota(jnp.int32, (1, 2), 1)
    losses_out[...] = jnp.where(lanes == 0, loss(policy), loss(value))


def join(ds, p_ref, *refs):
    out = refs[-1]
    size = refs[0].shape[0]
    for d, ref in zip(ds, refs[:-1]):
        out[pl.ds(pl.multiple_of(((p_ref[0] ^ d) // 2) * size, size), size)] = ref[...]


def factors(turned_refs, own_refs, other_refs, halved):
    turned = jnp.concatenate([ref[...] for ref in turned_refs], axis=1)
    for d_refs in (own_refs, other_refs):
        shards = [ref[...] for ref in d_refs]
        if halved:
            shards[-2:] = [jnp.concatenate(shards[-2:], axis=1)]
        yield dot(turned, jnp.concatenate(shards, axis=0))


def gradients_start(turned_count, count, p_ref, *refs):
    turned, own, other = refs[:turned_count], refs[turned_count:][:count], refs[turned_count + count : -2]
    for out, product in zip(refs[-2:], factors(turned, own, other, False)):
        out[...] = product


def gradients_end(turned_count, count, p_ref, *refs):
    sums, refs, outs = refs[:2], refs[2:-2], refs[-2:]
    turned, own, other = refs[:turned_count], refs[turned_count:][:count], refs[turned_count + count :]
    own, other = (
        (acc[...] + product).astype(BF16)
        for acc, product in zip(sums, factors(turned, own, other, True))
    )

    @pl.when(p_ref[0] % 2 == 0)
    def _():
        outs[0][...] = own
        outs[1][...] = other

    @pl.when(p_ref[0] % 2 == 1)
    def _():
        outs[1][...] = own
        outs[0][...] = other


def call(body, name, place, steps, operands, in_specs, outs, out_specs, flops, limit, scratch=(), aliases=None):
    bytes_accessed = sum(x.size * x.dtype.itemsize for x in (*operands, *outs)) if flops else 0
    return pl.pallas_call(
        body,
        name=name,
        out_shape=outs,
        input_output_aliases=aliases or {},
        grid_spec=pltpu.PrefetchScalarGridSpec(
            num_scalar_prefetch=1,
            grid=(steps,),
            in_specs=in_specs,
            out_specs=out_specs,
            scratch_shapes=scratch,
        ),
        compiler_params=pltpu.CompilerParams(
            dimension_semantics=("arbitrary",), vmem_limit_bytes=limit
        ),
        cost_estimate=pl.CostEstimate(
            flops=flops, bytes_accessed=bytes_accessed, transcendentals=0
        ),
    )(place, *operands)


def per_device(
    latent,
    actions,
    action_table,
    norm1_gain,
    w_query,
    w_key,
    w_value,
    w_out,
    key_cache,
    value_cache,
    norm2_gain,
    policy_in,
    value_in,
    policy_out,
    value_out,
    targets,
    returns,
):
    rows, width = latent.shape
    narrow_size = lax.axis_size("narrow")
    wide_size = lax.axis_size("wide")
    full_width = width * narrow_size
    cols = w_query.shape[1]
    total_rows = rows * wide_size
    action_count = action_table.shape[0]
    hidden_count = policy_in.shape[1]
    index = lax.axis_index("narrow").astype(jnp.int32)
    place = index[None]
    first = index % 2 == 0
    chips = narrow_size // 2
    near = [0, 1]
    direct = list(range(2, narrow_size, 2))
    passed = [d + 1 for d in direct]

    far = direct + passed
    scenes = key_cache.shape[0]
    branch = rows // scenes
    hbm = functools.partial(pltpu.with_memory_space_constraint, memory_space=pltpu.HBM)

    block_shape = (rows + 16, width)
    tokens, block = call(
        embed, "embed", place, 1,
        [
            hbm(latent), hbm(actions[None, :]), hbm(action_table),
            hbm(norm1_gain[None, :]),
        ],
        [
            whole((rows, width)), whole((1, rows)), whole(action_table.shape),
            whole((1, width)),
        ],
        [
            jax.ShapeDtypeStruct((rows, width), F32),
            jax.ShapeDtypeStruct(block_shape, BF16),
        ],
        [whole((rows, width)), whole(block_shape)],
        2 * rows * width * action_count, 16 * MIB,
    )
    blocks = {**far_blocks(block), 1: swap(block, 1)}

    weights = [hbm(w) for w in (w_query, w_key, w_value)]
    x_spec = whole((rows, width))
    acc_shape = jax.ShapeDtypeStruct((rows, 3 * cols), F32)
    weight_shape = jax.ShapeDtypeStruct((width, cols), BF16)
    weight_block = whole((width, cols))
    cache_shape = jax.ShapeDtypeStruct(key_cache.shape, BF16)
    outs = [weight_shape] * (3 * len(far)) + [cache_shape] * 2
    anywhere = pl.BlockSpec(memory_space=pl.ANY)
    flops = 2 * rows * width * 3 * cols
    acc, *staged, keys, values = call(
        functools.partial(begin, near, far), "begin", place, 1,
        [
            *(blocks[d] for d in near), *weights,
            hbm(key_cache), hbm(value_cache),
        ],
        [*[x_spec] * len(near), *[anywhere] * 5],
        [acc_shape, *outs], [whole(acc_shape.shape), *[anywhere] * len(outs)],
        flops * len(near), 20 * MIB,
        [
            pltpu.VMEM((3 * len(near), width, cols), BF16),
            pltpu.SemaphoreType.DMA((3 * len(near) + len(outs),)),
        ],
    )
    staged_direct = staged[: 3 * len(direct)]
    staged_passed = staged[3 * len(direct) :]

    acc_spec = whole(acc_shape.shape)
    blocks = pass_blocks(blocks, acc)
    acc = call(
        functools.partial(project_more, len(direct)), "project", place, 1,
        [acc, *(blocks[d] for d in direct), *staged_direct],
        [acc_spec, *[x_spec] * len(direct), *[weight_block] * len(staged_direct)],
        [acc_shape], [acc_spec], flops * len(direct), 24 * MIB,
    )[0]

    attended = []
    for s in range(scenes):
        at = functools.partial(lambda s, i, p: (s, 0), s)
        squares_spec = pl.BlockSpec(
            (16, branch), functools.partial(lambda s, i, p: (rows // 16, s), s)
        )
        cache_spec = pl.BlockSpec(
            (1, *key_cache.shape[1:]), functools.partial(lambda s, i, p: (s, 0, 0), s)
        )
        one = call(
            functools.partial(attend, len(passed), narrow_size, full_width), f"attend{s}", place, 1,
            [
                acc, keys, values, *blocks.values(),
                *(blocks[d] for d in passed), *staged_passed,
            ],
            [
                pl.BlockSpec((branch, 3 * cols), at), cache_spec, cache_spec,
                *[squares_spec] * narrow_size,
                *[pl.BlockSpec((branch, width), at)] * len(passed), *[weight_block] * len(staged_passed),
            ],
            [jax.ShapeDtypeStruct((branch, cols), BF16)], [whole((branch, cols))],
            0, 20 * MIB, [pltpu.VMEM((branch, 3 * cols), F32)],
        )[0]
        attended.append({**far_blocks(one), 1: swap(one, 1)})

    half = (rows, hidden_count)
    full_shapes = [
        jax.ShapeDtypeStruct((rows, width), BF16),
        jax.ShapeDtypeStruct(half, F32),
        jax.ShapeDtypeStruct(half, BF16),
        jax.ShapeDtypeStruct((8, rows), F32),
    ]
    chunk = whole((branch, cols))
    acc = call(
        functools.partial(update_near, scenes), "update_near", place, len(near),
        [tokens, *(one[d] for d in near for one in attended), w_out],
        [
            whole((rows, width)), *[chunk] * (scenes * len(near)),
            weight_spec(near, cols, width),
        ],
        [jax.ShapeDtypeStruct((rows, width), F32)], [whole((rows, width))],
        2 * rows * width * cols * len(near), 16 * MIB,
    )[0]
    filled, turned, shards = [], [], []
    ring = Ring()
    for s in range(scenes):
        ds = far
        around = pass_blocks(attended[s], *turned)
        at = functools.partial(lambda s, i, p: (s, 0), s)
        operands = [
            acc, norm2_gain[None, :], policy_in, value_in,
            *(around[d] for d in ds), w_out, *filled,
        ]
        *filled, one = call(
            functools.partial(update, len(ds)), f"update{s}", place, len(ds), operands,
            [
                pl.BlockSpec((branch, width), at),
                whole((1, width)), whole(policy_in.shape), whole(value_in.shape),
                *[chunk] * len(ds), weight_spec(ds, cols, width),
                *[anywhere] * len(filled),
            ],
            [*full_shapes, jax.ShapeDtypeStruct((width, branch), BF16)],
            [
                pl.BlockSpec((branch, width), at),
                pl.BlockSpec((branch, hidden_count), at),
                pl.BlockSpec((branch, hidden_count), at),
                pl.BlockSpec((8, branch), functools.partial(lambda s, i, p: (0, s), s)),
                whole((width, branch)),
            ],
            2 * branch * width * (cols * len(ds) + 2 * hidden_count), 28 * MIB,
            [pltpu.VMEM((branch, width), F32)],
            {1 + len(operands) - len(filled) + k: k for k in range(len(filled))},
        )
        turned.append(one)
        if s == 0:
            shards.append([ring.step(one, one)])
    new_latent, keep, give, squares = filled

    for bit in (1, *far_bits()):
        squares = squares + swap(squares, bit)
    pre = keep + swap(after(give, *shards[0][0]), 1).astype(F32)
    mine = pre.astype(BF16)
    *upper, last = far_bits()
    for bit in upper:
        mine = (mine.astype(F32) + swap(mine, bit).astype(F32)).astype(BF16)
    rounds = wide_size // 2
    shards += [[ring.step(one, one)] for one in turned[1:]]
    for shard in shards:
        shard.append(ring.step(*shard[-1]))
    theirs = after(swap(mine, last), *shards[0][-1], *(b for one in shards for b in one[0]))
    quarter = hidden_count // chips // 4
    payload_shape = (rows + quarter + 16, hidden_count)
    payload, give = call(
        functools.partial(heads, full_width, total_rows), "heads", place, 1,
        [
            mine, theirs, squares, policy_out, value_out[None, :], targets[None, :],
            returns[None, :],
        ],
        [
            whole(half), whole(half), whole((8, rows)), whole(policy_out.shape),
            whole((1, hidden_count)), whole((1, rows)), whole((1, rows)),
        ],
        [
            jax.ShapeDtypeStruct(payload_shape, BF16),
            jax.ShapeDtypeStruct((quarter, hidden_count), BF16),
        ],
        [whole(payload_shape), whole((quarter, hidden_count))],
        6 * rows * hidden_count * action_count, 16 * MIB, [pltpu.VMEM(half, BF16)],
    )
    shards[0].append(ring.step(*shards[0][-1]))
    given = swap(after(give, *shards[-1][-1]), 1)
    taken = jnp.where(first, payload[rows : rows + quarter], given)
    payload = lax.dynamic_update_slice(payload, taken, (rows, 0))

    payload_rounds = [[payload, payload]]
    payload_rounds.append(ring.step(*payload_rounds[-1]))
    for step in range(2, rounds - 1):
        for shard in shards:
            if len(shard) == step:
                shard.append(ring.step(*shard[-1]))
                if len(payload_rounds) < rounds - 1:
                    payload_rounds.append(ring.step(*payload_rounds[-1]))
    cut = scenes // 2
    for one, other in zip(shards[:cut], shards[cut:]):
        up, down = ring.step(one[-1][0], other[-1][1])
        one.append([up])
        other.append([down])
    while len(payload_rounds) < rounds:
        payload_rounds.append(ring.step(*payload_rounds[-1]))
    size = hidden_count // 2
    up, down = payload_rounds[-1]
    payload_rounds.append(ring.step(up[:, :size], down[:, size:]))
    turned_all = list(turned)
    for step in range(rounds):
        for way in range(len(shards[0][step])):
            turned_all += [shard[step][way] for shard in shards]
    payload_own = [payload, *(b for pair in payload_rounds[1:] for b in pair)]
    split = wide_size - 3
    payload_other = [swap(b, 1) for b in payload_own[:split]]

    block = 256
    grad_spec = pl.BlockSpec((block, hidden_count), lambda i, p: (i, 0))
    grad_flops = 4 * rows * width * hidden_count

    def gradient(body, name, operands, specs, count, turned, own, other, dtype):
        return call(
            functools.partial(body, len(turned), len(own)), name, place, width // block,
            [*operands, *turned, *own, *other],
            [
                *specs,
                *[pl.BlockSpec((block, branch), lambda i, p: (i, 0))] * len(turned),
                *[
                    pl.BlockSpec(
                        (rows, b.shape[1]), lambda i, p: (0, 0), pipeline_mode=pl.Buffered(1)
                    )
                    for b in (*own, *other)
                ],
            ],
            [jax.ShapeDtypeStruct((width, hidden_count), dtype)] * 2, [grad_spec] * 2,
            grad_flops * count, 18 * MIB,
        )

    starts = gradient(
        gradients_start, "gradients_start", [], [], split, turned_all[: scenes * split],
        payload_own[:split], payload_other[:split], F32,
    )
    payload_other += [swap(b, 1) for b in payload_own[split:-2]]
    payload_other += [swap(after(b, *starts), 1) for b in payload_own[-2:]]

    pieces = [*payload_own, *payload_other]
    share_shape = (4 * quarter, action_count)
    share, losses, value_out_grad = call(
        functools.partial(sums, total_rows), "sums", place, 1, [*pieces, *pieces],
        [
            pl.BlockSpec((count, b.shape[1]), functools.partial(lambda at, i, p: (at, 0), start // count))
            for start, count in ((rows, quarter), (rows + quarter, 16))
            for b in pieces
        ],
        [
            jax.ShapeDtypeStruct(share_shape, BF16),
            jax.ShapeDtypeStruct((1, 2), F32),
            jax.ShapeDtypeStruct((hidden_count,), BF16),
        ],
        [whole(share_shape), whole((1, 2)), whole((hidden_count,))], 0, 8 * MIB,
    )
    losses = losses.reshape(2)
    shares = far_blocks(share)
    policy_out_grad = call(
        functools.partial(join, list(shares)), "join", place, 1, list(shares.values()),
        [whole(share_shape)] * len(shares),
        [jax.ShapeDtypeStruct((hidden_count, action_count), BF16)],
        [whole((hidden_count, action_count))], 0, 8 * MIB,
    )[0]

    policy_in_grad, value_in_grad = gradient(
        gradients_end, "gradients_end", starts, [grad_spec] * 2, wide_size - split,
        turned_all[scenes * split :], payload_own[split:], payload_other[split:], BF16,
    )
    return (new_latent, losses, policy_in_grad, value_in_grad, policy_out_grad, value_out_grad)


def solution(mesh):
    placed = (
        P("wide", "narrow"),
        P("wide"),
        P(None, "narrow"),
        P("narrow"),
        P(None, "narrow"),
        P(None, "narrow"),
        P(None, "narrow"),
        P(None, "narrow"),
        P("wide", None, "narrow"),
        P("wide", None, "narrow"),
        P("narrow"),
        P("narrow", None),
        P("narrow", None),
        P(),
        P(),
        P("wide"),
        P("wide"),
    )
    return jax.shard_map(
        per_device,
        mesh=mesh,
        in_specs=placed,
        out_specs=(P("wide", "narrow"), P(), P("narrow", None), P("narrow", None), P(), P()),
        check_vma=False,
    )
```

```python
import functools

import jax
import jax.numpy as jnp
from jax import lax
from jax.experimental import pallas as pl
from jax.experimental.pallas import tpu as pltpu
from jax.sharding import PartitionSpec as P

HD = 128
EPSILON = 1e-05
F32 = jnp.float32
BF16 = jnp.bfloat16
MIB = 1 << 20


def swap(block, bit):
    size = lax.axis_size("narrow")
    return lax.ppermute(block, "narrow", [(n, n ^ bit) for n in range(size)])


def far_bits():
    bit = lax.axis_size("narrow") // 2
    while bit > 1:
        yield bit
        bit //= 2


def far_blocks(block):
    blocks = {0: block}
    for bit in far_bits():
        blocks.update({d ^ bit: swap(b, bit) for d, b in list(blocks.items())})
    return blocks


def pass_blocks(blocks, *earlier):
    far = {d ^ 1: swap(after(b, *earlier), 1) for d, b in blocks.items() if d > 1}
    return {**blocks, **far}


def after(block, *earlier):
    return lax.optimization_barrier((block, *earlier))[0]


def ring_order(size):
    return list(range(0, size, 2)) + list(range(size - 1, 0, -2))


def ring_step(block, way):
    order = ring_order(lax.axis_size("wide"))
    pairs = [(a, order[(i + way) % len(order)]) for i, a in enumerate(order)]
    return lax.ppermute(block, "wide", pairs)


def ring_round(up, down):
    return [ring_step(up, 1), ring_step(down, -1)]


def dot(a, b):
    return jnp.dot(a, b, preferred_element_type=F32)


def column(row):
    return jnp.transpose(jnp.broadcast_to(row, (128, row.shape[1])))[:, :1]


def whole(shape):
    return pl.BlockSpec(shape, lambda i, p: (0,) * len(shape))


def weight_spec(ds, rows, columns):
    def at(i, p):
        d = jnp.int32(ds[0])
        for j in range(1, len(ds)):
            d = jnp.where(i == j, ds[j], d)
        return (p[0] ^ d, 0)

    return pl.BlockSpec((rows, columns), at)


def add_products(x_refs, w_refs, add):
    for step, x_ref in enumerate(x_refs):

        @pl.when(pl.program_id(0) == step)
        def _():
            for j, w_ref in enumerate(w_refs):
                add(j, dot(x_ref[...], w_ref[...]))


def row_of(values):
    return jnp.transpose(jnp.broadcast_to(values, (values.shape[0], 128)))[:8]


def embed(p_ref, latent_ref, actions_ref, table_ref, gain_ref, tokens_out, block_out):
    shape = (table_ref.shape[0], latent_ref.shape[0])
    onehot = (lax.broadcasted_iota(jnp.int32, shape, 0) == actions_ref[...]).astype(BF16)
    picked = lax.dot_general(
        onehot, table_ref[...], (((0,), (0,)), ((), ())), preferred_element_type=F32
    )
    tokens = latent_ref[...].astype(F32) + picked
    tokens_out[...] = tokens
    count = latent_ref.shape[0]
    block_out[:count] = (tokens * gain_ref[...]).astype(BF16)
    block_out[count:] = jnp.zeros_like(block_out[count:])
    rest = row_of(jnp.sum(tokens * tokens, axis=1, keepdims=True))[:1]
    rows = lax.broadcasted_iota(jnp.int32, (16, count), 0)
    terms = jnp.zeros((16, count), F32)
    for k in range(3):
        term = rest.astype(BF16).astype(F32)
        terms = jnp.where(rows == k, term, terms)
        rest = rest - term
    block_out[count:, :count] = terms.astype(BF16)


def begin(near, far, p_ref, *refs):
    count = len(near)
    x_refs, weights, caches = refs[:count], refs[count : count + 3], refs[count + 3 : count + 5]
    acc, *outs, held, sems = refs[count + 5 :]
    size, cols = held.shape[1:]
    copies = []

    def send(src, dst):
        copies.append(pltpu.make_async_copy(src, dst, sems.at[len(copies)]))
        copies[-1].start()

    for i, d in enumerate(near + far):
        start = pl.multiple_of((p_ref[0] ^ d) * size, size)
        for j, w_ref in enumerate(weights):
            k = i * 3 + j
            send(
                w_ref.at[pl.ds(start, size)],
                held.at[k] if i < len(near) else outs[k - 3 * len(near)],
            )
    for src, dst in zip(caches, outs[-2:]):
        send(src, dst)
    for i in range(len(near)):
        for j in range(3):
            copies[i * 3 + j].wait()
            product = dot(x_refs[i][...], held[i * 3 + j])
            at = slice(j * cols, (j + 1) * cols)
            acc[:, at] = product if i == 0 else acc[:, at] + product
    for copy in copies[3 * len(near) :]:
        copy.wait()


def project_more(count, p_ref, acc_ref, *refs):
    x_refs, w_refs, out = refs[:count], refs[count:-1], refs[-1]
    cols = w_refs[0].shape[1]
    for j in range(3):
        at = slice(j * cols, (j + 1) * cols)
        total = acc_ref[:, at]
        for i, x_ref in enumerate(x_refs):
            total = total + dot(x_ref[...], w_refs[i * 3 + j][...])
        out[:, at] = total


def attend(count, sources, full_width, p_ref, acc_ref, keys_ref, values_ref, *refs):
    squares_refs, refs = refs[:sources], refs[sources:]
    project_more(count, p_ref, acc_ref, *refs[:-2], refs[-1])
    out, acc = refs[-2:]
    cols = refs[count].shape[1]
    squares = sum(jnp.sum(ref[:8].astype(F32), axis=0, keepdims=True) for ref in squares_refs)
    attend_heads(full_width, cols, squares, keys_ref, values_ref, out, acc)


def attend_heads(full_width, cols, squares, keys_ref, values_ref, out, acc):
    scenes = keys_ref.shape[0]
    branch = acc.shape[0] // scenes
    inverse = column(lax.rsqrt(squares / full_width + EPSILON))
    scaling = HD ** (-0.5)
    for s in range(scenes):
        rows = slice(s * branch, (s + 1) * branch)
        scale = inverse[rows]
        for h in range(cols // HD):
            at = slice(h * HD, (h + 1) * HD)
            q, k, v = (
                (acc[rows, j * cols + h * HD : j * cols + (h + 1) * HD] * scale).astype(BF16)
                for j in range(3)
            )
            scores = (
                lax.dot_general(
                    q,
                    keys_ref[s, :, at],
                    (((1,), (1,)), ((), ())),
                    preferred_element_type=F32,
                )
                * scaling
            )
            own = jnp.sum(q.astype(F32) * k.astype(F32), axis=1, keepdims=True) * scaling
            highest = jnp.maximum(jnp.max(scores, axis=1, keepdims=True), own)
            expd = jnp.exp(scores - highest)
            own_exp = jnp.exp(own - highest)
            total = jnp.sum(expd, axis=1, keepdims=True) + own_exp
            weights = (expd / total).astype(BF16)
            own_weight = (own_exp / total).astype(BF16)
            mixed = dot(weights, values_ref[s, :, at])
            mixed = mixed + own_weight.astype(F32) * v.astype(F32)
            out[rows, at] = mixed.astype(BF16)


def update_near(p_ref, tokens_ref, *refs):
    x_refs, w_ref, out = refs[:-2], refs[-2], refs[-1]

    @pl.when(pl.program_id(0) == 0)
    def _():
        out[...] = tokens_ref[...]

    def add(j, product):
        out[...] += product

    add_products(x_refs, [w_ref], add)


def update(count, p_ref, acc_ref, gain_ref, policy_ref, value_ref, *refs):
    x_refs, w_ref = refs[:count], refs[count]
    latent_out, keep_out, give_out, squares_out, turned_out, acc = refs[-6:]

    @pl.when(pl.program_id(0) == 0)
    def _():
        acc[...] = acc_ref[...]

    def add(j, product):
        acc[...] += product

    add_products(x_refs, [w_ref], add)

    @pl.when(pl.program_id(0) == count - 1)
    def _():
        state = acc[...]
        latent_out[...] = state.astype(BF16)
        squares = jnp.sum(state * state, axis=1, keepdims=True)
        squares_out[...] = row_of(squares)
        gained = (state * gain_ref[...]).astype(BF16)
        turned_out[...] = jnp.transpose(gained)
        policy = dot(gained, policy_ref[...])
        value = dot(gained, value_ref[...])

        @pl.when(p_ref[0] % 2 == 0)
        def _():
            keep_out[...] = policy
            give_out[...] = value.astype(BF16)

        @pl.when(p_ref[0] % 2 == 1)
        def _():
            keep_out[...] = value
            give_out[...] = policy.astype(BF16)


def heads(full_width, total_rows, p_ref, mine_ref, theirs_ref, squares_ref, policy_out_ref,
          value_out_ref, targets_ref, returns_ref, payload_out, give_out, hidden_ref):
    inverse = column(lax.rsqrt(squares_ref[:1] / full_width + EPSILON))
    pre = (mine_ref[...].astype(F32) + theirs_ref[...].astype(F32)) * inverse
    sigma = jax.nn.sigmoid(pre)
    hidden = (pre * sigma).astype(BF16)
    hidden_ref[...] = hidden
    slope = sigma * (1.0 + pre * (1.0 - sigma)) * inverse
    factor = total_rows ** (-0.5)
    count = hidden.shape[0]
    quarter = give_out.shape[0]
    part = 4 * quarter
    at = slice(count, count + quarter)

    def put_sums(grad, loss):
        shape = (payload_out.shape[0] - count - quarter, hidden.shape[1])
        rows = lax.broadcasted_iota(jnp.int32, shape, 0)
        lanes = lax.broadcasted_iota(jnp.int32, shape, 1)
        sums = jnp.where(rows == 0, grad, 0.0)
        for lane in range(3):
            term = loss.astype(BF16).astype(F32)
            sums = jnp.where((rows == 1) & (lanes == lane), term, sums)
            loss = loss - term
        payload_out[count + quarter :] = sums.astype(BF16)

    @pl.when(p_ref[0] % 2 == 0)
    def _():
        weight = policy_out_ref[...]
        logits = dot(hidden, weight)
        top = jnp.max(logits, axis=1, keepdims=True)
        log_total = top + jnp.log(jnp.sum(jnp.exp(logits - top), axis=1, keepdims=True))
        actions = lax.broadcasted_iota(jnp.int32, logits.shape, 1).astype(F32)
        onehot = (actions == column(targets_ref[...].astype(F32))).astype(F32)
        picked = jnp.sum(logits * onehot, axis=1, keepdims=True)
        loss = jnp.sum(log_total - picked, axis=0, keepdims=True)
        dlogits = ((jnp.exp(logits - log_total) - onehot) * factor).astype(BF16)
        back = lax.dot_general(
            dlogits, weight, (((1,), (1,)), ((), ())), preferred_element_type=F32
        )
        payload_out[:count] = (back * slope).astype(BF16)
        start = pl.multiple_of((p_ref[0] // 2) * part, part)
        grad = lax.dot_general(
            hidden_ref[:, pl.ds(start, part)],
            dlogits,
            (((0,), (0,)), ((), ())),
            preferred_element_type=F32,
        ).astype(BF16)
        parts = [grad[k * quarter : (k + 1) * quarter] for k in range(4)]
        payload_out[at] = jnp.concatenate(parts[:2], axis=1)
        give_out[...] = jnp.concatenate(parts[2:], axis=1)
        put_sums(jnp.zeros((1, hidden.shape[1]), F32), loss)

    @pl.when(p_ref[0] % 2 == 1)
    def _():
        weight = value_out_ref[...].astype(F32)
        hidden_f = hidden.astype(F32)
        value = jnp.sum(hidden_f * weight, axis=1, keepdims=True)
        errors = value - column(returns_ref[...])
        loss = 0.5 * jnp.sum(errors * errors, axis=0, keepdims=True)
        dvalue = (errors * factor).astype(BF16).astype(F32)
        payload_out[:count] = (dvalue * weight * slope).astype(BF16)
        payload_out[at] = jnp.zeros_like(give_out)
        give_out[...] = jnp.zeros_like(give_out)
        put_sums(jnp.sum(dvalue * hidden_f, axis=0, keepdims=True), loss)


def sums(total_rows, p_ref, *refs):
    count = (len(refs) - 3) // 4
    share_out, losses_out, grad_out = refs[-3:]

    def total(d_refs):
        *shards, ahead, back = [ref[...].astype(F32) for ref in d_refs]
        return sum(shards, jnp.concatenate([ahead, back], axis=1))

    own, other, own_sums, other_sums = (
        total(refs[k * count : (k + 1) * count]) for k in range(4)
    )
    first = p_ref[0] % 2 == 0
    quarter = own.shape[0]
    width = share_out.shape[1]
    for k, part in enumerate((jnp.where(first, own, other), jnp.where(first, other, own))):
        for j in range(2):
            at = (2 * k + j) * quarter
            share_out[at : at + quarter] = part[:, j * width : (j + 1) * width].astype(BF16)
    policy = jnp.where(first, own_sums, other_sums)
    value = jnp.where(first, other_sums, own_sums)
    grad_out[...] = value[0].astype(BF16)

    def loss(part):
        lanes = lax.broadcasted_iota(jnp.int32, (1, part.shape[1]), 1)
        return jnp.sum(jnp.where(lanes < 3, part[1:2], 0.0), axis=1, keepdims=True) / total_rows

    lanes = lax.broadcasted_iota(jnp.int32, (1, 2), 1)
    losses_out[...] = jnp.where(lanes == 0, loss(policy), loss(value))


def join(ds, p_ref, *refs):
    out = refs[-1]
    size = refs[0].shape[0]
    for d, ref in zip(ds, refs[:-1]):
        out[pl.ds(pl.multiple_of(((p_ref[0] ^ d) // 2) * size, size), size)] = ref[...]


def factors(turned_refs, own_refs, other_refs, halved):
    shards = [ref[...] for ref in turned_refs]
    if halved:
        upper = pl.program_id(0) < pl.num_programs(0) // 2
        shards[-2:] = [jnp.where(upper, *shards[-2:])]
    turned = jnp.concatenate(shards, axis=1)
    for d_refs in (own_refs, other_refs):
        shards = [ref[...] for ref in d_refs]
        if halved:
            shards[-2:] = [jnp.concatenate(shards[-2:], axis=1)]
        yield dot(turned, jnp.concatenate(shards, axis=0))


def gradients_start(turned_count, count, p_ref, *refs):
    turned, own, other = refs[:turned_count], refs[turned_count:][:count], refs[turned_count + count : -2]
    for out, product in zip(refs[-2:], factors(turned, own, other, False)):
        out[...] = product


def gradients_end(turned_count, count, p_ref, *refs):
    sums, refs, outs = refs[:2], refs[2:-2], refs[-2:]
    turned, own, other = refs[:turned_count], refs[turned_count:][:count], refs[turned_count + count :]
    own, other = (
        (acc[...] + product).astype(BF16)
        for acc, product in zip(sums, factors(turned, own, other, True))
    )

    @pl.when(p_ref[0] % 2 == 0)
    def _():
        outs[0][...] = own
        outs[1][...] = other

    @pl.when(p_ref[0] % 2 == 1)
    def _():
        outs[1][...] = own
        outs[0][...] = other


def call(body, name, place, steps, operands, in_specs, outs, out_specs, flops, limit, scratch=(), aliases=None):
    bytes_accessed = sum(x.size * x.dtype.itemsize for x in (*operands, *outs)) if flops else 0
    return pl.pallas_call(
        body,
        name=name,
        out_shape=outs,
        input_output_aliases=aliases or {},
        grid_spec=pltpu.PrefetchScalarGridSpec(
            num_scalar_prefetch=1,
            grid=(steps,),
            in_specs=in_specs,
            out_specs=out_specs,
            scratch_shapes=scratch,
        ),
        compiler_params=pltpu.CompilerParams(
            dimension_semantics=("arbitrary",), vmem_limit_bytes=limit
        ),
        cost_estimate=pl.CostEstimate(
            flops=flops, bytes_accessed=bytes_accessed, transcendentals=0
        ),
    )(place, *operands)


def per_device(
    latent,
    actions,
    action_table,
    norm1_gain,
    w_query,
    w_key,
    w_value,
    w_out,
    key_cache,
    value_cache,
    norm2_gain,
    policy_in,
    value_in,
    policy_out,
    value_out,
    targets,
    returns,
):
    rows, width = latent.shape
    narrow_size = lax.axis_size("narrow")
    wide_size = lax.axis_size("wide")
    full_width = width * narrow_size
    cols = w_query.shape[1]
    total_rows = rows * wide_size
    action_count = action_table.shape[0]
    hidden_count = policy_in.shape[1]
    index = lax.axis_index("narrow").astype(jnp.int32)
    place = index[None]
    first = index % 2 == 0
    chips = narrow_size // 2
    near = [0, 1]
    direct = list(range(2, narrow_size, 2))
    passed = [d + 1 for d in direct]

    far = direct + passed
    hbm = functools.partial(pltpu.with_memory_space_constraint, memory_space=pltpu.HBM)

    block_shape = (rows + 16, width)
    tokens, block = call(
        embed, "embed", place, 1,
        [
            hbm(latent), hbm(actions[None, :]), hbm(action_table),
            hbm(norm1_gain[None, :]),
        ],
        [
            whole((rows, width)), whole((1, rows)), whole(action_table.shape),
            whole((1, width)),
        ],
        [
            jax.ShapeDtypeStruct((rows, width), F32),
            jax.ShapeDtypeStruct(block_shape, BF16),
        ],
        [whole((rows, width)), whole(block_shape)],
        2 * rows * width * action_count, 16 * MIB,
    )
    blocks = {**far_blocks(block), 1: swap(block, 1)}

    weights = [hbm(w) for w in (w_query, w_key, w_value)]
    x_spec = whole((rows, width))
    acc_shape = jax.ShapeDtypeStruct((rows, 3 * cols), F32)
    weight_shape = jax.ShapeDtypeStruct((width, cols), BF16)
    weight_block = whole((width, cols))
    cache_shape = jax.ShapeDtypeStruct(key_cache.shape, BF16)
    outs = [weight_shape] * (3 * len(far)) + [cache_shape] * 2
    anywhere = pl.BlockSpec(memory_space=pl.ANY)
    flops = 2 * rows * width * 3 * cols
    acc, *staged, keys, values = call(
        functools.partial(begin, near, far), "begin", place, 1,
        [
            *(blocks[d] for d in near), *weights,
            hbm(key_cache), hbm(value_cache),
        ],
        [*[x_spec] * len(near), *[anywhere] * 5],
        [acc_shape, *outs], [whole(acc_shape.shape), *[anywhere] * len(outs)],
        flops * len(near), 20 * MIB,
        [
            pltpu.VMEM((3 * len(near), width, cols), BF16),
            pltpu.SemaphoreType.DMA((3 * len(near) + len(outs),)),
        ],
    )
    staged_direct = staged[: 3 * len(direct)]
    staged_passed = staged[3 * len(direct) :]

    acc_spec = whole(acc_shape.shape)
    blocks = pass_blocks(blocks, acc)
    acc = call(
        functools.partial(project_more, len(direct)), "project", place, 1,
        [acc, *(blocks[d] for d in direct), *staged_direct],
        [acc_spec, *[x_spec] * len(direct), *[weight_block] * len(staged_direct)],
        [acc_shape], [acc_spec], flops * len(direct), 24 * MIB,
    )[0]

    squares_spec = pl.BlockSpec((16, rows), lambda i, p: (rows // 16, 0))
    cache_spec = whole(key_cache.shape)
    attended = call(
        functools.partial(attend, len(passed), narrow_size, full_width), "attend", place, 1,
        [
            acc, keys, values, *blocks.values(),
            *(blocks[d] for d in passed), *staged_passed,
        ],
        [
            acc_spec, cache_spec, cache_spec, *[squares_spec] * narrow_size,
            *[x_spec] * len(passed), *[weight_block] * len(staged_passed),
        ],
        [jax.ShapeDtypeStruct((rows, cols), BF16)], [whole((rows, cols))],
        0, 24 * MIB, [pltpu.VMEM((rows, 3 * cols), F32)],
    )[0]

    blocks = {**far_blocks(attended), 1: swap(attended, 1)}
    half = (rows, hidden_count)
    x_spec = whole((rows, cols))
    state_spec = whole((rows, width))
    acc = call(
        update_near, "update_near", place, len(near),
        [tokens, *(blocks[d] for d in near), w_out],
        [state_spec, *[x_spec] * len(near), weight_spec(near, cols, width)],
        [jax.ShapeDtypeStruct((rows, width), F32)], [state_spec],
        2 * rows * width * cols * len(near), 16 * MIB,
    )[0]
    blocks = pass_blocks(blocks, acc)
    new_latent, keep, give, squares, turned = call(
        functools.partial(update, len(far)), "update", place, len(far),
        [
            acc, norm2_gain[None, :], policy_in, value_in,
            *(blocks[d] for d in far), w_out,
        ],
        [
            state_spec, whole((1, width)), whole(policy_in.shape), whole(value_in.shape),
            *[x_spec] * len(far), weight_spec(far, cols, width),
        ],
        [
            jax.ShapeDtypeStruct((rows, width), BF16),
            jax.ShapeDtypeStruct(half, F32),
            jax.ShapeDtypeStruct(half, BF16),
            jax.ShapeDtypeStruct((8, rows), F32),
            jax.ShapeDtypeStruct((width, rows), BF16),
        ],
        [state_spec, whole(half), whole(half), whole((8, rows)), whole((width, rows))],
        2 * rows * width * (cols * len(far) + 2 * hidden_count), 28 * MIB,
        [pltpu.VMEM((rows, width), F32)],
    )

    rounds = wide_size // 2
    shards = [[turned, turned]]
    shards.append(ring_round(*shards[0]))

    for bit in (1, *far_bits()):
        squares = squares + swap(squares, bit)
    pre = keep + swap(give, 1).astype(F32)
    mine = pre.astype(BF16)
    *upper, last = far_bits()
    for bit in upper:
        mine = (mine.astype(F32) + swap(mine, bit).astype(F32)).astype(BF16)
    theirs = after(swap(mine, last), *shards[1])
    quarter = hidden_count // chips // 4
    payload_shape = (rows + quarter + 16, hidden_count)
    payload, give = call(
        functools.partial(heads, full_width, total_rows), "heads", place, 1,
        [
            mine, theirs, squares, policy_out, value_out[None, :], targets[None, :],
            returns[None, :],
        ],
        [
            whole(half), whole(half), whole((8, rows)), whole(policy_out.shape),
            whole((1, hidden_count)), whole((1, rows)), whole((1, rows)),
        ],
        [
            jax.ShapeDtypeStruct(payload_shape, BF16),
            jax.ShapeDtypeStruct((quarter, hidden_count), BF16),
        ],
        [whole(payload_shape), whole((quarter, hidden_count))],
        6 * rows * hidden_count * action_count, 16 * MIB, [pltpu.VMEM(half, BF16)],
    )
    taken = jnp.where(first, payload[rows : rows + quarter], swap(give, 1))
    payload = lax.dynamic_update_slice(payload, taken, (rows, 0))

    payload_rounds = [[payload, payload]]
    for step in range(1, rounds):
        up, down = shards[-1]
        if step == rounds - 1:
            up, down = up[: width // 2], down[width // 2 :]
        shards.append(ring_round(up, down))
        payload_rounds.append(ring_round(*payload_rounds[-1]))
    up, down = payload_rounds[-1]
    size = hidden_count // 2
    up, down = after(up[:, :size], shards[-1][0]), after(down[:, size:], shards[-1][1])
    payload_rounds.append(ring_round(up, down))
    turned_all = [turned, *(b for pair in shards[1:] for b in pair)]
    payload_own = [payload, *(b for pair in payload_rounds[1:] for b in pair)]
    split = wide_size - 3
    payload_other = [swap(b, 1) for b in payload_own[:split]]

    block = 256
    grad_spec = pl.BlockSpec((block, hidden_count), lambda i, p: (i, 0))
    grad_flops = 4 * rows * width * hidden_count

    def block_at(count, k, i, p):
        at = i - count * (k % 2) if count * block < width else i
        return (jnp.clip(at, 0, count - 1), 0)

    def gradient(body, name, operands, specs, count, turned, own, other, dtype):
        return call(
            functools.partial(body, len(turned), len(own)), name, place, width // block,
            [*operands, *turned, *own, *other],
            [
                *specs,
                *[
                    pl.BlockSpec((block, rows), functools.partial(block_at, b.shape[0] // block, k))
                    for k, b in enumerate(turned)
                ],
                *[
                    pl.BlockSpec(
                        (rows, b.shape[1]), lambda i, p: (0, 0), pipeline_mode=pl.Buffered(1)
                    )
                    for b in (*own, *other)
                ],
            ],
            [jax.ShapeDtypeStruct((width, hidden_count), dtype)] * 2, [grad_spec] * 2,
            grad_flops * count, 18 * MIB,
        )

    starts = gradient(
        gradients_start, "gradients_start", [], [], split, turned_all[:split],
        payload_own[:split], payload_other[:split], F32,
    )
    payload_other += [swap(b, 1) for b in payload_own[split:-2]]
    payload_other += [swap(after(b, *starts), 1) for b in payload_own[-2:]]

    pieces = [*payload_own, *payload_other]
    share_shape = (4 * quarter, action_count)
    share, losses, value_out_grad = call(
        functools.partial(sums, total_rows), "sums", place, 1, [*pieces, *pieces],
        [
            pl.BlockSpec((count, b.shape[1]), functools.partial(lambda at, i, p: (at, 0), start // count))
            for start, count in ((rows, quarter), (rows + quarter, 16))
            for b in pieces
        ],
        [
            jax.ShapeDtypeStruct(share_shape, BF16),
            jax.ShapeDtypeStruct((1, 2), F32),
            jax.ShapeDtypeStruct((hidden_count,), BF16),
        ],
        [whole(share_shape), whole((1, 2)), whole((hidden_count,))], 0, 8 * MIB,
    )
    losses = losses.reshape(2)
    shares = far_blocks(share)
    policy_out_grad = call(
        functools.partial(join, list(shares)), "join", place, 1, list(shares.values()),
        [whole(share_shape)] * len(shares),
        [jax.ShapeDtypeStruct((hidden_count, action_count), BF16)],
        [whole((hidden_count, action_count))], 0, 8 * MIB,
    )[0]

    policy_in_grad, value_in_grad = gradient(
        gradients_end, "gradients_end", starts, [grad_spec] * 2, wide_size - split,
        turned_all[split:], payload_own[split:], payload_other[split:], BF16,
    )
    return (new_latent, losses, policy_in_grad, value_in_grad, policy_out_grad, value_out_grad)


def solution(mesh):
    placed = (
        P("wide", "narrow"),
        P("wide"),
        P(None, "narrow"),
        P("narrow"),
        P(None, "narrow"),
        P(None, "narrow"),
        P(None, "narrow"),
        P(None, "narrow"),
        P("wide", None, "narrow"),
        P("wide", None, "narrow"),
        P("narrow"),
        P("narrow", None),
        P("narrow", None),
        P(),
        P(),
        P("wide"),
        P("wide"),
    )
    return jax.shard_map(
        per_device,
        mesh=mesh,
        in_specs=placed,
        out_specs=(P("wide", "narrow"), P(), P("narrow", None), P("narrow", None), P(), P()),
        check_vma=False,
    )
```

```python
import functools

import jax
import jax.numpy as jnp
from jax import lax
from jax.experimental import pallas as pl
from jax.experimental.pallas import tpu as pltpu
from jax.sharding import PartitionSpec as P

HD = 128
EPSILON = 1e-05
F32 = jnp.float32
BF16 = jnp.bfloat16
MIB = 1 << 20
HOLDS = {
    "give": ("s0t1",),
    "heads": ("s0t2", "s1t1", "s1t2"),
    "share": ("s1t2",),
    "s0t3": ("s1t2",),
    "s1t3": ("s0t3",),
    "s0t4": ("s1t3",),
    "p4": ("s1t3",),
}
EARLY = ("s0t2", "s1t2", "s0t3")


def swap(block, bit):
    size = lax.axis_size("narrow")
    return lax.ppermute(block, "narrow", [(n, n ^ bit) for n in range(size)])


def far_bits():
    bit = lax.axis_size("narrow") // 2
    while bit > 1:
        yield bit
        bit //= 2


def far_blocks(block):
    blocks = {0: block}
    for bit in far_bits():
        blocks.update({d ^ bit: swap(b, bit) for d, b in list(blocks.items())})
    return blocks


def pass_blocks(blocks, *earlier):
    far = {d ^ 1: swap(after(b, *earlier), 1) for d, b in blocks.items() if d > 1}
    return {**blocks, **far}


def after(block, *earlier):
    return lax.optimization_barrier((block, *earlier))[0]


def ring_order(size):
    return list(range(0, size, 2)) + list(range(size - 1, 0, -2))


def ring_step(block, way):
    order = ring_order(lax.axis_size("wide"))
    pairs = [(a, order[(i + way) % len(order)]) for i, a in enumerate(order)]
    return lax.ppermute(block, "wide", pairs)


class Ring:
    def __init__(self):
        self.at = {}

    def arrived(self, names):
        return [b for name in names for b in self.at.get(name, ())]

    def step(self, name, up, down):
        held = HOLDS.get(name, ())
        up, down = after(up, *self.arrived(held)), after(down, *self.arrived(held))
        self.at[name] = [ring_step(up, 1), ring_step(down, -1)]
        return self.at[name]


def dot(a, b):
    return jnp.dot(a, b, preferred_element_type=F32)


def column(row):
    return jnp.transpose(jnp.broadcast_to(row, (128, row.shape[1])))[:, :1]


def whole(shape):
    return pl.BlockSpec(shape, lambda i, p: (0,) * len(shape))


def weight_spec(ds, rows, columns):
    def at(i, p):
        d = jnp.int32(ds[0])
        for j in range(1, len(ds)):
            d = jnp.where(i == j, ds[j], d)
        return (p[0] ^ d, 0)

    return pl.BlockSpec((rows, columns), at)


def add_products(x_refs, w_refs, add):
    for step, x_ref in enumerate(x_refs):

        @pl.when(pl.program_id(0) == step)
        def _():
            for j, w_ref in enumerate(w_refs):
                add(j, dot(x_ref[...], w_ref[...]))


def row_of(values):
    return jnp.transpose(jnp.broadcast_to(values, (values.shape[0], 128)))[:8]


def embed(p_ref, latent_ref, actions_ref, table_ref, gain_ref, tokens_out, block_out):
    shape = (table_ref.shape[0], latent_ref.shape[0])
    onehot = (lax.broadcasted_iota(jnp.int32, shape, 0) == actions_ref[...]).astype(BF16)
    picked = lax.dot_general(
        onehot, table_ref[...], (((0,), (0,)), ((), ())), preferred_element_type=F32
    )
    tokens = latent_ref[...].astype(F32) + picked
    tokens_out[...] = tokens
    count = latent_ref.shape[0]
    block_out[:count] = (tokens * gain_ref[...]).astype(BF16)
    block_out[count:] = jnp.zeros_like(block_out[count:])
    rest = row_of(jnp.sum(tokens * tokens, axis=1, keepdims=True))[:1]
    rows = lax.broadcasted_iota(jnp.int32, (16, count), 0)
    terms = jnp.zeros((16, count), F32)
    for k in range(3):
        term = rest.astype(BF16).astype(F32)
        terms = jnp.where(rows == k, term, terms)
        rest = rest - term
    block_out[count:, :count] = terms.astype(BF16)


def begin(near, far, p_ref, *refs):
    count = len(near)
    x_refs, weights, caches = refs[:count], refs[count : count + 3], refs[count + 3 : count + 5]
    acc, *outs, held, sems = refs[count + 5 :]
    size, cols = held.shape[1:]
    copies = []

    def send(src, dst):
        copies.append(pltpu.make_async_copy(src, dst, sems.at[len(copies)]))
        copies[-1].start()

    for i, d in enumerate(near + far):
        start = pl.multiple_of((p_ref[0] ^ d) * size, size)
        for j, w_ref in enumerate(weights):
            k = i * 3 + j
            send(
                w_ref.at[pl.ds(start, size)],
                held.at[k] if i < len(near) else outs[k - 3 * len(near)],
            )
    for src, dst in zip(caches, outs[-2:]):
        send(src, dst)
    for i in range(len(near)):
        for j in range(3):
            copies[i * 3 + j].wait()
            product = dot(x_refs[i][...], held[i * 3 + j])
            at = slice(j * cols, (j + 1) * cols)
            acc[:, at] = product if i == 0 else acc[:, at] + product
    for copy in copies[3 * len(near) :]:
        copy.wait()


def project_more(count, p_ref, acc_ref, *refs):
    x_refs, w_refs, out = refs[:count], refs[count:-1], refs[-1]
    cols = w_refs[0].shape[1]
    for j in range(3):
        at = slice(j * cols, (j + 1) * cols)
        total = acc_ref[:, at]
        for i, x_ref in enumerate(x_refs):
            total = total + dot(x_ref[...], w_refs[i * 3 + j][...])
        out[:, at] = total


def attend(count, sources, full_width, p_ref, acc_ref, keys_ref, values_ref, *refs):
    squares_refs, refs = refs[:sources], refs[sources:]
    project_more(count, p_ref, acc_ref, *refs[:-2], refs[-1])
    out, acc = refs[-2:]
    cols = refs[count].shape[1]
    squares = sum(jnp.sum(ref[:8].astype(F32), axis=0, keepdims=True) for ref in squares_refs)
    attend_heads(full_width, cols, squares, keys_ref, values_ref, out, acc)


def attend_heads(full_width, cols, squares, keys_ref, values_ref, out, acc):
    scenes = keys_ref.shape[0]
    branch = acc.shape[0] // scenes
    inverse = column(lax.rsqrt(squares / full_width + EPSILON))
    scaling = HD ** (-0.5)
    for s in range(scenes):
        rows = slice(s * branch, (s + 1) * branch)
        scale = inverse[rows]
        for h in range(cols // HD):
            at = slice(h * HD, (h + 1) * HD)
            q, k, v = (
                (acc[rows, j * cols + h * HD : j * cols + (h + 1) * HD] * scale).astype(BF16)
                for j in range(3)
            )
            scores = (
                lax.dot_general(
                    q,
                    keys_ref[s, :, at],
                    (((1,), (1,)), ((), ())),
                    preferred_element_type=F32,
                )
                * scaling
            )
            own = jnp.sum(q.astype(F32) * k.astype(F32), axis=1, keepdims=True) * scaling
            highest = jnp.maximum(jnp.max(scores, axis=1, keepdims=True), own)
            expd = jnp.exp(scores - highest)
            own_exp = jnp.exp(own - highest)
            total = jnp.sum(expd, axis=1, keepdims=True) + own_exp
            weights = (expd / total).astype(BF16)
            own_weight = (own_exp / total).astype(BF16)
            mixed = dot(weights, values_ref[s, :, at])
            mixed = mixed + own_weight.astype(F32) * v.astype(F32)
            out[rows, at] = mixed.astype(BF16)


def update_near(scenes, p_ref, tokens_ref, *refs):
    x_refs, w_ref, out = refs[:-2], refs[-2], refs[-1]
    for step in range(len(x_refs) // scenes):

        @pl.when(pl.program_id(0) == step)
        def _():
            x = jnp.concatenate(
                [ref[...] for ref in x_refs[step * scenes : (step + 1) * scenes]], axis=0
            )
            out[...] = (tokens_ref if step == 0 else out)[...] + dot(x, w_ref[...])


def update(count, p_ref, acc_ref, gain_ref, policy_ref, value_ref, *refs):
    x_refs, w_ref = refs[:count], refs[count]
    latent_out, keep_out, give_out, squares_out, turned_out, acc = refs[-6:]

    @pl.when(pl.program_id(0) == 0)
    def _():
        acc[...] = acc_ref[...]

    def add(j, product):
        acc[...] += product

    add_products(x_refs, [w_ref], add)

    @pl.when(pl.program_id(0) == count - 1)
    def _():
        state = acc[...]
        latent_out[...] = state.astype(BF16)
        squares = jnp.sum(state * state, axis=1, keepdims=True)
        squares_out[...] = row_of(squares)
        gained = (state * gain_ref[...]).astype(BF16)
        turned_out[...] = jnp.transpose(gained)
        policy = dot(gained, policy_ref[...])
        value = dot(gained, value_ref[...])

        @pl.when(p_ref[0] % 2 == 0)
        def _():
            keep_out[...] = policy
            give_out[...] = value.astype(BF16)

        @pl.when(p_ref[0] % 2 == 1)
        def _():
            keep_out[...] = value
            give_out[...] = policy.astype(BF16)


def heads(full_width, total_rows, p_ref, mine_ref, theirs_ref, squares_ref, policy_out_ref,
          value_out_ref, targets_ref, returns_ref, payload_out, give_out, hidden_ref):
    inverse = column(lax.rsqrt(squares_ref[:1] / full_width + EPSILON))
    pre = (mine_ref[...].astype(F32) + theirs_ref[...].astype(F32)) * inverse
    sigma = jax.nn.sigmoid(pre)
    hidden = (pre * sigma).astype(BF16)
    hidden_ref[...] = hidden
    slope = sigma * (1.0 + pre * (1.0 - sigma)) * inverse
    factor = total_rows ** (-0.5)
    count = hidden.shape[0]
    quarter = give_out.shape[0]
    part = 4 * quarter
    at = slice(count, count + quarter)

    def put_sums(grad, loss):
        shape = (payload_out.shape[0] - count - quarter, hidden.shape[1])
        rows = lax.broadcasted_iota(jnp.int32, shape, 0)
        lanes = lax.broadcasted_iota(jnp.int32, shape, 1)
        sums = jnp.where(rows == 0, grad, 0.0)
        for lane in range(3):
            term = loss.astype(BF16).astype(F32)
            sums = jnp.where((rows == 1) & (lanes == lane), term, sums)
            loss = loss - term
        payload_out[count + quarter :] = sums.astype(BF16)

    @pl.when(p_ref[0] % 2 == 0)
    def _():
        weight = policy_out_ref[...]
        logits = dot(hidden, weight)
        top = jnp.max(logits, axis=1, keepdims=True)
        log_total = top + jnp.log(jnp.sum(jnp.exp(logits - top), axis=1, keepdims=True))
        actions = lax.broadcasted_iota(jnp.int32, logits.shape, 1).astype(F32)
        onehot = (actions == column(targets_ref[...].astype(F32))).astype(F32)
        picked = jnp.sum(logits * onehot, axis=1, keepdims=True)
        loss = jnp.sum(log_total - picked, axis=0, keepdims=True)
        dlogits = ((jnp.exp(logits - log_total) - onehot) * factor).astype(BF16)
        back = lax.dot_general(
            dlogits, weight, (((1,), (1,)), ((), ())), preferred_element_type=F32
        )
        payload_out[:count] = (back * slope).astype(BF16)
        start = pl.multiple_of((p_ref[0] // 2) * part, part)
        grad = lax.dot_general(
            hidden_ref[:, pl.ds(start, part)],
            dlogits,
            (((0,), (0,)), ((), ())),
            preferred_element_type=F32,
        ).astype(BF16)
        parts = [grad[k * quarter : (k + 1) * quarter] for k in range(4)]
        payload_out[at] = jnp.concatenate(parts[:2], axis=1)
        give_out[...] = jnp.concatenate(parts[2:], axis=1)
        put_sums(jnp.zeros((1, hidden.shape[1]), F32), loss)

    @pl.when(p_ref[0] % 2 == 1)
    def _():
        weight = value_out_ref[...].astype(F32)
        hidden_f = hidden.astype(F32)
        value = jnp.sum(hidden_f * weight, axis=1, keepdims=True)
        errors = value - column(returns_ref[...])
        loss = 0.5 * jnp.sum(errors * errors, axis=0, keepdims=True)
        dvalue = (errors * factor).astype(BF16).astype(F32)
        payload_out[:count] = (dvalue * weight * slope).astype(BF16)
        payload_out[at] = jnp.zeros_like(give_out)
        give_out[...] = jnp.zeros_like(give_out)
        put_sums(jnp.sum(dvalue * hidden_f, axis=0, keepdims=True), loss)


def sums(total_rows, p_ref, *refs):
    count = (len(refs) - 3) // 4
    share_out, losses_out, grad_out = refs[-3:]

    def total(d_refs):
        *shards, ahead, back = [ref[...].astype(F32) for ref in d_refs]
        return sum(shards, jnp.concatenate([ahead, back], axis=1))

    own, other, own_sums, other_sums = (
        total(refs[k * count : (k + 1) * count]) for k in range(4)
    )
    first = p_ref[0] % 2 == 0
    quarter = own.shape[0]
    width = share_out.shape[1]
    for k, part in enumerate((jnp.where(first, own, other), jnp.where(first, other, own))):
        for j in range(2):
            at = (2 * k + j) * quarter
            share_out[at : at + quarter] = part[:, j * width : (j + 1) * width].astype(BF16)
    policy = jnp.where(first, own_sums, other_sums)
    value = jnp.where(first, other_sums, own_sums)
    grad_out[...] = value[0].astype(BF16)

    def loss(part):
        lanes = lax.broadcasted_iota(jnp.int32, (1, part.shape[1]), 1)
        return jnp.sum(jnp.where(lanes < 3, part[1:2], 0.0), axis=1, keepdims=True) / total_rows

    lanes = lax.broadcasted_iota(jnp.int32, (1, 2), 1)
    losses_out[...] = jnp.where(lanes == 0, loss(policy), loss(value))


def join(ds, p_ref, *refs):
    out = refs[-1]
    size = refs[0].shape[0]
    for d, ref in zip(ds, refs[:-1]):
        out[pl.ds(pl.multiple_of(((p_ref[0] ^ d) // 2) * size, size), size)] = ref[...]


def factors(turned_refs, own_refs, other_refs, halved):
    turned = jnp.concatenate([ref[...] for ref in turned_refs], axis=1)
    for d_refs in (own_refs, other_refs):
        shards = [ref[...] for ref in d_refs]
        if halved:
            shards[-2:] = [jnp.concatenate(shards[-2:], axis=1)]
        yield dot(turned, jnp.concatenate(shards, axis=0))


def gradients_start(turned_count, count, p_ref, *refs):
    turned, own, other = refs[:turned_count], refs[turned_count:][:count], refs[turned_count + count : -2]
    for out, product in zip(refs[-2:], factors(turned, own, other, False)):
        out[...] = product


def gradients_end(turned_count, count, p_ref, *refs):
    sums, refs, outs = refs[:2], refs[2:-2], refs[-2:]
    turned, own, other = refs[:turned_count], refs[turned_count:][:count], refs[turned_count + count :]
    own, other = (
        (acc[...] + product).astype(BF16)
        for acc, product in zip(sums, factors(turned, own, other, True))
    )

    @pl.when(p_ref[0] % 2 == 0)
    def _():
        outs[0][...] = own
        outs[1][...] = other

    @pl.when(p_ref[0] % 2 == 1)
    def _():
        outs[1][...] = own
        outs[0][...] = other


def call(body, name, place, steps, operands, in_specs, outs, out_specs, flops, limit, scratch=(), aliases=None):
    bytes_accessed = sum(x.size * x.dtype.itemsize for x in (*operands, *outs)) if flops else 0
    return pl.pallas_call(
        body,
        name=name,
        out_shape=outs,
        input_output_aliases=aliases or {},
        grid_spec=pltpu.PrefetchScalarGridSpec(
            num_scalar_prefetch=1,
            grid=(steps,),
            in_specs=in_specs,
            out_specs=out_specs,
            scratch_shapes=scratch,
        ),
        compiler_params=pltpu.CompilerParams(
            dimension_semantics=("arbitrary",), vmem_limit_bytes=limit
        ),
        cost_estimate=pl.CostEstimate(
            flops=flops, bytes_accessed=bytes_accessed, transcendentals=0
        ),
    )(place, *operands)


def per_device(
    latent,
    actions,
    action_table,
    norm1_gain,
    w_query,
    w_key,
    w_value,
    w_out,
    key_cache,
    value_cache,
    norm2_gain,
    policy_in,
    value_in,
    policy_out,
    value_out,
    targets,
    returns,
):
    rows, width = latent.shape
    narrow_size = lax.axis_size("narrow")
    wide_size = lax.axis_size("wide")
    full_width = width * narrow_size
    cols = w_query.shape[1]
    total_rows = rows * wide_size
    action_count = action_table.shape[0]
    hidden_count = policy_in.shape[1]
    index = lax.axis_index("narrow").astype(jnp.int32)
    place = index[None]
    first = index % 2 == 0
    chips = narrow_size // 2
    near = [0, 1]
    direct = list(range(2, narrow_size, 2))
    passed = [d + 1 for d in direct]

    far = direct + passed
    scenes = key_cache.shape[0]
    branch = rows // scenes
    hbm = functools.partial(pltpu.with_memory_space_constraint, memory_space=pltpu.HBM)

    block_shape = (rows + 16, width)
    tokens, block = call(
        embed, "embed", place, 1,
        [
            hbm(latent), hbm(actions[None, :]), hbm(action_table),
            hbm(norm1_gain[None, :]),
        ],
        [
            whole((rows, width)), whole((1, rows)), whole(action_table.shape),
            whole((1, width)),
        ],
        [
            jax.ShapeDtypeStruct((rows, width), F32),
            jax.ShapeDtypeStruct(block_shape, BF16),
        ],
        [whole((rows, width)), whole(block_shape)],
        2 * rows * width * action_count, 16 * MIB,
    )
    blocks = {**far_blocks(block), 1: swap(block, 1)}

    weights = [hbm(w) for w in (w_query, w_key, w_value)]
    x_spec = whole((rows, width))
    acc_shape = jax.ShapeDtypeStruct((rows, 3 * cols), F32)
    weight_shape = jax.ShapeDtypeStruct((width, cols), BF16)
    weight_block = whole((width, cols))
    cache_shape = jax.ShapeDtypeStruct(key_cache.shape, BF16)
    outs = [weight_shape] * (3 * len(far)) + [cache_shape] * 2
    anywhere = pl.BlockSpec(memory_space=pl.ANY)
    flops = 2 * rows * width * 3 * cols
    acc, *staged, keys, values = call(
        functools.partial(begin, near, far), "begin", place, 1,
        [
            *(blocks[d] for d in near), *weights,
            hbm(key_cache), hbm(value_cache),
        ],
        [*[x_spec] * len(near), *[anywhere] * 5],
        [acc_shape, *outs], [whole(acc_shape.shape), *[anywhere] * len(outs)],
        flops * len(near), 20 * MIB,
        [
            pltpu.VMEM((3 * len(near), width, cols), BF16),
            pltpu.SemaphoreType.DMA((3 * len(near) + len(outs),)),
        ],
    )
    staged_direct = staged[: 3 * len(direct)]
    staged_passed = staged[3 * len(direct) :]

    acc_spec = whole(acc_shape.shape)
    blocks = pass_blocks(blocks, acc)
    acc = call(
        functools.partial(project_more, len(direct)), "project", place, 1,
        [acc, *(blocks[d] for d in direct), *staged_direct],
        [acc_spec, *[x_spec] * len(direct), *[weight_block] * len(staged_direct)],
        [acc_shape], [acc_spec], flops * len(direct), 24 * MIB,
    )[0]

    attended = []
    for s in range(scenes):
        at = functools.partial(lambda s, i, p: (s, 0), s)
        squares_spec = pl.BlockSpec(
            (16, branch), functools.partial(lambda s, i, p: (rows // 16, s), s)
        )
        cache_spec = pl.BlockSpec(
            (1, *key_cache.shape[1:]), functools.partial(lambda s, i, p: (s, 0, 0), s)
        )
        one = call(
            functools.partial(attend, len(passed), narrow_size, full_width), f"attend{s}", place, 1,
            [
                acc, keys, values, *blocks.values(),
                *(blocks[d] for d in passed), *staged_passed,
            ],
            [
                pl.BlockSpec((branch, 3 * cols), at), cache_spec, cache_spec,
                *[squares_spec] * narrow_size,
                *[pl.BlockSpec((branch, width), at)] * len(passed), *[weight_block] * len(staged_passed),
            ],
            [jax.ShapeDtypeStruct((branch, cols), BF16)], [whole((branch, cols))],
            0, 20 * MIB, [pltpu.VMEM((branch, 3 * cols), F32)],
        )[0]
        attended.append({**far_blocks(one), 1: swap(one, 1)})

    half = (rows, hidden_count)
    full_shapes = [
        jax.ShapeDtypeStruct((rows, width), BF16),
        jax.ShapeDtypeStruct(half, F32),
        jax.ShapeDtypeStruct(half, BF16),
        jax.ShapeDtypeStruct((8, rows), F32),
    ]
    chunk = whole((branch, cols))
    acc = call(
        functools.partial(update_near, scenes), "update_near", place, len(near),
        [tokens, *(one[d] for d in near for one in attended), w_out],
        [
            whole((rows, width)), *[chunk] * (scenes * len(near)),
            weight_spec(near, cols, width),
        ],
        [jax.ShapeDtypeStruct((rows, width), F32)], [whole((rows, width))],
        2 * rows * width * cols * len(near), 16 * MIB,
    )[0]
    filled, turned, shards = [], [], []
    ring = Ring()
    for s in range(scenes):
        ds = far
        around = pass_blocks(attended[s], *turned)
        at = functools.partial(lambda s, i, p: (s, 0), s)
        operands = [
            acc, norm2_gain[None, :], policy_in, value_in,
            *(around[d] for d in ds), w_out, *filled,
        ]
        *filled, one = call(
            functools.partial(update, len(ds)), f"update{s}", place, len(ds), operands,
            [
                pl.BlockSpec((branch, width), at),
                whole((1, width)), whole(policy_in.shape), whole(value_in.shape),
                *[chunk] * len(ds), weight_spec(ds, cols, width),
                *[anywhere] * len(filled),
            ],
            [*full_shapes, jax.ShapeDtypeStruct((width, branch), BF16)],
            [
                pl.BlockSpec((branch, width), at),
                pl.BlockSpec((branch, hidden_count), at),
                pl.BlockSpec((branch, hidden_count), at),
                pl.BlockSpec((8, branch), functools.partial(lambda s, i, p: (0, s), s)),
                whole((width, branch)),
            ],
            2 * branch * width * (cols * len(ds) + 2 * hidden_count), 28 * MIB,
            [pltpu.VMEM((branch, width), F32)],
            {1 + len(operands) - len(filled) + k: k for k in range(len(filled))},
        )
        turned.append(one)
        if s == 0:
            shards.append([ring.step("s0t1", one, one)])
    new_latent, keep, give, squares = filled

    for bit in (1, *far_bits()):
        squares = squares + swap(squares, bit)
    shards += [[ring.step(f"s{k + 1}t1", one, one)] for k, one in enumerate(turned[1:])]
    pre = keep + swap(after(give, *ring.arrived(HOLDS["give"])), 1).astype(F32)
    mine = pre.astype(BF16)
    *upper, last = far_bits()
    for bit in upper:
        mine = (mine.astype(F32) + swap(mine, bit).astype(F32)).astype(BF16)
    rounds = wide_size // 2
    for step in range(2, rounds):
        for k, shard in enumerate(shards):
            if f"s{k}t{step}" in EARLY:
                shard.append(ring.step(f"s{k}t{step}", *shard[-1]))
    theirs = after(swap(mine, last), *ring.arrived(HOLDS["heads"]))
    quarter = hidden_count // chips // 4
    payload_shape = (rows + quarter + 16, hidden_count)
    payload, give = call(
        functools.partial(heads, full_width, total_rows), "heads", place, 1,
        [
            mine, theirs, squares, policy_out, value_out[None, :], targets[None, :],
            returns[None, :],
        ],
        [
            whole(half), whole(half), whole((8, rows)), whole(policy_out.shape),
            whole((1, hidden_count)), whole((1, rows)), whole((1, rows)),
        ],
        [
            jax.ShapeDtypeStruct(payload_shape, BF16),
            jax.ShapeDtypeStruct((quarter, hidden_count), BF16),
        ],
        [whole(payload_shape), whole((quarter, hidden_count))],
        6 * rows * hidden_count * action_count, 16 * MIB, [pltpu.VMEM(half, BF16)],
    )
    taken = jnp.where(first, payload[rows : rows + quarter], swap(after(give, *ring.arrived(HOLDS["share"])), 1))
    payload = lax.dynamic_update_slice(payload, taken, (rows, 0))

    payload_rounds = [[payload, payload]]
    cut, size = scenes // 2, hidden_count // 2
    for step in range(1, rounds + 1):
        up, down = payload_rounds[-1]
        if step == rounds:
            up, down = up[:, :size], down[:, size:]
        payload_rounds.append(ring.step(f"p{step}", up, down))
        for k, shard in enumerate(shards):
            if len(shard) == step and step < rounds - 1:
                shard.append(ring.step(f"s{k}t{step + 1}", *shard[-1]))
        if step == rounds - 1:
            for k, (one, other) in enumerate(zip(shards[:cut], shards[cut:])):
                up, down = ring.step(f"s{k}t{rounds}", one[-1][0], other[-1][1])
                one.append([up])
                other.append([down])
    turned_all = list(turned)
    for step in range(rounds):
        for way in range(len(shards[0][step])):
            turned_all += [shard[step][way] for shard in shards]
    payload_own = [payload, *(b for pair in payload_rounds[1:] for b in pair)]
    split = wide_size - 3
    payload_other = [swap(b, 1) for b in payload_own[:split]]

    block = 256
    grad_spec = pl.BlockSpec((block, hidden_count), lambda i, p: (i, 0))
    grad_flops = 4 * rows * width * hidden_count

    def gradient(body, name, operands, specs, count, turned, own, other, dtype):
        return call(
            functools.partial(body, len(turned), len(own)), name, place, width // block,
            [*operands, *turned, *own, *other],
            [
                *specs,
                *[pl.BlockSpec((block, branch), lambda i, p: (i, 0))] * len(turned),
                *[
                    pl.BlockSpec(
                        (rows, b.shape[1]), lambda i, p: (0, 0), pipeline_mode=pl.Buffered(1)
                    )
                    for b in (*own, *other)
                ],
            ],
            [jax.ShapeDtypeStruct((width, hidden_count), dtype)] * 2, [grad_spec] * 2,
            grad_flops * count, 18 * MIB,
        )

    starts = gradient(
        gradients_start, "gradients_start", [], [], 0, turned_all[: scenes * split],
        payload_own[:split], payload_other[:split], F32,
    )
    payload_other += [swap(b, 1) for b in payload_own[split:-2]]
    payload_other += [swap(after(b, *starts), 1) for b in payload_own[-2:]]

    pieces = [*payload_own, *payload_other]
    share_shape = (4 * quarter, action_count)
    share, losses, value_out_grad = call(
        functools.partial(sums, total_rows), "sums", place, 1, [*pieces, *pieces],
        [
            pl.BlockSpec((count, b.shape[1]), functools.partial(lambda at, i, p: (at, 0), start // count))
            for start, count in ((rows, quarter), (rows + quarter, 16))
            for b in pieces
        ],
        [
            jax.ShapeDtypeStruct(share_shape, BF16),
            jax.ShapeDtypeStruct((1, 2), F32),
            jax.ShapeDtypeStruct((hidden_count,), BF16),
        ],
        [whole(share_shape), whole((1, 2)), whole((hidden_count,))], 0, 8 * MIB,
    )
    losses = losses.reshape(2)
    shares = far_blocks(share)
    policy_out_grad = call(
        functools.partial(join, list(shares)), "join", place, 1, list(shares.values()),
        [whole(share_shape)] * len(shares),
        [jax.ShapeDtypeStruct((hidden_count, action_count), BF16)],
        [whole((hidden_count, action_count))], 0, 8 * MIB,
    )[0]

    policy_in_grad, value_in_grad = gradient(
        gradients_end, "gradients_end", starts, [grad_spec] * 2, wide_size - split,
        turned_all[scenes * split :], payload_own[split:], payload_other[split:], BF16,
    )
    return (new_latent, losses, policy_in_grad, value_in_grad, policy_out_grad, value_out_grad)


def solution(mesh):
    placed = (
        P("wide", "narrow"),
        P("wide"),
        P(None, "narrow"),
        P("narrow"),
        P(None, "narrow"),
        P(None, "narrow"),
        P(None, "narrow"),
        P(None, "narrow"),
        P("wide", None, "narrow"),
        P("wide", None, "narrow"),
        P("narrow"),
        P("narrow", None),
        P("narrow", None),
        P(),
        P(),
        P("wide"),
        P("wide"),
    )
    return jax.shard_map(
        per_device,
        mesh=mesh,
        in_specs=placed,
        out_specs=(P("wide", "narrow"), P(), P("narrow", None), P("narrow", None), P(), P()),
        check_vma=False,
    )
```

```python
import functools

import jax
import jax.numpy as jnp
from jax import lax
from jax.experimental import pallas as pl
from jax.experimental.pallas import tpu as pltpu
from jax.sharding import PartitionSpec as P

HD = 128
EPSILON = 1e-05
F32 = jnp.float32
BF16 = jnp.bfloat16
MIB = 1 << 20
HOLDS = {
    "give": ("s0t1",),
    "heads": ("s0t2", "s1t1", "s1t2"),
    "share": ("s1t2",),
    "s0t3": ("s1t2",),
    "s1t3": ("s0t3",),
    "s0t4": ("s1t3",),
    "p4": ("s1t3",),
}
EARLY = ("s0t2", "s1t2", "s0t3")


def swap(block, bit):
    size = lax.axis_size("narrow")
    return lax.ppermute(block, "narrow", [(n, n ^ bit) for n in range(size)])


def far_bits():
    bit = lax.axis_size("narrow") // 2
    while bit > 1:
        yield bit
        bit //= 2


def far_blocks(block):
    blocks = {0: block}
    for bit in far_bits():
        blocks.update({d ^ bit: swap(b, bit) for d, b in list(blocks.items())})
    return blocks


def pass_blocks(blocks, *earlier):
    far = {d ^ 1: swap(after(b, *earlier), 1) for d, b in blocks.items() if d > 1}
    return {**blocks, **far}


def after(block, *earlier):
    return lax.optimization_barrier((block, *earlier))[0]


def ring_order(size):
    return list(range(0, size, 2)) + list(range(size - 1, 0, -2))


def ring_step(block, way):
    order = ring_order(lax.axis_size("wide"))
    pairs = [(a, order[(i + way) % len(order)]) for i, a in enumerate(order)]
    return lax.ppermute(block, "wide", pairs)


class Ring:
    def __init__(self):
        self.at = {}

    def arrived(self, names):
        return [b for name in names for b in self.at.get(name, ())]

    def step(self, name, up, down):
        held = HOLDS.get(name, ())
        up, down = after(up, *self.arrived(held)), after(down, *self.arrived(held))
        self.at[name] = [ring_step(up, 1), ring_step(down, -1)]
        return self.at[name]


def dot(a, b):
    return jnp.dot(a, b, preferred_element_type=F32)


def column(row):
    return jnp.transpose(jnp.broadcast_to(row, (128, row.shape[1])))[:, :1]


def whole(shape):
    return pl.BlockSpec(shape, lambda i, p: (0,) * len(shape))


def weight_spec(ds, rows, columns):
    def at(i, p):
        d = jnp.int32(ds[0])
        for j in range(1, len(ds)):
            d = jnp.where(i == j, ds[j], d)
        return (p[0] ^ d, 0)

    return pl.BlockSpec((rows, columns), at)


def add_products(x_refs, w_refs, add):
    for step, x_ref in enumerate(x_refs):

        @pl.when(pl.program_id(0) == step)
        def _():
            for j, w_ref in enumerate(w_refs):
                add(j, dot(x_ref[...], w_ref[...]))


def row_of(values):
    return jnp.transpose(jnp.broadcast_to(values, (values.shape[0], 128)))[:8]


def embed(p_ref, latent_ref, actions_ref, table_ref, gain_ref, tokens_out, block_out):
    shape = (table_ref.shape[0], latent_ref.shape[0])
    onehot = (lax.broadcasted_iota(jnp.int32, shape, 0) == actions_ref[...]).astype(BF16)
    picked = lax.dot_general(
        onehot, table_ref[...], (((0,), (0,)), ((), ())), preferred_element_type=F32
    )
    tokens = latent_ref[...].astype(F32) + picked
    tokens_out[...] = tokens
    count = latent_ref.shape[0]
    block_out[:count] = (tokens * gain_ref[...]).astype(BF16)
    block_out[count:] = jnp.zeros_like(block_out[count:])
    rest = row_of(jnp.sum(tokens * tokens, axis=1, keepdims=True))[:1]
    rows = lax.broadcasted_iota(jnp.int32, (16, count), 0)
    terms = jnp.zeros((16, count), F32)
    for k in range(3):
        term = rest.astype(BF16).astype(F32)
        terms = jnp.where(rows == k, term, terms)
        rest = rest - term
    block_out[count:, :count] = terms.astype(BF16)


def begin(near, far, p_ref, *refs):
    count = len(near)
    x_refs, weights, caches = refs[:count], refs[count : count + 3], refs[count + 3 : count + 5]
    acc, *outs, held, sems = refs[count + 5 :]
    size, cols = held.shape[1:]
    copies = []

    def send(src, dst):
        copies.append(pltpu.make_async_copy(src, dst, sems.at[len(copies)]))
        copies[-1].start()

    for i, d in enumerate(near + far):
        start = pl.multiple_of((p_ref[0] ^ d) * size, size)
        for j, w_ref in enumerate(weights):
            k = i * 3 + j
            send(
                w_ref.at[pl.ds(start, size)],
                held.at[k] if i < len(near) else outs[k - 3 * len(near)],
            )
    for src, dst in zip(caches, outs[-2:]):
        send(src, dst)
    for i in range(len(near)):
        for j in range(3):
            copies[i * 3 + j].wait()
            product = dot(x_refs[i][...], held[i * 3 + j])
            at = slice(j * cols, (j + 1) * cols)
            acc[:, at] = product if i == 0 else acc[:, at] + product
    for copy in copies[3 * len(near) :]:
        copy.wait()


def project_more(count, p_ref, acc_ref, *refs):
    x_refs, w_refs, out = refs[:count], refs[count:-1], refs[-1]
    cols = w_refs[0].shape[1]
    for j in range(3):
        at = slice(j * cols, (j + 1) * cols)
        total = acc_ref[:, at]
        for i, x_ref in enumerate(x_refs):
            total = total + dot(x_ref[...], w_refs[i * 3 + j][...])
        out[:, at] = total


def attend(count, sources, full_width, p_ref, acc_ref, keys_ref, values_ref, *refs):
    squares_refs, refs = refs[:sources], refs[sources:]
    project_more(count, p_ref, acc_ref, *refs[:-2], refs[-1])
    out, acc = refs[-2:]
    cols = refs[count].shape[1]
    squares = sum(jnp.sum(ref[:8].astype(F32), axis=0, keepdims=True) for ref in squares_refs)
    attend_heads(full_width, cols, squares, keys_ref, values_ref, out, acc)


def attend_heads(full_width, cols, squares, keys_ref, values_ref, out, acc):
    scenes = keys_ref.shape[0]
    branch = acc.shape[0] // scenes
    inverse = column(lax.rsqrt(squares / full_width + EPSILON))
    scaling = HD ** (-0.5)
    for s in range(scenes):
        rows = slice(s * branch, (s + 1) * branch)
        scale = inverse[rows]
        for h in range(cols // HD):
            at = slice(h * HD, (h + 1) * HD)
            q, k, v = (
                (acc[rows, j * cols + h * HD : j * cols + (h + 1) * HD] * scale).astype(BF16)
                for j in range(3)
            )
            scores = (
                lax.dot_general(
                    q,
                    keys_ref[s, :, at],
                    (((1,), (1,)), ((), ())),
                    preferred_element_type=F32,
                )
                * scaling
            )
            own = jnp.sum(q.astype(F32) * k.astype(F32), axis=1, keepdims=True) * scaling
            highest = jnp.maximum(jnp.max(scores, axis=1, keepdims=True), own)
            expd = jnp.exp(scores - highest)
            own_exp = jnp.exp(own - highest)
            total = jnp.sum(expd, axis=1, keepdims=True) + own_exp
            weights = (expd / total).astype(BF16)
            own_weight = (own_exp / total).astype(BF16)
            mixed = dot(weights, values_ref[s, :, at])
            mixed = mixed + own_weight.astype(F32) * v.astype(F32)
            out[rows, at] = mixed.astype(BF16)


def update_near(scenes, p_ref, tokens_ref, *refs):
    x_refs, w_ref, out = refs[:-2], refs[-2], refs[-1]
    for step in range(len(x_refs) // scenes):

        @pl.when(pl.program_id(0) == step)
        def _():
            x = jnp.concatenate(
                [ref[...] for ref in x_refs[step * scenes : (step + 1) * scenes]], axis=0
            )
            out[...] = (tokens_ref if step == 0 else out)[...] + dot(x, w_ref[...])


def update(count, p_ref, acc_ref, gain_ref, policy_ref, value_ref, *refs):
    x_refs, w_ref = refs[:count], refs[count]
    latent_out, keep_out, give_out, squares_out, turned_out, acc = refs[-6:]

    @pl.when(pl.program_id(0) == 0)
    def _():
        acc[...] = acc_ref[...]

    def add(j, product):
        acc[...] += product

    add_products(x_refs, [w_ref], add)

    @pl.when(pl.program_id(0) == count - 1)
    def _():
        state = acc[...]
        latent_out[...] = state.astype(BF16)
        squares = jnp.sum(state * state, axis=1, keepdims=True)
        squares_out[...] = row_of(squares)
        gained = (state * gain_ref[...]).astype(BF16)
        turned_out[...] = jnp.transpose(gained)
        policy = dot(gained, policy_ref[...])
        value = dot(gained, value_ref[...])

        @pl.when(p_ref[0] % 2 == 0)
        def _():
            keep_out[...] = policy
            give_out[...] = value.astype(BF16)

        @pl.when(p_ref[0] % 2 == 1)
        def _():
            keep_out[...] = value
            give_out[...] = policy.astype(BF16)


def heads(full_width, total_rows, p_ref, mine_ref, theirs_ref, squares_ref, policy_out_ref,
          value_out_ref, targets_ref, returns_ref, payload_out, give_out, hidden_ref):
    inverse = column(lax.rsqrt(squares_ref[:1] / full_width + EPSILON))
    pre = (mine_ref[...].astype(F32) + theirs_ref[...].astype(F32)) * inverse
    sigma = jax.nn.sigmoid(pre)
    hidden = (pre * sigma).astype(BF16)
    hidden_ref[...] = hidden
    slope = sigma * (1.0 + pre * (1.0 - sigma)) * inverse
    factor = total_rows ** (-0.5)
    count = hidden.shape[0]
    quarter = give_out.shape[0]
    part = 4 * quarter
    at = slice(count, count + quarter)

    def put_sums(grad, loss):
        shape = (payload_out.shape[0] - count - quarter, hidden.shape[1])
        rows = lax.broadcasted_iota(jnp.int32, shape, 0)
        lanes = lax.broadcasted_iota(jnp.int32, shape, 1)
        sums = jnp.where(rows == 0, grad, 0.0)
        for lane in range(3):
            term = loss.astype(BF16).astype(F32)
            sums = jnp.where((rows == 1) & (lanes == lane), term, sums)
            loss = loss - term
        payload_out[count + quarter :] = sums.astype(BF16)

    @pl.when(p_ref[0] % 2 == 0)
    def _():
        weight = policy_out_ref[...]
        logits = dot(hidden, weight)
        top = jnp.max(logits, axis=1, keepdims=True)
        log_total = top + jnp.log(jnp.sum(jnp.exp(logits - top), axis=1, keepdims=True))
        actions = lax.broadcasted_iota(jnp.int32, logits.shape, 1).astype(F32)
        onehot = (actions == column(targets_ref[...].astype(F32))).astype(F32)
        picked = jnp.sum(logits * onehot, axis=1, keepdims=True)
        loss = jnp.sum(log_total - picked, axis=0, keepdims=True)
        dlogits = ((jnp.exp(logits - log_total) - onehot) * factor).astype(BF16)
        back = lax.dot_general(
            dlogits, weight, (((1,), (1,)), ((), ())), preferred_element_type=F32
        )
        payload_out[:count] = (back * slope).astype(BF16)
        start = pl.multiple_of((p_ref[0] // 2) * part, part)
        grad = lax.dot_general(
            hidden_ref[:, pl.ds(start, part)],
            dlogits,
            (((0,), (0,)), ((), ())),
            preferred_element_type=F32,
        ).astype(BF16)
        parts = [grad[k * quarter : (k + 1) * quarter] for k in range(4)]
        payload_out[at] = jnp.concatenate(parts[:2], axis=1)
        give_out[...] = jnp.concatenate(parts[2:], axis=1)
        put_sums(jnp.zeros((1, hidden.shape[1]), F32), loss)

    @pl.when(p_ref[0] % 2 == 1)
    def _():
        weight = value_out_ref[...].astype(F32)
        hidden_f = hidden.astype(F32)
        value = jnp.sum(hidden_f * weight, axis=1, keepdims=True)
        errors = value - column(returns_ref[...])
        loss = 0.5 * jnp.sum(errors * errors, axis=0, keepdims=True)
        dvalue = (errors * factor).astype(BF16).astype(F32)
        payload_out[:count] = (dvalue * weight * slope).astype(BF16)
        payload_out[at] = jnp.zeros_like(give_out)
        give_out[...] = jnp.zeros_like(give_out)
        put_sums(jnp.sum(dvalue * hidden_f, axis=0, keepdims=True), loss)


def sums(total_rows, p_ref, *refs):
    count = (len(refs) - 3) // 4
    share_out, losses_out, grad_out = refs[-3:]

    def total(d_refs):
        *shards, ahead, back = [ref[...].astype(F32) for ref in d_refs]
        return sum(shards, jnp.concatenate([ahead, back], axis=1))

    own, other, own_sums, other_sums = (
        total(refs[k * count : (k + 1) * count]) for k in range(4)
    )
    first = p_ref[0] % 2 == 0
    quarter = own.shape[0]
    width = share_out.shape[1]
    for k, part in enumerate((jnp.where(first, own, other), jnp.where(first, other, own))):
        for j in range(2):
            at = (2 * k + j) * quarter
            share_out[at : at + quarter] = part[:, j * width : (j + 1) * width].astype(BF16)
    policy = jnp.where(first, own_sums, other_sums)
    value = jnp.where(first, other_sums, own_sums)
    grad_out[...] = value[0].astype(BF16)

    def loss(part):
        lanes = lax.broadcasted_iota(jnp.int32, (1, part.shape[1]), 1)
        return jnp.sum(jnp.where(lanes < 3, part[1:2], 0.0), axis=1, keepdims=True) / total_rows

    lanes = lax.broadcasted_iota(jnp.int32, (1, 2), 1)
    losses_out[...] = jnp.where(lanes == 0, loss(policy), loss(value))


def join(ds, p_ref, *refs):
    out = refs[-1]
    size = refs[0].shape[0]
    for d, ref in zip(ds, refs[:-1]):
        out[pl.ds(pl.multiple_of(((p_ref[0] ^ d) // 2) * size, size), size)] = ref[...]


def factors(turned_refs, own_refs, other_refs, halved):
    turned = jnp.concatenate([ref[...] for ref in turned_refs], axis=1)
    for d_refs in (own_refs, other_refs):
        shards = [ref[...] for ref in d_refs]
        if halved:
            shards[-2:] = [jnp.concatenate(shards[-2:], axis=1)]
        yield dot(turned, jnp.concatenate(shards, axis=0))


def gradients_start(turned_count, count, p_ref, *refs):
    turned, own, other = refs[:turned_count], refs[turned_count:][:count], refs[turned_count + count : -2]
    for out, product in zip(refs[-2:], factors(turned, own, other, False)):
        out[...] = product


def gradients_end(turned_count, count, p_ref, *refs):
    sums, refs, outs = refs[:2], refs[2:-2], refs[-2:]
    turned, own, other = refs[:turned_count], refs[turned_count:][:count], refs[turned_count + count :]
    own, other = (
        (acc[...] + product).astype(BF16)
        for acc, product in zip(sums, factors(turned, own, other, True))
    )

    @pl.when(p_ref[0] % 2 == 0)
    def _():
        outs[0][...] = own
        outs[1][...] = other

    @pl.when(p_ref[0] % 2 == 1)
    def _():
        outs[1][...] = own
        outs[0][...] = other


def call(body, name, place, steps, operands, in_specs, outs, out_specs, flops, limit, scratch=(), aliases=None):
    bytes_accessed = sum(x.size * x.dtype.itemsize for x in (*operands, *outs)) if flops else 0
    return pl.pallas_call(
        body,
        name=name,
        out_shape=outs,
        input_output_aliases=aliases or {},
        grid_spec=pltpu.PrefetchScalarGridSpec(
            num_scalar_prefetch=1,
            grid=(steps,),
            in_specs=in_specs,
            out_specs=out_specs,
            scratch_shapes=scratch,
        ),
        compiler_params=pltpu.CompilerParams(
            dimension_semantics=("arbitrary",), vmem_limit_bytes=limit
        ),
        cost_estimate=pl.CostEstimate(
            flops=flops, bytes_accessed=bytes_accessed, transcendentals=0
        ),
    )(place, *operands)


def per_device(
    latent,
    actions,
    action_table,
    norm1_gain,
    w_query,
    w_key,
    w_value,
    w_out,
    key_cache,
    value_cache,
    norm2_gain,
    policy_in,
    value_in,
    policy_out,
    value_out,
    targets,
    returns,
):
    rows, width = latent.shape
    narrow_size = lax.axis_size("narrow")
    wide_size = lax.axis_size("wide")
    full_width = width * narrow_size
    cols = w_query.shape[1]
    total_rows = rows * wide_size
    action_count = action_table.shape[0]
    hidden_count = policy_in.shape[1]
    index = lax.axis_index("narrow").astype(jnp.int32)
    place = index[None]
    first = index % 2 == 0
    chips = narrow_size // 2
    near = [0, 1]
    direct = list(range(2, narrow_size, 2))
    passed = [d + 1 for d in direct]

    far = direct + passed
    scenes = key_cache.shape[0]
    branch = rows // scenes
    hbm = functools.partial(pltpu.with_memory_space_constraint, memory_space=pltpu.HBM)

    block_shape = (rows + 16, width)
    tokens, block = call(
        embed, "embed", place, 1,
        [
            hbm(latent), hbm(actions[None, :]), hbm(action_table),
            hbm(norm1_gain[None, :]),
        ],
        [
            whole((rows, width)), whole((1, rows)), whole(action_table.shape),
            whole((1, width)),
        ],
        [
            jax.ShapeDtypeStruct((rows, width), F32),
            jax.ShapeDtypeStruct(block_shape, BF16),
        ],
        [whole((rows, width)), whole(block_shape)],
        2 * rows * width * action_count, 16 * MIB,
    )
    blocks = {**far_blocks(block), 1: swap(block, 1)}

    weights = [hbm(w) for w in (w_query, w_key, w_value)]
    x_spec = whole((rows, width))
    acc_shape = jax.ShapeDtypeStruct((rows, 3 * cols), F32)
    weight_shape = jax.ShapeDtypeStruct((width, cols), BF16)
    weight_block = whole((width, cols))
    cache_shape = jax.ShapeDtypeStruct(key_cache.shape, BF16)
    outs = [weight_shape] * (3 * len(far)) + [cache_shape] * 2
    anywhere = pl.BlockSpec(memory_space=pl.ANY)
    flops = 2 * rows * width * 3 * cols
    acc, *staged, keys, values = call(
        functools.partial(begin, near, far), "begin", place, 1,
        [
            *(blocks[d] for d in near), *weights,
            hbm(key_cache), hbm(value_cache),
        ],
        [*[x_spec] * len(near), *[anywhere] * 5],
        [acc_shape, *outs], [whole(acc_shape.shape), *[anywhere] * len(outs)],
        flops * len(near), 20 * MIB,
        [
            pltpu.VMEM((3 * len(near), width, cols), BF16),
            pltpu.SemaphoreType.DMA((3 * len(near) + len(outs),)),
        ],
    )
    staged_direct = staged[: 3 * len(direct)]
    staged_passed = staged[3 * len(direct) :]

    acc_spec = whole(acc_shape.shape)
    blocks = pass_blocks(blocks, acc)
    acc = call(
        functools.partial(project_more, len(direct)), "project", place, 1,
        [acc, *(blocks[d] for d in direct), *staged_direct],
        [acc_spec, *[x_spec] * len(direct), *[weight_block] * len(staged_direct)],
        [acc_shape], [acc_spec], flops * len(direct), 24 * MIB,
    )[0]

    attended = []
    for s in range(scenes):
        at = functools.partial(lambda s, i, p: (s, 0), s)
        squares_spec = pl.BlockSpec(
            (16, branch), functools.partial(lambda s, i, p: (rows // 16, s), s)
        )
        cache_spec = pl.BlockSpec(
            (1, *key_cache.shape[1:]), functools.partial(lambda s, i, p: (s, 0, 0), s)
        )
        one = call(
            functools.partial(attend, len(passed), narrow_size, full_width), f"attend{s}", place, 1,
            [
                acc, keys, values, *blocks.values(),
                *(blocks[d] for d in passed), *staged_passed,
            ],
            [
                pl.BlockSpec((branch, 3 * cols), at), cache_spec, cache_spec,
                *[squares_spec] * narrow_size,
                *[pl.BlockSpec((branch, width), at)] * len(passed), *[weight_block] * len(staged_passed),
            ],
            [jax.ShapeDtypeStruct((branch, cols), BF16)], [whole((branch, cols))],
            0, 20 * MIB, [pltpu.VMEM((branch, 3 * cols), F32)],
        )[0]
        attended.append({**far_blocks(one), 1: swap(one, 1)})

    half = (rows, hidden_count)
    full_shapes = [
        jax.ShapeDtypeStruct((rows, width), BF16),
        jax.ShapeDtypeStruct(half, F32),
        jax.ShapeDtypeStruct(half, BF16),
        jax.ShapeDtypeStruct((8, rows), F32),
    ]
    chunk = whole((branch, cols))
    acc = call(
        functools.partial(update_near, scenes), "update_near", place, len(near),
        [tokens, *(one[d] for d in near for one in attended), w_out],
        [
            whole((rows, width)), *[chunk] * (scenes * len(near)),
            weight_spec(near, cols, width),
        ],
        [jax.ShapeDtypeStruct((rows, width), F32)], [whole((rows, width))],
        2 * rows * width * cols * len(near), 16 * MIB,
    )[0]
    filled, turned, shards = [], [], []
    ring = Ring()
    for s in range(scenes):
        ds = far
        around = pass_blocks(attended[s], *turned)
        at = functools.partial(lambda s, i, p: (s, 0), s)
        operands = [
            acc, norm2_gain[None, :], policy_in, value_in,
            *(around[d] for d in ds), w_out, *filled,
        ]
        *filled, one = call(
            functools.partial(update, len(ds)), f"update{s}", place, len(ds), operands,
            [
                pl.BlockSpec((branch, width), at),
                whole((1, width)), whole(policy_in.shape), whole(value_in.shape),
                *[chunk] * len(ds), weight_spec(ds, cols, width),
                *[anywhere] * len(filled),
            ],
            [*full_shapes, jax.ShapeDtypeStruct((width, branch), BF16)],
            [
                pl.BlockSpec((branch, width), at),
                pl.BlockSpec((branch, hidden_count), at),
                pl.BlockSpec((branch, hidden_count), at),
                pl.BlockSpec((8, branch), functools.partial(lambda s, i, p: (0, s), s)),
                whole((width, branch)),
            ],
            2 * branch * width * (cols * len(ds) + 2 * hidden_count), 28 * MIB,
            [pltpu.VMEM((branch, width), F32)],
            {1 + len(operands) - len(filled) + k: k for k in range(len(filled))},
        )
        turned.append(one)
        if s == 0:
            shards.append([ring.step("s0t1", one, one)])
    new_latent, keep, give, squares = filled

    for bit in (1, *far_bits()):
        squares = squares + swap(squares, bit)
    shards += [[ring.step(f"s{k + 1}t1", one, one)] for k, one in enumerate(turned[1:])]
    pre = keep + swap(after(give, *ring.arrived(HOLDS["give"])), 1).astype(F32)
    mine = pre.astype(BF16)
    *upper, last = far_bits()
    for bit in upper:
        mine = (mine.astype(F32) + swap(mine, bit).astype(F32)).astype(BF16)
    rounds = wide_size // 2
    for step in range(2, rounds):
        for k, shard in enumerate(shards):
            if f"s{k}t{step}" in EARLY:
                shard.append(ring.step(f"s{k}t{step}", *shard[-1]))
    theirs = after(swap(mine, last), *ring.arrived(HOLDS["heads"]))
    quarter = hidden_count // chips // 4
    payload_shape = (rows + quarter + 16, hidden_count)
    payload, give = call(
        functools.partial(heads, full_width, total_rows), "heads", place, 1,
        [
            mine, theirs, squares, policy_out, value_out[None, :], targets[None, :],
            returns[None, :],
        ],
        [
            whole(half), whole(half), whole((8, rows)), whole(policy_out.shape),
            whole((1, hidden_count)), whole((1, rows)), whole((1, rows)),
        ],
        [
            jax.ShapeDtypeStruct(payload_shape, BF16),
            jax.ShapeDtypeStruct((quarter, hidden_count), BF16),
        ],
        [whole(payload_shape), whole((quarter, hidden_count))],
        6 * rows * hidden_count * action_count, 16 * MIB, [pltpu.VMEM(half, BF16)],
    )
    taken = jnp.where(first, payload[rows : rows + quarter], swap(after(give, *ring.arrived(HOLDS["share"])), 1))
    payload = lax.dynamic_update_slice(payload, taken, (rows, 0))

    payload_rounds = [[payload, payload]]
    cut, size = scenes // 2, hidden_count // 2
    for step in range(1, rounds + 1):
        up, down = payload_rounds[-1]
        if step == rounds:
            up, down = up[:, :size], down[:, size:]
        payload_rounds.append(ring.step(f"p{step}", up, down))
        for k, shard in enumerate(shards):
            if len(shard) == step and step < rounds - 1:
                shard.append(ring.step(f"s{k}t{step + 1}", *shard[-1]))
        if step == rounds - 1:
            for k, (one, other) in enumerate(zip(shards[:cut], shards[cut:])):
                up, down = ring.step(f"s{k}t{rounds}", one[-1][0], other[-1][1])
                one.append([up])
                other.append([down])
    turned_all = list(turned)
    for step in range(rounds):
        for way in range(len(shards[0][step])):
            turned_all += [shard[step][way] for shard in shards]
    payload_own = [payload, *(b for pair in payload_rounds[1:] for b in pair)]
    split = wide_size - 1
    payload_other = [swap(b, 1) for b in payload_own[:split]]

    block = 256
    grad_spec = pl.BlockSpec((block, hidden_count), lambda i, p: (i, 0))
    grad_flops = 4 * rows * width * hidden_count

    def gradient(body, name, operands, specs, count, turned, own, other, dtype):
        return call(
            functools.partial(body, len(turned), len(own)), name, place, width // block,
            [*operands, *turned, *own, *other],
            [
                *specs,
                *[pl.BlockSpec((block, branch), lambda i, p: (i, 0))] * len(turned),
                *[
                    pl.BlockSpec(
                        (rows, b.shape[1]), lambda i, p: (0, 0), pipeline_mode=pl.Buffered(1)
                    )
                    for b in (*own, *other)
                ],
            ],
            [jax.ShapeDtypeStruct((width, hidden_count), dtype)] * 2, [grad_spec] * 2,
            grad_flops * count, 18 * MIB,
        )

    starts = gradient(
        gradients_start, "gradients_start", [], [], 0, turned_all[: scenes * split],
        payload_own[:split], payload_other[:split], F32,
    )
    payload_other += [swap(b, 1) for b in payload_own[split:-2]]
    payload_other += [swap(b, 1) for b in payload_own[-2:]]

    pieces = [*payload_own, *payload_other]
    share_shape = (4 * quarter, action_count)
    share, losses, value_out_grad = call(
        functools.partial(sums, total_rows), "sums", place, 1, [*pieces, *pieces],
        [
            pl.BlockSpec((count, b.shape[1]), functools.partial(lambda at, i, p: (at, 0), start // count))
            for start, count in ((rows, quarter), (rows + quarter, 16))
            for b in pieces
        ],
        [
            jax.ShapeDtypeStruct(share_shape, BF16),
            jax.ShapeDtypeStruct((1, 2), F32),
            jax.ShapeDtypeStruct((hidden_count,), BF16),
        ],
        [whole(share_shape), whole((1, 2)), whole((hidden_count,))], 0, 8 * MIB,
    )
    losses = losses.reshape(2)
    shares = far_blocks(share)
    policy_out_grad = call(
        functools.partial(join, list(shares)), "join", place, 1, list(shares.values()),
        [whole(share_shape)] * len(shares),
        [jax.ShapeDtypeStruct((hidden_count, action_count), BF16)],
        [whole((hidden_count, action_count))], 0, 8 * MIB,
    )[0]

    policy_in_grad, value_in_grad = gradient(
        gradients_end, "gradients_end", starts, [grad_spec] * 2, wide_size - split,
        turned_all[scenes * split :], payload_own[split:], payload_other[split:], BF16,
    )
    return (new_latent, losses, policy_in_grad, value_in_grad, policy_out_grad, value_out_grad)


def solution(mesh):
    placed = (
        P("wide", "narrow"),
        P("wide"),
        P(None, "narrow"),
        P("narrow"),
        P(None, "narrow"),
        P(None, "narrow"),
        P(None, "narrow"),
        P(None, "narrow"),
        P("wide", None, "narrow"),
        P("wide", None, "narrow"),
        P("narrow"),
        P("narrow", None),
        P("narrow", None),
        P(),
        P(),
        P("wide"),
        P("wide"),
    )
    return jax.shard_map(
        per_device,
        mesh=mesh,
        in_specs=placed,
        out_specs=(P("wide", "narrow"), P(), P("narrow", None), P("narrow", None), P(), P()),
        check_vma=False,
    )
```

```python
import functools

import jax
import jax.numpy as jnp
from jax import lax
from jax.experimental import pallas as pl
from jax.experimental.pallas import tpu as pltpu
from jax.sharding import PartitionSpec as P

HD = 128
EPSILON = 1e-05
F32 = jnp.float32
BF16 = jnp.bfloat16
MIB = 1 << 20
HOLDS = {
    "give": ("s0t1",),
    "heads": ("s0t2", "s1t1", "s1t2"),
    "share": ("s1t2",),
    "s0t3": ("s1t2",),
    "s1t3": ("s0t3",),
    "s0t4": ("s1t3",),
    "p4": ("s1t3",),
}
EARLY = ("s0t2", "s1t2", "s0t3")


def swap(block, bit):
    size = lax.axis_size("narrow")
    return lax.ppermute(block, "narrow", [(n, n ^ bit) for n in range(size)])


def far_bits():
    bit = lax.axis_size("narrow") // 2
    while bit > 1:
        yield bit
        bit //= 2


def far_blocks(block):
    blocks = {0: block}
    for bit in far_bits():
        blocks.update({d ^ bit: swap(b, bit) for d, b in list(blocks.items())})
    return blocks


def pass_blocks(blocks, *earlier):
    far = {d ^ 1: swap(after(b, *earlier), 1) for d, b in blocks.items() if d > 1}
    return {**blocks, **far}


def after(block, *earlier):
    return lax.optimization_barrier((block, *earlier))[0]


def ring_order(size):
    return list(range(0, size, 2)) + list(range(size - 1, 0, -2))


def ring_step(block, way):
    order = ring_order(lax.axis_size("wide"))
    pairs = [(a, order[(i + way) % len(order)]) for i, a in enumerate(order)]
    return lax.ppermute(block, "wide", pairs)


class Ring:
    def __init__(self):
        self.at = {}

    def arrived(self, names):
        return [b for name in names for b in self.at.get(name, ())]

    def step(self, name, up, down):
        held = HOLDS.get(name, ())
        up, down = after(up, *self.arrived(held)), after(down, *self.arrived(held))
        self.at[name] = [ring_step(up, 1), ring_step(down, -1)]
        return self.at[name]


def dot(a, b):
    return jnp.dot(a, b, preferred_element_type=F32)


def column(row):
    return jnp.transpose(jnp.broadcast_to(row, (128, row.shape[1])))[:, :1]


def whole(shape):
    return pl.BlockSpec(shape, lambda i, p: (0,) * len(shape))


def weight_spec(ds, rows, columns):
    def at(i, p):
        d = jnp.int32(ds[0])
        for j in range(1, len(ds)):
            d = jnp.where(i == j, ds[j], d)
        return (p[0] ^ d, 0)

    return pl.BlockSpec((rows, columns), at)


def add_products(x_refs, w_refs, add):
    for step, x_ref in enumerate(x_refs):

        @pl.when(pl.program_id(0) == step)
        def _():
            for j, w_ref in enumerate(w_refs):
                add(j, dot(x_ref[...], w_ref[...]))


def row_of(values):
    return jnp.transpose(jnp.broadcast_to(values, (values.shape[0], 128)))[:8]


def embed(p_ref, latent_ref, actions_ref, table_ref, gain_ref, tokens_out, block_out):
    shape = (table_ref.shape[0], latent_ref.shape[0])
    onehot = (lax.broadcasted_iota(jnp.int32, shape, 0) == actions_ref[...]).astype(BF16)
    picked = lax.dot_general(
        onehot, table_ref[...], (((0,), (0,)), ((), ())), preferred_element_type=F32
    )
    tokens = latent_ref[...].astype(F32) + picked
    tokens_out[...] = tokens
    count = latent_ref.shape[0]
    block_out[:count] = (tokens * gain_ref[...]).astype(BF16)
    block_out[count:] = jnp.zeros_like(block_out[count:])
    rest = row_of(jnp.sum(tokens * tokens, axis=1, keepdims=True))[:1]
    rows = lax.broadcasted_iota(jnp.int32, (16, count), 0)
    terms = jnp.zeros((16, count), F32)
    for k in range(3):
        term = rest.astype(BF16).astype(F32)
        terms = jnp.where(rows == k, term, terms)
        rest = rest - term
    block_out[count:, :count] = terms.astype(BF16)


def begin(near, far, p_ref, *refs):
    count = len(near)
    x_refs, weights, caches = refs[:count], refs[count : count + 3], refs[count + 3 : count + 5]
    acc, *outs, held, sems = refs[count + 5 :]
    size, cols = held.shape[1:]
    copies = []

    def send(src, dst):
        copies.append(pltpu.make_async_copy(src, dst, sems.at[len(copies)]))
        copies[-1].start()

    for i, d in enumerate(near + far):
        start = pl.multiple_of((p_ref[0] ^ d) * size, size)
        for j, w_ref in enumerate(weights):
            k = i * 3 + j
            send(
                w_ref.at[pl.ds(start, size)],
                held.at[k] if i < len(near) else outs[k - 3 * len(near)],
            )
    for src, dst in zip(caches, outs[-2:]):
        send(src, dst)
    for i in range(len(near)):
        for j in range(3):
            copies[i * 3 + j].wait()
            product = dot(x_refs[i][...], held[i * 3 + j])
            at = slice(j * cols, (j + 1) * cols)
            acc[:, at] = product if i == 0 else acc[:, at] + product
    for copy in copies[3 * len(near) :]:
        copy.wait()


def project_more(count, p_ref, acc_ref, *refs):
    x_refs, w_refs, out = refs[:count], refs[count:-1], refs[-1]
    cols = w_refs[0].shape[1]
    for j in range(3):
        at = slice(j * cols, (j + 1) * cols)
        total = acc_ref[:, at]
        for i, x_ref in enumerate(x_refs):
            total = total + dot(x_ref[...], w_refs[i * 3 + j][...])
        out[:, at] = total


def attend(count, sources, full_width, p_ref, acc_ref, keys_ref, values_ref, *refs):
    squares_refs, refs = refs[:sources], refs[sources:]
    project_more(count, p_ref, acc_ref, *refs[:-2], refs[-1])
    out, acc = refs[-2:]
    cols = refs[count].shape[1]
    squares = sum(jnp.sum(ref[:8].astype(F32), axis=0, keepdims=True) for ref in squares_refs)
    attend_heads(full_width, cols, squares, keys_ref, values_ref, out, acc)


def attend_heads(full_width, cols, squares, keys_ref, values_ref, out, acc):
    scenes = keys_ref.shape[0]
    branch = acc.shape[0] // scenes
    inverse = column(lax.rsqrt(squares / full_width + EPSILON))
    scaling = HD ** (-0.5)
    for s in range(scenes):
        rows = slice(s * branch, (s + 1) * branch)
        scale = inverse[rows]
        for h in range(cols // HD):
            at = slice(h * HD, (h + 1) * HD)
            q, k, v = (
                (acc[rows, j * cols + h * HD : j * cols + (h + 1) * HD] * scale).astype(BF16)
                for j in range(3)
            )
            scores = (
                lax.dot_general(
                    q,
                    keys_ref[s, :, at],
                    (((1,), (1,)), ((), ())),
                    preferred_element_type=F32,
                )
                * scaling
            )
            own = jnp.sum(q.astype(F32) * k.astype(F32), axis=1, keepdims=True) * scaling
            highest = jnp.maximum(jnp.max(scores, axis=1, keepdims=True), own)
            expd = jnp.exp(scores - highest)
            own_exp = jnp.exp(own - highest)
            total = jnp.sum(expd, axis=1, keepdims=True) + own_exp
            weights = (expd / total).astype(BF16)
            own_weight = (own_exp / total).astype(BF16)
            mixed = dot(weights, values_ref[s, :, at])
            mixed = mixed + own_weight.astype(F32) * v.astype(F32)
            out[rows, at] = mixed.astype(BF16)


def update_near(scenes, p_ref, tokens_ref, *refs):
    x_refs, w_ref, out = refs[:-2], refs[-2], refs[-1]
    for step in range(len(x_refs) // scenes):

        @pl.when(pl.program_id(0) == step)
        def _():
            x = jnp.concatenate(
                [ref[...] for ref in x_refs[step * scenes : (step + 1) * scenes]], axis=0
            )
            out[...] = (tokens_ref if step == 0 else out)[...] + dot(x, w_ref[...])


def update(count, p_ref, acc_ref, gain_ref, policy_ref, value_ref, *refs):
    x_refs, w_ref = refs[:count], refs[count]
    latent_out, keep_out, give_out, squares_out, turned_out, acc = refs[-6:]

    @pl.when(pl.program_id(0) == 0)
    def _():
        acc[...] = acc_ref[...]

    def add(j, product):
        acc[...] += product

    add_products(x_refs, [w_ref], add)

    @pl.when(pl.program_id(0) == count - 1)
    def _():
        state = acc[...]
        latent_out[...] = state.astype(BF16)
        squares = jnp.sum(state * state, axis=1, keepdims=True)
        squares_out[...] = row_of(squares)
        gained = (state * gain_ref[...]).astype(BF16)
        turned_out[...] = jnp.transpose(gained)
        policy = dot(gained, policy_ref[...])
        value = dot(gained, value_ref[...])

        @pl.when(p_ref[0] % 2 == 0)
        def _():
            keep_out[...] = policy
            give_out[...] = value.astype(BF16)

        @pl.when(p_ref[0] % 2 == 1)
        def _():
            keep_out[...] = value
            give_out[...] = policy.astype(BF16)


def heads(full_width, total_rows, p_ref, mine_ref, theirs_ref, squares_ref, policy_out_ref,
          value_out_ref, targets_ref, returns_ref, payload_out, give_out, hidden_ref):
    inverse = column(lax.rsqrt(squares_ref[:1] / full_width + EPSILON))
    pre = (mine_ref[...].astype(F32) + theirs_ref[...].astype(F32)) * inverse
    sigma = jax.nn.sigmoid(pre)
    hidden = (pre * sigma).astype(BF16)
    hidden_ref[...] = hidden
    slope = sigma * (1.0 + pre * (1.0 - sigma)) * inverse
    factor = total_rows ** (-0.5)
    count = hidden.shape[0]
    quarter = give_out.shape[0]
    part = 4 * quarter
    at = slice(count, count + quarter)

    def put_sums(grad, loss):
        shape = (payload_out.shape[0] - count - quarter, hidden.shape[1])
        rows = lax.broadcasted_iota(jnp.int32, shape, 0)
        lanes = lax.broadcasted_iota(jnp.int32, shape, 1)
        sums = jnp.where(rows == 0, grad, 0.0)
        for lane in range(3):
            term = loss.astype(BF16).astype(F32)
            sums = jnp.where((rows == 1) & (lanes == lane), term, sums)
            loss = loss - term
        payload_out[count + quarter :] = sums.astype(BF16)

    @pl.when(p_ref[0] % 2 == 0)
    def _():
        weight = policy_out_ref[...]
        logits = dot(hidden, weight)
        top = jnp.max(logits, axis=1, keepdims=True)
        log_total = top + jnp.log(jnp.sum(jnp.exp(logits - top), axis=1, keepdims=True))
        actions = lax.broadcasted_iota(jnp.int32, logits.shape, 1).astype(F32)
        onehot = (actions == column(targets_ref[...].astype(F32))).astype(F32)
        picked = jnp.sum(logits * onehot, axis=1, keepdims=True)
        loss = jnp.sum(log_total - picked, axis=0, keepdims=True)
        dlogits = ((jnp.exp(logits - log_total) - onehot) * factor).astype(BF16)
        back = lax.dot_general(
            dlogits, weight, (((1,), (1,)), ((), ())), preferred_element_type=F32
        )
        payload_out[:count] = (back * slope).astype(BF16)
        start = pl.multiple_of((p_ref[0] // 2) * part, part)
        grad = lax.dot_general(
            hidden_ref[:, pl.ds(start, part)],
            dlogits,
            (((0,), (0,)), ((), ())),
            preferred_element_type=F32,
        ).astype(BF16)
        parts = [grad[k * quarter : (k + 1) * quarter] for k in range(4)]
        payload_out[at] = jnp.concatenate(parts[:2], axis=1)
        give_out[...] = jnp.concatenate(parts[2:], axis=1)
        put_sums(jnp.zeros((1, hidden.shape[1]), F32), loss)

    @pl.when(p_ref[0] % 2 == 1)
    def _():
        weight = value_out_ref[...].astype(F32)
        hidden_f = hidden.astype(F32)
        value = jnp.sum(hidden_f * weight, axis=1, keepdims=True)
        errors = value - column(returns_ref[...])
        loss = 0.5 * jnp.sum(errors * errors, axis=0, keepdims=True)
        dvalue = (errors * factor).astype(BF16).astype(F32)
        payload_out[:count] = (dvalue * weight * slope).astype(BF16)
        payload_out[at] = jnp.zeros_like(give_out)
        give_out[...] = jnp.zeros_like(give_out)
        put_sums(jnp.sum(dvalue * hidden_f, axis=0, keepdims=True), loss)


def sums(total_rows, p_ref, *refs):
    count = (len(refs) - 3) // 4
    share_out, losses_out, grad_out = refs[-3:]

    def total(d_refs):
        *shards, ahead, back = [ref[...].astype(F32) for ref in d_refs]
        return sum(shards, jnp.concatenate([ahead, back], axis=1))

    own, other, own_sums, other_sums = (
        total(refs[k * count : (k + 1) * count]) for k in range(4)
    )
    first = p_ref[0] % 2 == 0
    quarter = own.shape[0]
    width = share_out.shape[1]
    for k, part in enumerate((jnp.where(first, own, other), jnp.where(first, other, own))):
        for j in range(2):
            at = (2 * k + j) * quarter
            share_out[at : at + quarter] = part[:, j * width : (j + 1) * width].astype(BF16)
    policy = jnp.where(first, own_sums, other_sums)
    value = jnp.where(first, other_sums, own_sums)
    grad_out[...] = value[0].astype(BF16)

    def loss(part):
        lanes = lax.broadcasted_iota(jnp.int32, (1, part.shape[1]), 1)
        return jnp.sum(jnp.where(lanes < 3, part[1:2], 0.0), axis=1, keepdims=True) / total_rows

    lanes = lax.broadcasted_iota(jnp.int32, (1, 2), 1)
    losses_out[...] = jnp.where(lanes == 0, loss(policy), loss(value))


def join(ds, p_ref, *refs):
    out = refs[-1]
    size = refs[0].shape[0]
    for d, ref in zip(ds, refs[:-1]):
        out[pl.ds(pl.multiple_of(((p_ref[0] ^ d) // 2) * size, size), size)] = ref[...]


def factors(turned_refs, own_refs, other_refs, halved):
    turned = jnp.concatenate([ref[...] for ref in turned_refs], axis=1)
    for d_refs in (own_refs, other_refs):
        shards = [ref[...] for ref in d_refs]
        if halved:
            shards[-2:] = [jnp.concatenate(shards[-2:], axis=1)]
        yield dot(turned, jnp.concatenate(shards, axis=0))


def gradients_start(turned_count, count, p_ref, *refs):
    turned, own, other = refs[:turned_count], refs[turned_count:][:count], refs[turned_count + count : -2]
    for out, product in zip(refs[-2:], factors(turned, own, other, False)):
        out[...] = product


def gradients_end(turned_count, count, p_ref, *refs):
    sums, refs, outs = refs[:2], refs[2:-2], refs[-2:]
    turned, own, other = refs[:turned_count], refs[turned_count:][:count], refs[turned_count + count :]
    own, other = (
        (acc[...] + product).astype(BF16)
        for acc, product in zip(sums, factors(turned, own, other, True))
    )

    @pl.when(p_ref[0] % 2 == 0)
    def _():
        outs[0][...] = own
        outs[1][...] = other

    @pl.when(p_ref[0] % 2 == 1)
    def _():
        outs[1][...] = own
        outs[0][...] = other


def call(body, name, place, steps, operands, in_specs, outs, out_specs, flops, limit, scratch=(), aliases=None):
    bytes_accessed = sum(x.size * x.dtype.itemsize for x in (*operands, *outs)) if flops else 0
    return pl.pallas_call(
        body,
        name=name,
        out_shape=outs,
        input_output_aliases=aliases or {},
        grid_spec=pltpu.PrefetchScalarGridSpec(
            num_scalar_prefetch=1,
            grid=(steps,),
            in_specs=in_specs,
            out_specs=out_specs,
            scratch_shapes=scratch,
        ),
        compiler_params=pltpu.CompilerParams(
            dimension_semantics=("arbitrary",), vmem_limit_bytes=limit
        ),
        cost_estimate=pl.CostEstimate(
            flops=flops, bytes_accessed=bytes_accessed, transcendentals=0
        ),
    )(place, *operands)


def per_device(
    latent,
    actions,
    action_table,
    norm1_gain,
    w_query,
    w_key,
    w_value,
    w_out,
    key_cache,
    value_cache,
    norm2_gain,
    policy_in,
    value_in,
    policy_out,
    value_out,
    targets,
    returns,
):
    rows, width = latent.shape
    narrow_size = lax.axis_size("narrow")
    wide_size = lax.axis_size("wide")
    full_width = width * narrow_size
    cols = w_query.shape[1]
    total_rows = rows * wide_size
    action_count = action_table.shape[0]
    hidden_count = policy_in.shape[1]
    index = lax.axis_index("narrow").astype(jnp.int32)
    place = index[None]
    first = index % 2 == 0
    chips = narrow_size // 2
    near = [0, 1]
    direct = list(range(2, narrow_size, 2))
    passed = [d + 1 for d in direct]

    far = direct + passed
    scenes = key_cache.shape[0]
    branch = rows // scenes
    hbm = functools.partial(pltpu.with_memory_space_constraint, memory_space=pltpu.HBM)

    block_shape = (rows + 16, width)
    tokens, block = call(
        embed, "embed", place, 1,
        [
            hbm(latent), hbm(actions[None, :]), hbm(action_table),
            hbm(norm1_gain[None, :]),
        ],
        [
            whole((rows, width)), whole((1, rows)), whole(action_table.shape),
            whole((1, width)),
        ],
        [
            jax.ShapeDtypeStruct((rows, width), F32),
            jax.ShapeDtypeStruct(block_shape, BF16),
        ],
        [whole((rows, width)), whole(block_shape)],
        2 * rows * width * action_count, 16 * MIB,
    )
    blocks = {**far_blocks(block), 1: swap(block, 1)}

    weights = [hbm(w) for w in (w_query, w_key, w_value)]
    x_spec = whole((rows, width))
    acc_shape = jax.ShapeDtypeStruct((rows, 3 * cols), F32)
    weight_shape = jax.ShapeDtypeStruct((width, cols), BF16)
    weight_block = whole((width, cols))
    cache_shape = jax.ShapeDtypeStruct(key_cache.shape, BF16)
    outs = [weight_shape] * (3 * len(far)) + [cache_shape] * 2
    anywhere = pl.BlockSpec(memory_space=pl.ANY)
    flops = 2 * rows * width * 3 * cols
    acc, *staged, keys, values = call(
        functools.partial(begin, near, far), "begin", place, 1,
        [
            *(blocks[d] for d in near), *weights,
            hbm(key_cache), hbm(value_cache),
        ],
        [*[x_spec] * len(near), *[anywhere] * 5],
        [acc_shape, *outs], [whole(acc_shape.shape), *[anywhere] * len(outs)],
        flops * len(near), 20 * MIB,
        [
            pltpu.VMEM((3 * len(near), width, cols), BF16),
            pltpu.SemaphoreType.DMA((3 * len(near) + len(outs),)),
        ],
    )
    staged_direct = staged[: 3 * len(direct)]
    staged_passed = staged[3 * len(direct) :]

    acc_spec = whole(acc_shape.shape)
    blocks = pass_blocks(blocks, acc)
    acc = call(
        functools.partial(project_more, len(direct)), "project", place, 1,
        [acc, *(blocks[d] for d in direct), *staged_direct],
        [acc_spec, *[x_spec] * len(direct), *[weight_block] * len(staged_direct)],
        [acc_shape], [acc_spec], flops * len(direct), 24 * MIB,
    )[0]

    attended = []
    for s in range(scenes):
        at = functools.partial(lambda s, i, p: (s, 0), s)
        squares_spec = pl.BlockSpec(
            (16, branch), functools.partial(lambda s, i, p: (rows // 16, s), s)
        )
        cache_spec = pl.BlockSpec(
            (1, *key_cache.shape[1:]), functools.partial(lambda s, i, p: (s, 0, 0), s)
        )
        one = call(
            functools.partial(attend, len(passed), narrow_size, full_width), f"attend{s}", place, 1,
            [
                acc, keys, values, *blocks.values(),
                *(blocks[d] for d in passed), *staged_passed,
            ],
            [
                pl.BlockSpec((branch, 3 * cols), at), cache_spec, cache_spec,
                *[squares_spec] * narrow_size,
                *[pl.BlockSpec((branch, width), at)] * len(passed), *[weight_block] * len(staged_passed),
            ],
            [jax.ShapeDtypeStruct((branch, cols), BF16)], [whole((branch, cols))],
            0, 20 * MIB, [pltpu.VMEM((branch, 3 * cols), F32)],
        )[0]
        attended.append({**far_blocks(one), 1: swap(one, 1)})

    half = (rows, hidden_count)
    full_shapes = [
        jax.ShapeDtypeStruct((rows, width), BF16),
        jax.ShapeDtypeStruct(half, F32),
        jax.ShapeDtypeStruct(half, BF16),
        jax.ShapeDtypeStruct((8, rows), F32),
    ]
    chunk = whole((branch, cols))
    acc = call(
        functools.partial(update_near, scenes), "update_near", place, len(near),
        [tokens, *(one[d] for d in near for one in attended), w_out],
        [
            whole((rows, width)), *[chunk] * (scenes * len(near)),
            weight_spec(near, cols, width),
        ],
        [jax.ShapeDtypeStruct((rows, width), F32)], [whole((rows, width))],
        2 * rows * width * cols * len(near), 16 * MIB,
    )[0]
    filled, turned, shards = [], [], []
    ring = Ring()
    for s in range(scenes):
        ds = far
        around = pass_blocks(attended[s], *turned)
        at = functools.partial(lambda s, i, p: (s, 0), s)
        operands = [
            acc, norm2_gain[None, :], policy_in, value_in,
            *(around[d] for d in ds), w_out, *filled,
        ]
        *filled, one = call(
            functools.partial(update, len(ds)), f"update{s}", place, len(ds), operands,
            [
                pl.BlockSpec((branch, width), at),
                whole((1, width)), whole(policy_in.shape), whole(value_in.shape),
                *[chunk] * len(ds), weight_spec(ds, cols, width),
                *[anywhere] * len(filled),
            ],
            [*full_shapes, jax.ShapeDtypeStruct((width, branch), BF16)],
            [
                pl.BlockSpec((branch, width), at),
                pl.BlockSpec((branch, hidden_count), at),
                pl.BlockSpec((branch, hidden_count), at),
                pl.BlockSpec((8, branch), functools.partial(lambda s, i, p: (0, s), s)),
                whole((width, branch)),
            ],
            2 * branch * width * (cols * len(ds) + 2 * hidden_count), 28 * MIB,
            [pltpu.VMEM((branch, width), F32)],
            {1 + len(operands) - len(filled) + k: k for k in range(len(filled))},
        )
        turned.append(one)
        if s == 0:
            shards.append([ring.step("s0t1", one, one)])
    new_latent, keep, give, squares = filled

    for bit in (1, *far_bits()):
        squares = squares + swap(squares, bit)
    shards += [[ring.step(f"s{k + 1}t1", one, one)] for k, one in enumerate(turned[1:])]
    pre = keep + swap(after(give, *ring.arrived(HOLDS["give"])), 1).astype(F32)
    mine = pre.astype(BF16)
    *upper, last = far_bits()
    for bit in upper:
        mine = (mine.astype(F32) + swap(mine, bit).astype(F32)).astype(BF16)
    rounds = wide_size // 2
    for step in range(2, rounds):
        for k, shard in enumerate(shards):
            if f"s{k}t{step}" in EARLY:
                shard.append(ring.step(f"s{k}t{step}", *shard[-1]))
    theirs = after(swap(mine, last), *ring.arrived(HOLDS["heads"]))
    quarter = hidden_count // chips // 4
    payload_shape = (rows + quarter + 16, hidden_count)
    payload, give = call(
        functools.partial(heads, full_width, total_rows), "heads", place, 1,
        [
            mine, theirs, squares, policy_out, value_out[None, :], targets[None, :],
            returns[None, :],
        ],
        [
            whole(half), whole(half), whole((8, rows)), whole(policy_out.shape),
            whole((1, hidden_count)), whole((1, rows)), whole((1, rows)),
        ],
        [
            jax.ShapeDtypeStruct(payload_shape, BF16),
            jax.ShapeDtypeStruct((quarter, hidden_count), BF16),
        ],
        [whole(payload_shape), whole((quarter, hidden_count))],
        6 * rows * hidden_count * action_count, 16 * MIB, [pltpu.VMEM(half, BF16)],
    )
    taken = jnp.where(first, payload[rows : rows + quarter], swap(after(give, *ring.arrived(HOLDS["share"])), 1))
    payload = lax.dynamic_update_slice(payload, taken, (rows, 0))

    payload_rounds = [[payload, payload]]
    cut, size = scenes // 2, hidden_count // 2
    for step in range(1, rounds + 1):
        up, down = payload_rounds[-1]
        if step == rounds:
            up, down = up[:, :size], down[:, size:]
        payload_rounds.append(ring.step(f"p{step}", up, down))
        for k, shard in enumerate(shards):
            if len(shard) == step and step < rounds - 1:
                shard.append(ring.step(f"s{k}t{step + 1}", *shard[-1]))
        if step == rounds - 1:
            for k, (one, other) in enumerate(zip(shards[:cut], shards[cut:])):
                up, down = ring.step(f"s{k}t{rounds}", one[-1][0], other[-1][1])
                one.append([up])
                other.append([down])
    turned_all = list(turned)
    for step in range(rounds):
        for way in range(len(shards[0][step])):
            turned_all += [shard[step][way] for shard in shards]
    payload_own = [payload, *(b for pair in payload_rounds[1:] for b in pair)]
    split = wide_size - 1
    payload_other = [swap(b, 1) for b in payload_own[:split]]

    block = 512
    grad_spec = pl.BlockSpec((block, hidden_count), lambda i, p: (i, 0))
    grad_flops = 4 * rows * width * hidden_count

    def gradient(body, name, operands, specs, count, turned, own, other, dtype):
        return call(
            functools.partial(body, len(turned), len(own)), name, place, width // block,
            [*operands, *turned, *own, *other],
            [
                *specs,
                *[pl.BlockSpec((block, branch), lambda i, p: (i, 0))] * len(turned),
                *[
                    pl.BlockSpec(
                        (rows, b.shape[1]), lambda i, p: (0, 0), pipeline_mode=pl.Buffered(1)
                    )
                    for b in (*own, *other)
                ],
            ],
            [jax.ShapeDtypeStruct((width, hidden_count), dtype)] * 2, [grad_spec] * 2,
            grad_flops * count, 26 * MIB,
        )

    starts = gradient(
        gradients_start, "gradients_start", [], [], 0, turned_all[: scenes * split],
        payload_own[:split], payload_other[:split], F32,
    )
    payload_other += [swap(b, 1) for b in payload_own[split:-2]]
    payload_other += [swap(b, 1) for b in payload_own[-2:]]

    pieces = [*payload_own, *payload_other]
    share_shape = (4 * quarter, action_count)
    share, losses, value_out_grad = call(
        functools.partial(sums, total_rows), "sums", place, 1, [*pieces, *pieces],
        [
            pl.BlockSpec((count, b.shape[1]), functools.partial(lambda at, i, p: (at, 0), start // count))
            for start, count in ((rows, quarter), (rows + quarter, 16))
            for b in pieces
        ],
        [
            jax.ShapeDtypeStruct(share_shape, BF16),
            jax.ShapeDtypeStruct((1, 2), F32),
            jax.ShapeDtypeStruct((hidden_count,), BF16),
        ],
        [whole(share_shape), whole((1, 2)), whole((hidden_count,))], 0, 8 * MIB,
    )
    losses = losses.reshape(2)
    shares = far_blocks(share)
    policy_out_grad = call(
        functools.partial(join, list(shares)), "join", place, 1, list(shares.values()),
        [whole(share_shape)] * len(shares),
        [jax.ShapeDtypeStruct((hidden_count, action_count), BF16)],
        [whole((hidden_count, action_count))], 0, 8 * MIB,
    )[0]

    policy_in_grad, value_in_grad = gradient(
        gradients_end, "gradients_end", starts, [grad_spec] * 2, wide_size - split,
        turned_all[scenes * split :], payload_own[split:], payload_other[split:], BF16,
    )
    return (new_latent, losses, policy_in_grad, value_in_grad, policy_out_grad, value_out_grad)


def solution(mesh):
    placed = (
        P("wide", "narrow"),
        P("wide"),
        P(None, "narrow"),
        P("narrow"),
        P(None, "narrow"),
        P(None, "narrow"),
        P(None, "narrow"),
        P(None, "narrow"),
        P("wide", None, "narrow"),
        P("wide", None, "narrow"),
        P("narrow"),
        P("narrow", None),
        P("narrow", None),
        P(),
        P(),
        P("wide"),
        P("wide"),
    )
    return jax.shard_map(
        per_device,
        mesh=mesh,
        in_specs=placed,
        out_specs=(P("wide", "narrow"), P(), P("narrow", None), P("narrow", None), P(), P()),
        check_vma=False,
    )
```
